128 devices in a mesh: visit: 8 (over x, core), det: 16 (over z, y).
Axes of the slice: x: 4, y: 4, z: 4, core: 2. Of those that a mesh axis runs over, the one named last changes fastest.
Arguments:
- strips: float32 [8192, 16, 512], P(('visit', 'det')), may hold values from -6 to 6
- patch_of: int32 [8192, 1], P(('visit', 'det')), may hold values from 0 to 127, as said below
- box_row: int32 [8192], P(('visit', 'det')), may hold values from 0 to 112
- kernel_set: int32 [8192], P(('visit', 'det')), may hold values from 0 to 7
- template: float32 [1024, 8192], P('visit', 'det'), may hold values from -6 to 6
- row_taps: float32 [40, 21], replicated, may hold values from -1.25 to 1.25
- col_taps: float32 [40, 21], replicated, may hold values from -1.25 to 1.25
- kernel_coef: float32 [8, 6, 40], replicated, may hold values from -0.6 to 0.6
Outputs:
- difference: float32 [8192, 16, 512], P(('visit', 'det'))
- coadd: float32 [1024, 8192], P('visit', 'det')
The draws below stay inside these ranges and needn't reach their ends.
Inputs may be any that keep to these rules, and one draw needn't show every extreme that they name: `patch_of`: device b = v * 16 + d holds strips b * 64 to (b + 1) * 64 - 1, and each of them names patch (v + i) * 16 + d + j with i and j in -1, 0, 1, inside the grid of 8 x 16 patches. Among one device's strips no patch is named more than 16 times. In every draw some patch is named exactly 16 times by the strips of each of its eight neighbouring devices.
All inputs are finite; a program needn't handle non-finite values.
Results may differ from the reference program's by a relative error of at most 0.0003.
Values sent between devices are 32-bit elements; how exact they have to be, the bound alone decides.
No kernel may reach another device: no remote copies, remote signals or barrier semaphores. Data moves between devices by JAX's collectives and lax.ppermute only.
A program may use at most 128 MiB of HBM per device.

```python
import jax
import jax.numpy as jnp
from jax import lax

N_BASIS = 40
TAPS = 21
NTERM = 6
NSETS = 8
PH = 128
PW = 512
SH = 16
TILES_DEV = 64
CAP = 16
TILES = 8192
NY = 1024
NX = 8192
N_VISIT = 8
N_DET = 16
DEVICES = 128


def draw_patch_of(key, part):
    key = jax.random.fold_in(key, 11)
    hot_key, prio_key, tie_key, perm_key = jax.random.split(key, 4)
    hot_row = jax.random.randint(hot_key, (), 1, N_VISIT - 1)
    hot_col = jax.random.randint(jax.random.fold_in(hot_key, 1), (), 1, N_DET - 1)
    device_ids = jnp.arange(DEVICES, dtype=jnp.int32)
    dev_row = device_ids // N_DET
    dev_col = device_ids % N_DET
    neighbour = jnp.arange(9, dtype=jnp.int32)
    patch_row = dev_row[:, None] + neighbour[None, :] // 3 - 1
    patch_col = dev_col[:, None] + neighbour[None, :] % 3 - 1
    inside = (patch_row >= 0) & (patch_row < N_VISIT) & (patch_col >= 0) & (patch_col < N_DET)
    is_hot = (patch_row == hot_row) & (patch_col == hot_col)
    priority = jax.random.randint(prio_key, (DEVICES, 9), 0, 5)
    priority = jnp.where(is_hot, 20, priority)
    level = jnp.where(inside, priority + 2, 0)
    cell_level = jnp.repeat(level, CAP, axis=1)
    tie_break = jax.random.randint(tie_key, (DEVICES, 9 * CAP), 0, 64)
    score = (cell_level * 64 + tie_break) * (9 * CAP) + jnp.arange(9 * CAP, dtype=jnp.int32)[None, :]
    _, picked = lax.top_k(score, TILES_DEV)
    offset = picked // CAP
    patch = (dev_row[:, None] + offset // 3 - 1) * N_DET + dev_col[:, None] + offset % 3 - 1
    row_keys = jax.random.split(perm_key, DEVICES)
    shuffled = jax.vmap(lambda one_key, row_values: jax.random.permutation(one_key, row_values))(row_keys, patch)
    return shuffled.reshape(DEVICES * TILES_DEV, 1).astype(jnp.int32)


def with_ends(array, stream_key, low, top_value):
    longest = array.shape.index(max(array.shape))
    spots = []
    for shift in (0, 1):
        where = [jax.random.randint(jax.random.fold_in(stream_key, axis), (), 0, length) for axis, length in enumerate(array.shape)]
        where[longest] = (where[longest] + shift) % array.shape[longest]
        spots.append(tuple(where))
    return array.at[spots[0]].set(low).at[spots[1]].set(top_value)


def block_scale(own_key, extent, cuts, low, largest):
    gain = 1.0
    for position, shards_of in cuts:
        draws = jax.random.uniform(jax.random.fold_in(jax.random.fold_in(own_key, 6), position), (shards_of,), jnp.float32, low / len(cuts), largest / len(cuts))
        gain = gain * jnp.repeat(jnp.exp(draws), extent[position] // shards_of).reshape((-1,) + (1,) * (len(extent) - 1 - position))
    return gain


def normal_values(rng, shape, width, bound, pieces=(), kind=jnp.bfloat16):
    loudness = block_scale(rng, shape, pieces, -0.22, 0.18) if pieces else 1.0
    result = jax.random.normal(rng, shape, jnp.float32) * width * loudness
    return jnp.minimum(jnp.maximum(result, -bound), bound).astype(kind)


def setup_inputs(seed: int = 0) -> dict:
    key_list = jax.random.split(jax.random.key(seed), 9)
    return {
        "strips": normal_values(key_list[0], (TILES, SH, PW), 1.0, 6.0, ((0, 128),), jnp.float32),
        "patch_of": draw_patch_of(jax.random.fold_in(key_list[8], 71), 0),
        "box_row": with_ends(jax.random.randint(key_list[2], (TILES,), 0, PH - SH + 1), jax.random.fold_in(key_list[2], 1), 0, PH - SH).astype(jnp.int32),
        "kernel_set": with_ends(jax.random.randint(key_list[3], (TILES,), 0, NSETS), jax.random.fold_in(key_list[3], 1), 0, NSETS - 1).astype(jnp.int32),
        "template": normal_values(key_list[4], (NY, NX), 1.0, 6.0, ((0, 8), (1, 16)), jnp.float32),
        "row_taps": normal_values(key_list[5], (N_BASIS, TAPS), TAPS ** -0.5, 1.25, (), jnp.float32),
        "col_taps": normal_values(key_list[6], (N_BASIS, TAPS), TAPS ** -0.5, 1.25, (), jnp.float32),
        "kernel_coef": normal_values(key_list[7], (NSETS, NTERM, N_BASIS), 0.1, 0.6, (), jnp.float32),
    }


def reference(strips, patch_of, box_row, kernel_set, template, row_taps, col_taps, kernel_coef):
    half_width = TAPS // 2
    padded = jnp.pad(template, half_width)
    v_coord = (2.0 * (jnp.arange(NY, dtype=jnp.float32) + 0.5) / NY - 1.0)[:, None]
    u_coord = (2.0 * (jnp.arange(NX, dtype=jnp.float32) + 0.5) / NX - 1.0)[None, :]
    ones_grid = jnp.ones((NY, NX), jnp.float32)
    poly_terms = jnp.stack([ones_grid, u_coord * ones_grid, v_coord * ones_grid,
                            u_coord * u_coord * ones_grid, u_coord * v_coord, v_coord * v_coord * ones_grid])

    def one_basis(models, which):
        row_kernel = row_taps[which][None, None, :, None]
        col_kernel = col_taps[which][None, None, None, :]
        rowpass = lax.conv_general_dilated(padded[None, None], row_kernel, (1, 1), 'VALID',
                                           precision=lax.Precision.HIGHEST)
        image = lax.conv_general_dilated(rowpass, col_kernel, (1, 1), 'VALID',
                                         precision=lax.Precision.HIGHEST)[0, 0]
        weights = jnp.einsum('sp,pyx->syx', kernel_coef[:, :, which], poly_terms,
                             precision=lax.Precision.HIGHEST)
        return models + weights * image[None], None

    models, _ = lax.scan(one_basis, jnp.zeros((NSETS, NY, NX), jnp.float32),
                         jnp.arange(N_BASIS, dtype=jnp.int32))
    target = patch_of[:, 0]
    top_row = ((target // N_DET) * PH + box_row).astype(jnp.int32)
    left_col = ((target % N_DET) * PW).astype(jnp.int32)

    def cut_rows(which, row_start, col_start):
        return lax.dynamic_slice(models, (which.astype(jnp.int32), row_start, col_start), (1, SH, PW))[0]

    model_strips = jax.vmap(cut_rows)(kernel_set, top_row, left_col)
    difference = strips - model_strips
    row_index = top_row[:, None] + jnp.arange(SH, dtype=jnp.int32)[None, :]
    col_patch = (target % N_DET).astype(jnp.int32)
    coadd = jnp.zeros((NY, N_DET, PW), jnp.float32).at[row_index, col_patch[:, None]].add(difference)
    return difference, coadd.reshape(NY, NX)
```

```python
import functools

import jax
import jax.numpy as jnp
from jax import lax
from jax.experimental import pallas as pl
from jax.experimental.pallas import tpu as pltpu
from jax.sharding import PartitionSpec as P

F32 = jnp.float32
BF16 = jnp.bfloat16
HIGHEST = lax.Precision.HIGHEST

HALF = 10
SIDE = 12
EDGE = 16
PHASES = 4
LANES = 128
ROWS = 8
WIN = 32
SHIFTS = 24
DEPTH = SHIFTS * WIN
VMEM = 56 * 1024 * 1024


def iota(shape, dim):
    return lax.broadcasted_iota(jnp.int32, shape, dim)


def split(x):
    hi = x.astype(BF16)
    lo = (x - hi.astype(F32)).astype(BF16)
    return hi, lo


def mxu(a, b):
    return jnp.dot(a, b, preferred_element_type=F32)


def exact(a, b):
    return jnp.dot(a, b, precision=HIGHEST, preferred_element_type=F32)


def to_phases(width):
    out = iota((width, PHASES * LANES), 1)
    source = (out % LANES) * PHASES + out // LANES
    return jnp.where(iota((width, PHASES * LANES), 0) == source, 1.0, 0.0).astype(BF16)


def from_phases():
    src = iota((PHASES * LANES, PHASES * LANES), 0)
    target = (src % LANES) * PHASES + src // LANES
    return jnp.where(iota((PHASES * LANES, PHASES * LANES), 1) == target, 1.0, 0.0).astype(BF16)


def place(patch, n_cols):
    step_row = patch // n_cols - lax.axis_index("visit") + 1
    step_col = patch % n_cols - lax.axis_index("det") + 1
    return step_row, step_col


def sums_kernel(n_cols, patch_ref, row_ref, set_ref, strips_ref, up_ref, mid_ref, down_ref, acc):
    height = up_ref.shape[1] - ROWS
    strip_rows = strips_ref.shape[1]
    acc[...] = jnp.zeros(acc.shape, F32)
    lane = iota((ROWS, LANES), 1)
    sub = iota((ROWS, LANES), 0)

    def one_strip(t, carry):
        step_row, step_col = place(patch_ref[t, 0], n_cols)
        top = row_ref[t]
        q = step_row * 3 + step_col
        for c in range(PHASES):
            acc[q, c, pl.ds(top, strip_rows), :] += strips_ref[t, :, c * LANES : (c + 1) * LANES]
        hit = (sub == set_ref[t]) & (lane >= top) & (lane < top + strip_rows)
        acc[q, 0, height:, :] += jnp.where(hit, 1.0, 0.0)
        return carry

    lax.fori_loop(0, strips_ref.shape[0], one_strip, 0)
    for i, out in enumerate((up_ref, mid_ref, down_ref)):
        for c in range(PHASES):
            out[:, :, c * LANES : (c + 1) * LANES] = acc[3 * i : 3 * i + 3, c]


def taps_kernel(row_ref, col_ref, coef_ref, flat_ref, table_ref, wide):
    taps = row_ref.shape[1]
    lane = iota((taps, DEPTH), 1)
    sub = iota((taps, DEPTH), 0)
    row_part = exact(row_ref[...], jnp.where(lane % WIN == sub, 1.0, 0.0))
    col_part = exact(col_ref[...], jnp.where(lane // WIN == sub, 1.0, 0.0))
    flat = exact(coef_ref[...], row_part * col_part)
    flat_ref[...] = flat
    n = flat.shape[0]
    block = PHASES * ROWS
    for dx in range(PHASES):
        for dy in range(ROWS):
            shift = dx * WIN + dy
            moved = flat if shift == 0 else pltpu.roll(flat, shift, 1)
            for c in range(DEPTH // LANES):
                wide[c, pl.ds(dx * ROWS + dy, n, stride=block), :] = moved[:, c * LANES : (c + 1) * LANES]
    n_sets = table_ref.shape[0]
    n_terms = n // n_sets
    for s in range(n_sets):
        for p in range(n_terms):
            first = (p * n_sets + s) * block
            for c in range(DEPTH // LANES):
                hi, lo = split(wide[c, first : first + block, :])
                cols = slice(c * LANES, (c + 1) * LANES)
                table_ref[s, p * block : (p + 1) * block, cols] = hi
                table_ref[s, (n_terms + p) * block : (n_terms + p + 1) * block, cols] = lo


def columns_of(step_col, n_cols, width):
    shape = (PHASES * ROWS, LANES)
    col = (lax.axis_index("det") + step_col - 1) * width + iota(shape, 1) * PHASES + iota(shape, 0) // ROWS
    return 2.0 * (col.astype(F32) + 0.5) / (n_cols * width) - 1.0


def window(image_ref, row, col, rows, store):
    for k in range(SHIFTS):
        place_in = k + SIDE - HALF
        phase, shift = place_in % PHASES, place_in // PHASES
        if shift == 0:
            store(k, image_ref[phase, col, pl.ds(row, rows), :])
        else:
            pair = [image_ref[phase, col + i, pl.ds(row, rows), :] for i in range(2)]
            store(k, jnp.concatenate(pair, axis=1)[:, shift : shift + LANES])


def strips_kernel(
    n_rows, n_cols, patch_ref, row_ref, set_ref, top_ref, above_ref, here_ref, below_ref, bottom_ref,
    table_ref, strips_ref, diff_ref, centre_ref, image, models, data_hi, data_lo,
):
    height = here_ref.shape[0]
    width = PHASES * LANES
    n_strips, strip_rows, _ = strips_ref.shape
    per_set = table_ref.shape[1] // 2

    scatter = to_phases(width)
    first = 0
    for piece in (top_ref, above_ref, here_ref, below_ref, bottom_ref):
        rows = piece.shape[0]
        for b in range(4):
            cols = min(width, piece.shape[1] - b * width)
            hi, lo = split(piece[:, b * width : b * width + cols])
            pick = scatter if cols == width else scatter[:cols]
            moved = mxu(hi, pick) + mxu(lo, pick)
            for f in range(PHASES):
                image[f, b, first : first + rows, :] = moved[:, f * LANES : (f + 1) * LANES]
        first += rows
    for f in range(PHASES):
        centre_ref[f] = image[f, 1:3, height : height + centre_ref.shape[2], :]

    shape = (PHASES * ROWS, 2 * LANES)
    row_in = iota(shape, 0) % ROWS + iota(shape, 1) // LANES * ROWS

    def one_strip(t, carry):
        step_row, step_col = place(patch_ref[t, 0], n_cols)
        top = row_ref[t]
        row = step_row * height + top + EDGE - HALF

        def store(k, part):
            both = jnp.concatenate([part[0:WIN], part[ROWS : ROWS + WIN]], axis=1)
            hi, lo = split(both)
            data_hi[k * WIN : (k + 1) * WIN, :] = hi
            data_lo[k * WIN : (k + 1) * WIN, :] = lo

        window(image, row, step_col, WIN + ROWS, store)
        which = set_ref[t]
        big = mxu(table_ref[which], data_hi[...])
        terms = big[:per_set] + big[per_set:] + mxu(table_ref[which, 0:per_set, :], data_lo[...])
        terms = terms.reshape(6, PHASES * ROWS, 2 * LANES)
        one_u = columns_of(step_col, n_cols, width)
        u = jnp.concatenate([one_u, one_u], axis=1)
        y = (lax.axis_index("visit") + step_row - 1) * height + top + row_in
        v = 2.0 * (y.astype(F32) + 0.5) / (n_rows * height) - 1.0
        model = terms[0] + u * (terms[1] + u * terms[3] + v * terms[4]) + v * (terms[2] + v * terms[5])
        for half in range(2):
            for dx in range(PHASES):
                models[pl.ds(pl.multiple_of(t * strip_rows + half * ROWS, ROWS), ROWS), dx * LANES : (dx + 1) * LANES] = model[
                    dx * ROWS : (dx + 1) * ROWS, half * LANES : (half + 1) * LANES
                ]
        return carry

    lax.fori_loop(0, n_strips, one_strip, 0)

    gather = from_phases()
    some = 16
    for c in range(n_strips // some):
        hi, lo = split(models[c * some * strip_rows : (c + 1) * some * strip_rows, :])
        natural = mxu(hi, gather) + mxu(lo, gather)
        for i in range(some):
            diff_ref[c * some + i] = strips_ref[c * some + i] - natural[i * strip_rows : (i + 1) * strip_rows]


def coadd_kernel(n_rows, n_cols, flat_ref, centre_ref, mid_ref, left_ref, right_ref, coadd_ref, taps, wide, models, data_hi, data_lo):
    height, width = coadd_ref.shape
    total = mid_ref[...] + left_ref[...] + right_ref[...]
    counts = total[height:, 0:LANES].T
    n_sets = counts.shape[1]
    y = lax.axis_index("visit") * height + iota((height, 1), 0)
    v = 2.0 * (y.astype(F32) + 0.5) / (n_rows * height) - 1.0
    parts = [exact(counts, flat_ref[p * n_sets : (p + 1) * n_sets, :]) for p in range(6)]
    by_power = (parts[0] + v * (parts[2] + v * parts[5]), parts[1] + v * parts[4], parts[3])
    for a in range(3):
        for c in range(DEPTH // LANES):
            taps[c, a * height : (a + 1) * height, :] = by_power[a][:, c * LANES : (c + 1) * LANES]
    n = 3 * height // ROWS
    for dx in range(PHASES):
        for dy in range(ROWS):
            shift = dx * WIN + dy
            some = jnp.concatenate([taps[c, pl.ds(dy, n, stride=ROWS), :] for c in range(DEPTH // LANES)], axis=1)
            moved = some if shift == 0 else pltpu.roll(some, shift, 1)
            for c in range(DEPTH // LANES):
                wide[dx, c, pl.ds(dy, n, stride=ROWS), :] = moved[:, c * LANES : (c + 1) * LANES]
    one_u = columns_of(1, n_cols, width)

    def one_block(b, carry):
        def store(k, part):
            hi, lo = split(part)
            data_hi[k * WIN : (k + 1) * WIN, :] = hi
            data_lo[k * WIN : (k + 1) * WIN, :] = lo

        row = pl.multiple_of(b * ROWS, ROWS)
        window(centre_ref, row + EDGE - HALF, 0, WIN, store)
        mine = jnp.concatenate(
            [
                jnp.concatenate([wide[dx, c, pl.ds(a * height + row, ROWS), :] for c in range(DEPTH // LANES)], axis=1)
                for a in range(3)
                for dx in range(PHASES)
            ],
            axis=0,
        )
        hi, lo = split(mine)
        terms = mxu(hi, data_hi[...]) + mxu(lo, data_hi[...]) + mxu(hi, data_lo[...])
        terms = terms.reshape(3, PHASES * ROWS, LANES)
        model = terms[0] + one_u * (terms[1] + one_u * terms[2])
        for dx in range(PHASES):
            models[pl.ds(row, ROWS), dx * LANES : (dx + 1) * LANES] = model[dx * ROWS : (dx + 1) * ROWS]
        return carry

    lax.fori_loop(0, height // ROWS, one_block, 0)
    hi, lo = split(models[...])
    gather = from_phases()
    coadd_ref[...] = total[:height] - (mxu(hi, gather) + mxu(lo, gather))


def shifted(x, axis, by):
    size = lax.axis_size(axis)
    pairs = [(i, i + by) for i in range(size) if 0 <= i + by < size]
    return lax.ppermute(x, axis, pairs)


def per_device(strips, patch_of, box_row, kernel_set, template, row_taps, col_taps, kernel_coef):
    n_rows, n_cols = lax.axis_size("visit"), lax.axis_size("det")
    n_strips, strip_rows, width = strips.shape
    height = template.shape[0]
    n_sets, n_terms, n_basis = kernel_coef.shape
    rows_out = n_terms * PHASES * ROWS
    smem = pl.BlockSpec(memory_space=pltpu.SMEM)
    vmem = pl.BlockSpec(memory_space=pltpu.VMEM)
    params = pltpu.CompilerParams(vmem_limit_bytes=VMEM)

    left = shifted(template, "det", 1)
    right = shifted(template, "det", -1)
    far_left = shifted(template[:, width - SIDE :], "det", 2)
    far_right = shifted(template[:, :SIDE], "det", -2)

    sums = jax.ShapeDtypeStruct((3, height + ROWS, width), F32)
    up, mid, down = pl.pallas_call(
        functools.partial(sums_kernel, n_cols),
        out_shape=(sums, sums, sums),
        in_specs=[smem, smem, smem, vmem],
        out_specs=(vmem, vmem, vmem),
        scratch_shapes=[pltpu.VMEM((9, PHASES, height + ROWS, LANES), F32)],
        compiler_params=params,
        name="strip_sums",
    )(patch_of, box_row, kernel_set, strips)

    flat, table = pl.pallas_call(
        taps_kernel,
        out_shape=(
            jax.ShapeDtypeStruct((n_sets * n_terms, DEPTH), F32),
            jax.ShapeDtypeStruct((n_sets, 2 * rows_out, DEPTH), BF16),
        ),
        in_specs=[vmem, vmem, vmem],
        out_specs=(vmem, vmem),
        scratch_shapes=[pltpu.VMEM((DEPTH // LANES, n_sets * rows_out, LANES), F32)],
        compiler_params=params,
        name="tap_tables",
    )(row_taps, col_taps, jnp.swapaxes(kernel_coef, 0, 1).reshape(n_terms * n_sets, n_basis))

    here = jnp.concatenate([far_left, left, template, right, far_right], axis=1)
    above = shifted(here, "visit", 1)
    below = shifted(here, "visit", -1)
    top = shifted(here[height - EDGE :], "visit", 2)
    bottom = shifted(here[:EDGE], "visit", -2)

    mid = mid + shifted(down, "visit", 1) + shifted(up, "visit", -1)
    from_left = shifted(mid[2], "det", 1)
    from_right = shifted(mid[0], "det", -1)

    image_rows = 3 * height + 2 * EDGE
    flops = n_strips * 3 * rows_out * DEPTH * 2 * LANES * 2
    difference, centre = pl.pallas_call(
        functools.partial(strips_kernel, n_rows, n_cols),
        out_shape=(
            jax.ShapeDtypeStruct(strips.shape, F32),
            jax.ShapeDtypeStruct((PHASES, 2, height + 2 * EDGE, LANES), F32),
        ),
        in_specs=[smem] * 3 + [vmem] * 7,
        out_specs=(vmem, vmem),
        scratch_shapes=[
            pltpu.VMEM((PHASES, 4, image_rows, LANES), F32),
            pltpu.VMEM((n_strips * strip_rows, PHASES * LANES), F32),
            pltpu.VMEM((DEPTH, 2 * LANES), BF16),
            pltpu.VMEM((DEPTH, 2 * LANES), BF16),
        ],
        compiler_params=params,
        cost_estimate=pl.CostEstimate(flops=flops, bytes_accessed=14 << 20, transcendentals=0),
        name="strip_models",
    )(patch_of, box_row, kernel_set, top, above, here, below, bottom, table, strips)

    coadd = pl.pallas_call(
        functools.partial(coadd_kernel, n_rows, n_cols),
        out_shape=jax.ShapeDtypeStruct(template.shape, F32),
        in_specs=[vmem] * 5,
        out_specs=vmem,
        scratch_shapes=[
            pltpu.VMEM((DEPTH // LANES, 3 * height, LANES), F32),
            pltpu.VMEM((PHASES, DEPTH // LANES, 3 * height, LANES), F32),
            pltpu.VMEM((height, PHASES * LANES), F32),
            pltpu.VMEM((DEPTH, LANES), BF16),
            pltpu.VMEM((DEPTH, LANES), BF16),
        ],
        compiler_params=params,
        name="coadd_models",
    )(flat, centre, mid[1], from_left, from_right)
    return difference, coadd


def solution(mesh):
    tiles = ("visit", "det")
    in_specs = (P(tiles, None, None), P(tiles, None), P(tiles), P(tiles), P("visit", "det"), P(), P(), P())
    out_specs = (P(tiles, None, None), P("visit", "det"))
    return jax.shard_map(per_device, mesh=mesh, in_specs=in_specs, out_specs=out_specs, check_vma=False)
```

```python
import functools

import jax
import jax.numpy as jnp
from jax import lax
from jax.experimental import pallas as pl
from jax.experimental.pallas import tpu as pltpu
from jax.sharding import PartitionSpec as P

F32 = jnp.float32
BF16 = jnp.bfloat16
HIGHEST = lax.Precision.HIGHEST

HALF = 10
SIDE = 12
EDGE = 16
PHASES = 4
LANES = 128
ROWS = 8
WIN = 32
SHIFTS = 24
DEPTH = SHIFTS * WIN
TILES = DEPTH // LANES
VMEM = 56 * 1024 * 1024


def iota(shape, dim):
    return lax.broadcasted_iota(jnp.int32, shape, dim)


def split(x):
    hi = x.astype(BF16)
    lo = (x - hi.astype(F32)).astype(BF16)
    return hi, lo


def mxu(a, b):
    return jnp.dot(a, b, preferred_element_type=F32)


def exact(a, b):
    return jnp.dot(a, b, precision=HIGHEST, preferred_element_type=F32)


def to_phases(width):
    out = iota((width, PHASES * LANES), 1)
    source = (out % LANES) * PHASES + out // LANES
    return jnp.where(iota((width, PHASES * LANES), 0) == source, 1.0, 0.0).astype(BF16)


def from_phases():
    src = iota((PHASES * LANES, PHASES * LANES), 0)
    target = (src % LANES) * PHASES + src // LANES
    return jnp.where(iota((PHASES * LANES, PHASES * LANES), 1) == target, 1.0, 0.0).astype(BF16)


def place(patch, n_cols):
    step_row = (patch >> (n_cols.bit_length() - 1)) - lax.axis_index("visit") + 1
    step_col = (patch & (n_cols - 1)) - lax.axis_index("det") + 1
    return step_row, step_col


def prepare_kernel(
    n_cols, patch_ref, row_ref, set_ref, row_taps_ref, col_taps_ref, coef_ref, strips_hbm,
    left_ref, mid_ref, right_ref, flat_ref, table_ref, strips_ref, acc, wide, sem,
):
    copy_strips = pltpu.make_async_copy(strips_hbm, strips_ref, sem)
    copy_strips.start()

    taps = row_taps_ref.shape[0]
    lane = iota((taps, DEPTH), 1)
    sub = iota((taps, DEPTH), 0)
    row_part = exact(row_taps_ref[...].T, jnp.where(lane % WIN == sub, 1.0, 0.0))
    col_part = exact(col_taps_ref[...].T, jnp.where(lane // WIN == sub, 1.0, 0.0))
    flat = exact(coef_ref[...], row_part * col_part)
    flat_ref[...] = flat
    n = flat.shape[0]
    block = PHASES * ROWS
    for dy in range(ROWS):
        moved = flat if dy == 0 else pltpu.roll(flat, dy, 1)
        for c in range(TILES):
            wide[c, pl.ds(dy, n, stride=ROWS), :] = moved[:, c * LANES : (c + 1) * LANES]
    n_sets = table_ref.shape[0]
    n_terms = n // n_sets
    for s in range(n_sets):
        for p in range(n_terms):
            hi, lo = split(on_phases(wide, (p * n_sets + s) * ROWS))
            table_ref[s, p * block : (p + 1) * block, :] = hi
            table_ref[s, (n_terms + p) * block : (n_terms + p + 1) * block, :] = lo

    acc[...] = jnp.zeros(acc.shape, F32)
    copy_strips.wait()
    height = mid_ref.shape[1] - ROWS
    strip_rows = strips_ref.shape[1]
    place_lane = iota((ROWS, LANES), 1)
    place_sub = iota((ROWS, LANES), 0)

    def one_strip(t, carry):
        step_row, step_col = place(patch_ref[t], n_cols)
        top = row_ref[t]
        q = step_col * 3 + step_row
        for c in range(PHASES):
            acc[q, c, pl.ds(top, strip_rows), :] += strips_ref[t, :, c * LANES : (c + 1) * LANES]
        hit = (place_sub == set_ref[t]) & (place_lane >= top) & (place_lane < top + strip_rows)
        acc[q, 0, height:, :] += jnp.where(hit, 1.0, 0.0)
        return carry

    lax.fori_loop(0, strips_ref.shape[0], one_strip, 0, unroll=4)
    for i, out in enumerate((left_ref, mid_ref, right_ref)):
        for c in range(PHASES):
            out[:, :, c * LANES : (c + 1) * LANES] = acc[3 * i : 3 * i + 3, c]


def on_phases(wide, first):
    rows = jnp.concatenate([wide[c, pl.ds(first, ROWS), :] for c in range(TILES)], axis=1)
    return jnp.concatenate([rows] + [pltpu.roll(rows, dx * WIN, 1) for dx in range(1, PHASES)], axis=0)


def columns_of(step_col, n_cols, width):
    shape = (PHASES * ROWS, LANES)
    col = (lax.axis_index("det") + step_col - 1) * width + iota(shape, 1) * PHASES + iota(shape, 0) // ROWS
    return 2.0 * (col.astype(F32) + 0.5) / (n_cols * width) - 1.0


def fill(image_ref, row, col, halves, data_hi, data_lo):
    lane = iota((WIN, LANES), 1)
    for phase in range(PHASES):
        near, far = [image_ref[phase, col + i, pl.ds(row, WIN + (halves - 1) * ROWS), :] for i in range(2)]
        for half in range(halves):
            rows = slice(half * ROWS, half * ROWS + WIN)
            for a, b, data in zip(split(near[rows]), split(far[rows]), (data_hi, data_lo)):
                for shift in range((SIDE - HALF + SHIFTS - 1) // PHASES + 1):
                    k = shift * PHASES + phase - (SIDE - HALF)
                    if 0 <= k < SHIFTS:
                        part = a if shift == 0 else pltpu.roll(jnp.where(lane < shift, b, a), LANES - shift, 1)
                        data[k * WIN : (k + 1) * WIN, half * LANES : (half + 1) * LANES] = part


def strips_kernel(
    n_rows, n_cols, patch_ref, row_ref, set_ref, top_ref, above_ref, here_ref, below_ref, bottom_ref,
    table_hbm, strips_hbm, diff_hbm, centre_ref, table_ref, strips_ref, image, models, hi_a, lo_a, hi_b, lo_b, sems,
):
    copy_table = pltpu.make_async_copy(table_hbm, table_ref, sems.at[0])
    copy_strips = pltpu.make_async_copy(strips_hbm, strips_ref, sems.at[1])
    copy_table.start()
    copy_strips.start()
    height = here_ref.shape[0]
    width = PHASES * LANES
    n_strips, strip_rows, _ = strips_ref.shape
    per_set = table_ref.shape[1] // 2

    scatter = to_phases(width)
    pieces = (top_ref, above_ref, here_ref, below_ref, bottom_ref)
    rows = image.shape[2]
    for b in range(4):
        cols = min(width, here_ref.shape[1] - b * width)
        parts = [split(piece[:, b * width : b * width + cols]) for piece in pieces]
        both = jnp.concatenate([hi for hi, _ in parts] + [lo for _, lo in parts], axis=0)
        moved = mxu(both, scatter[:cols])
        moved = moved[:rows] + moved[rows:]
        for f in range(PHASES):
            image[f, b] = moved[:, f * LANES : (f + 1) * LANES]
    for f in range(PHASES):
        centre_ref[f] = image[f, 1:3, height : height + centre_ref.shape[2], :]

    shape = (PHASES * ROWS, 2 * LANES)
    row_in = iota(shape, 0) % ROWS + iota(shape, 1) // LANES * ROWS

    def build(t, data_hi, data_lo):
        step_row, step_col = place(patch_ref[t], n_cols)
        row = step_row * height + row_ref[t] + EDGE - HALF
        fill(image, row, step_col, 2, data_hi, data_lo)

    def multiply(t, data_hi, data_lo):
        step_row, step_col = place(patch_ref[t], n_cols)
        which = set_ref[t]
        big = mxu(table_ref[which], data_hi[...])
        terms = big[:per_set] + big[per_set:] + mxu(table_ref[which, 0:per_set, :], data_lo[...])
        terms = terms.reshape(6, PHASES * ROWS, 2 * LANES)
        one_u = columns_of(step_col, n_cols, width)
        u = jnp.concatenate([one_u, one_u], axis=1)
        y = (lax.axis_index("visit") + step_row - 1) * height + row_ref[t] + row_in
        v = 2.0 * (y.astype(F32) + 0.5) / (n_rows * height) - 1.0
        model = terms[0] + u * (terms[1] + u * terms[3] + v * terms[4]) + v * (terms[2] + v * terms[5])
        for half in range(2):
            rows_of = pl.ds(pl.multiple_of(t * strip_rows + half * ROWS, ROWS), ROWS)
            for dx in range(PHASES):
                models[rows_of, dx * LANES : (dx + 1) * LANES] = model[
                    dx * ROWS : (dx + 1) * ROWS, half * LANES : (half + 1) * LANES
                ]

    build(0, hi_a, lo_a)
    copy_table.wait()

    some = 4
    buffers = ((hi_a, lo_a), (hi_b, lo_b))

    def some_strips(i, carry):
        for j in range(some):
            t = some * i + j
            build(jnp.minimum(t + 1, n_strips - 1), *buffers[(j + 1) % 2])
            multiply(t, *buffers[j % 2])
        return carry

    lax.fori_loop(0, n_strips // some, some_strips, 0)

    copy_strips.wait()
    gather = from_phases()
    some = 16
    for c in range(n_strips // some):
        hi, lo = split(models[c * some * strip_rows : (c + 1) * some * strip_rows, :])
        natural = mxu(hi, gather) + mxu(lo, gather)
        part = pl.ds(c * some, some)
        strips_ref[part] = strips_ref[part] - natural.reshape(some, strip_rows, width)
        pltpu.make_async_copy(strips_ref.at[part], diff_hbm.at[part], sems.at[2 + c]).start()
    for c in range(n_strips // some):
        part = pl.ds(c * some, some)
        pltpu.make_async_copy(strips_ref.at[part], diff_hbm.at[part], sems.at[2 + c]).wait()


def coadd_kernel(n_rows, n_cols, flat_ref, centre_ref, mid_ref, above_ref, below_ref, coadd_ref, taps, wide, models, hi_a, lo_a, hi_b, lo_b):
    height, width = coadd_ref.shape
    total = mid_ref[...] + above_ref[...] + below_ref[...]
    counts = total[height:, 0:LANES].T.astype(BF16)
    n_sets = counts.shape[1]
    y = lax.axis_index("visit") * height + iota((height, 1), 0)
    v = 2.0 * (y.astype(F32) + 0.5) / (n_rows * height) - 1.0
    parts = []
    for p in range(6):
        hi, lo = split(flat_ref[p * n_sets : (p + 1) * n_sets, :])
        parts.append(mxu(counts, hi) + mxu(counts, lo))
    by_power = (parts[0] + v * (parts[2] + v * parts[5]), parts[1] + v * parts[4], parts[3])
    for a in range(3):
        for c in range(TILES):
            taps[c, a * height : (a + 1) * height, :] = by_power[a][:, c * LANES : (c + 1) * LANES]
    n = 3 * height // ROWS
    for dy in range(ROWS):
        some = jnp.concatenate([taps[c, pl.ds(dy, n, stride=ROWS), :] for c in range(TILES)], axis=1)
        moved = some if dy == 0 else pltpu.roll(some, dy, 1)
        for c in range(TILES):
            wide[c, pl.ds(dy, n, stride=ROWS), :] = moved[:, c * LANES : (c + 1) * LANES]
    one_u = columns_of(1, n_cols, width)

    def build(b, data_hi, data_lo):
        fill(centre_ref, b * ROWS + EDGE - HALF, 0, 1, data_hi, data_lo)

    def multiply(b, data_hi, data_lo):
        row = pl.multiple_of(b * ROWS, ROWS)
        parts = [split(on_phases(wide, a * height + row)) for a in range(3)]
        big = mxu(jnp.concatenate([hi for hi, _ in parts] + [lo for _, lo in parts], axis=0), data_hi[...])
        small = mxu(jnp.concatenate([hi for hi, _ in parts], axis=0), data_lo[...])
        terms = (big[: big.shape[0] // 2] + big[big.shape[0] // 2 :] + small).reshape(3, PHASES * ROWS, LANES)
        model = terms[0] + one_u * (terms[1] + one_u * terms[2])
        for dx in range(PHASES):
            models[pl.ds(row, ROWS), dx * LANES : (dx + 1) * LANES] = model[dx * ROWS : (dx + 1) * ROWS]

    n_blocks = height // ROWS
    build(0, hi_a, lo_a)

    def two_blocks(i, carry):
        b = 2 * i
        build(b + 1, hi_b, lo_b)
        multiply(b, hi_a, lo_a)
        build(jnp.minimum(b + 2, n_blocks - 1), hi_a, lo_a)
        multiply(b + 1, hi_b, lo_b)
        return carry

    lax.fori_loop(0, n_blocks // 2, two_blocks, 0)
    hi, lo = split(models[...])
    gather = from_phases()
    coadd_ref[...] = total[:height] - (mxu(hi, gather) + mxu(lo, gather))


def shifted(x, axis, by):
    size = lax.axis_size(axis)
    pairs = [(i, i + by) for i in range(size) if 0 <= i + by < size]
    return lax.ppermute(x, axis, pairs)


def per_device(strips, patch_of, box_row, kernel_set, template, row_taps, col_taps, kernel_coef):
    n_rows, n_cols = lax.axis_size("visit"), lax.axis_size("det")
    n_strips, strip_rows, width = strips.shape
    height = template.shape[0]
    n_sets, n_terms, n_basis = kernel_coef.shape
    rows_out = n_terms * PHASES * ROWS
    smem = pl.BlockSpec(memory_space=pltpu.SMEM)
    vmem = pl.BlockSpec(memory_space=pltpu.VMEM)
    hbm = pl.BlockSpec(memory_space=pl.ANY)
    params = pltpu.CompilerParams(vmem_limit_bytes=VMEM)

    patch_of = patch_of.reshape(n_strips)

    far_left = shifted(template[:, width - SIDE :], "det", 2)
    far_right = shifted(template[:, :SIDE], "det", -2)
    left = shifted(template, "det", 1)
    right = shifted(template, "det", -1)
    patch_of, far_left, far_right = lax.optimization_barrier((patch_of, far_left, far_right))

    sums = jax.ShapeDtypeStruct((3, height + ROWS, width), F32)
    for_left, mid, for_right, flat, table = pl.pallas_call(
        functools.partial(prepare_kernel, n_cols),
        out_shape=(
            sums,
            sums,
            sums,
            jax.ShapeDtypeStruct((n_sets * n_terms, DEPTH), F32),
            jax.ShapeDtypeStruct((n_sets, 2 * rows_out, DEPTH), BF16),
        ),
        in_specs=[smem] * 3 + [vmem] * 3 + [hbm],
        out_specs=(vmem,) * 5,
        scratch_shapes=[
            pltpu.VMEM(strips.shape, F32),
            pltpu.VMEM((9, PHASES, height + ROWS, LANES), F32),
            pltpu.VMEM((TILES, n_sets * n_terms * ROWS, LANES), F32),
            pltpu.SemaphoreType.DMA,
        ],
        compiler_params=params,
        cost_estimate=pl.CostEstimate(flops=6 << 30, bytes_accessed=10 << 20, transcendentals=0),
        name="prepare",
    )(
        patch_of, box_row, kernel_set, row_taps.T, col_taps.T,
        jnp.swapaxes(kernel_coef, 0, 1).reshape(n_terms * n_sets, n_basis), strips,
    )

    left, right, for_left, for_right = lax.optimization_barrier((left, right, for_left, for_right))
    blank = jnp.zeros((height, LANES - 2 * SIDE), F32)
    here = jnp.concatenate([far_left, left, template, right, far_right, blank], axis=1)
    above = shifted(here, "visit", 1)
    below = shifted(here, "visit", -1)
    top = shifted(here[height - EDGE :], "visit", 2)
    bottom = shifted(here[:EDGE], "visit", -2)

    mid = mid + shifted(for_right, "det", 1) + shifted(for_left, "det", -1)
    from_above = shifted(mid[2], "visit", 1)
    from_below = shifted(mid[0], "visit", -1)
    patch_of, mid = lax.optimization_barrier((patch_of, mid))

    image_rows = 3 * height + 2 * EDGE
    flops = n_strips * 3 * rows_out * DEPTH * 2 * LANES * 2
    difference, centre = pl.pallas_call(
        functools.partial(strips_kernel, n_rows, n_cols),
        out_shape=(
            jax.ShapeDtypeStruct(strips.shape, F32),
            jax.ShapeDtypeStruct((PHASES, 2, height + 2 * EDGE, LANES), F32),
        ),
        in_specs=[smem] * 3 + [vmem] * 5 + [hbm] * 2,
        out_specs=(hbm, vmem),
        scratch_shapes=[
            pltpu.VMEM(table.shape, BF16),
            pltpu.VMEM(strips.shape, F32),
            pltpu.VMEM((PHASES, 4, image_rows, LANES), F32),
            pltpu.VMEM((n_strips * strip_rows, PHASES * LANES), F32),
        ]
        + [pltpu.VMEM((DEPTH, 2 * LANES), BF16)] * 4
        + [pltpu.SemaphoreType.DMA((6,))],
        compiler_params=params,
        cost_estimate=pl.CostEstimate(flops=flops, bytes_accessed=14 << 20, transcendentals=0),
        name="strip_models",
    )(patch_of, box_row, kernel_set, top, above, here, below, bottom, table, strips)

    coadd = pl.pallas_call(
        functools.partial(coadd_kernel, n_rows, n_cols),
        out_shape=jax.ShapeDtypeStruct(template.shape, F32),
        in_specs=[vmem] * 5,
        out_specs=vmem,
        scratch_shapes=[
            pltpu.VMEM((TILES, 3 * height, LANES), F32),
            pltpu.VMEM((TILES, 3 * height, LANES), F32),
            pltpu.VMEM((height, PHASES * LANES), F32),
        ]
        + [pltpu.VMEM((DEPTH, LANES), BF16)] * 4,
        compiler_params=params,
        cost_estimate=pl.CostEstimate(flops=6 << 30, bytes_accessed=3 << 20, transcendentals=0),
        name="coadd_models",
    )(flat, centre, mid[1], from_above, from_below)
    return difference, coadd


def solution(mesh):
    tiles = ("visit", "det")
    in_specs = (P(tiles, None, None), P(tiles, None), P(tiles), P(tiles), P("visit", "det"), P(), P(), P())
    out_specs = (P(tiles, None, None), P("visit", "det"))
    return jax.shard_map(per_device, mesh=mesh, in_specs=in_specs, out_specs=out_specs, check_vma=False)
```

```python
import functools

import jax
import jax.numpy as jnp
from jax import lax
from jax.experimental import pallas as pl
from jax.experimental.pallas import tpu as pltpu
from jax.sharding import PartitionSpec as P

F32 = jnp.float32
BF16 = jnp.bfloat16
HIGHEST = lax.Precision.HIGHEST

HALF = 10
SIDE = 12
EDGE = 16
PHASES = 4
LANES = 128
ROWS = 8
WIN = 32
SHIFTS = 24
DEPTH = SHIFTS * WIN
TILES = DEPTH // LANES
VMEM = 56 * 1024 * 1024


def iota(shape, dim):
    return lax.broadcasted_iota(jnp.int32, shape, dim)


def split(x):
    hi = x.astype(BF16)
    lo = (x - hi.astype(F32)).astype(BF16)
    return hi, lo


def mxu(a, b):
    return jnp.dot(a, b, preferred_element_type=F32)


def exact(a, b):
    return jnp.dot(a, b, precision=HIGHEST, preferred_element_type=F32)


def to_phases(width):
    out = iota((width, PHASES * LANES), 1)
    source = (out % LANES) * PHASES + out // LANES
    return jnp.where(iota((width, PHASES * LANES), 0) == source, 1.0, 0.0).astype(BF16)


def from_phases():
    src = iota((PHASES * LANES, PHASES * LANES), 0)
    target = (src % LANES) * PHASES + src // LANES
    return jnp.where(iota((PHASES * LANES, PHASES * LANES), 1) == target, 1.0, 0.0).astype(BF16)


def place(patch, n_cols):
    step_row = (patch >> (n_cols.bit_length() - 1)) - lax.axis_index("visit") + 1
    step_col = (patch & (n_cols - 1)) - lax.axis_index("det") + 1
    return step_row, step_col


def prepare_kernel(
    n_cols, patch_ref, row_ref, set_ref, row_taps_ref, col_taps_ref, coef_ref, strips_hbm,
    even_ref, mid_ref, odd_ref, flat_ref, table_ref, strips_ref, acc, wide, sem,
):
    copy_strips = pltpu.make_async_copy(strips_hbm, strips_ref, sem)
    copy_strips.start()

    taps = row_taps_ref.shape[0]
    lane = iota((taps, DEPTH), 1)
    sub = iota((taps, DEPTH), 0)
    row_part = exact(row_taps_ref[...].T, jnp.where(lane % WIN == sub, 1.0, 0.0))
    col_part = exact(col_taps_ref[...].T, jnp.where(lane // WIN == sub, 1.0, 0.0))
    flat = exact(coef_ref[...], row_part * col_part)
    flat_ref[...] = flat
    n = flat.shape[0]
    block = PHASES * ROWS
    for dy in range(ROWS):
        moved = flat if dy == 0 else pltpu.roll(flat, dy, 1)
        for c in range(TILES):
            wide[c, pl.ds(dy, n, stride=ROWS), :] = moved[:, c * LANES : (c + 1) * LANES]
    n_sets = table_ref.shape[0]
    n_terms = n // n_sets
    for s in range(n_sets):
        for p in range(n_terms):
            hi, lo = split(on_phases(wide, (p * n_sets + s) * ROWS))
            table_ref[s, p * block : (p + 1) * block, :] = hi
            table_ref[s, (n_terms + p) * block : (n_terms + p + 1) * block, :] = lo

    acc[...] = jnp.zeros(acc.shape, F32)
    copy_strips.wait()
    height = mid_ref.shape[1] - ROWS
    strip_rows = strips_ref.shape[1]
    place_lane = iota((ROWS, LANES), 1)
    place_sub = iota((ROWS, LANES), 0)

    def one_strip(t, carry):
        step_row, step_col = place(patch_ref[t], n_cols)
        top = row_ref[t]
        q = step_col * 3 + step_row
        for c in range(PHASES):
            acc[q, c, pl.ds(top, strip_rows), :] += strips_ref[t, :, c * LANES : (c + 1) * LANES]
        hit = (place_sub == set_ref[t]) & (place_lane >= top) & (place_lane < top + strip_rows)
        acc[q, 0, height:, :] += jnp.where(hit, 1.0, 0.0)
        return carry

    lax.fori_loop(0, strips_ref.shape[0], one_strip, 0, unroll=4)
    parity = lax.axis_index("det") % 2
    for first, out in ((6 - 6 * parity, even_ref), (3, mid_ref), (6 * parity, odd_ref)):
        for c in range(PHASES):
            out[:, :, c * LANES : (c + 1) * LANES] = acc[pl.ds(first, 3), c]


def on_phases(wide, first):
    rows = jnp.concatenate([wide[c, pl.ds(first, ROWS), :] for c in range(TILES)], axis=1)
    return jnp.concatenate([rows] + [pltpu.roll(rows, dx * WIN, 1) for dx in range(1, PHASES)], axis=0)


def columns_of(step_col, n_cols, width):
    shape = (PHASES * ROWS, LANES)
    col = (lax.axis_index("det") + step_col - 1) * width + iota(shape, 1) * PHASES + iota(shape, 0) // ROWS
    return 2.0 * (col.astype(F32) + 0.5) / (n_cols * width) - 1.0


def fill(image_ref, row, col, halves, data_hi, data_lo):
    lane = iota((WIN, LANES), 1)
    for part, data in enumerate((data_hi, data_lo)):
        for phase in range(PHASES):
            near, far = [image_ref[part, phase, col + i, pl.ds(row, WIN + (halves - 1) * ROWS), :] for i in range(2)]
            for half in range(halves):
                rows = slice(half * ROWS, half * ROWS + WIN)
                a, b = near[rows].astype(BF16), far[rows].astype(BF16)
                for shift in range((SIDE - HALF + SHIFTS - 1) // PHASES + 1):
                    k = shift * PHASES + phase - (SIDE - HALF)
                    if 0 <= k < SHIFTS:
                        moved = a if shift == 0 else pltpu.roll(jnp.where(lane < shift, b, a), LANES - shift, 1)
                        data[k * WIN : (k + 1) * WIN, half * LANES : (half + 1) * LANES] = moved


def strips_kernel(
    n_rows, n_cols, patch_ref, row_ref, set_ref, near_rows, away_rows, here_ref, even_ref, odd_ref,
    table_hbm, strips_hbm, diff_hbm, centre_ref, table_ref, strips_ref, image, models, hi_a, lo_a, hi_b, lo_b, sems,
):
    copy_table = pltpu.make_async_copy(table_hbm, table_ref, sems.at[0])
    copy_strips = pltpu.make_async_copy(strips_hbm, strips_ref, sems.at[1])
    copy_table.start()
    copy_strips.start()
    height = here_ref.shape[0]
    width = PHASES * LANES
    n_strips, strip_rows, _ = strips_ref.shape
    per_set = table_ref.shape[1] // 2

    scatter = to_phases(width)
    rows = image.shape[3]
    upper = lax.axis_index("visit") % 2 == 0
    ahead = lax.axis_index("visit") % 4 < 2
    for b in range(4):
        cols = slice(b * width, min((b + 1) * width, here_ref.shape[1]))
        near, away, even, odd = [r[:, cols] for r in (near_rows, away_rows, even_ref, odd_ref)]
        pieces = (
            jnp.where(ahead, away, near),
            jnp.where(upper, odd, even),
            here_ref[:, cols],
            jnp.where(upper, even, odd),
            jnp.where(ahead, near, away),
        )
        parts = [split(piece) for piece in pieces]
        both = jnp.concatenate([hi for hi, _ in parts] + [lo for _, lo in parts], axis=0)
        moved = mxu(both, scatter[: cols.stop - cols.start])
        for f in range(PHASES):
            for part in range(2):
                image[part, f, b] = moved[part * rows : (part + 1) * rows, f * LANES : (f + 1) * LANES]
    centre_ref[...] = image[:, :, 1:3, height : height + centre_ref.shape[3], :]

    shape = (PHASES * ROWS, 2 * LANES)
    row_in = iota(shape, 0) % ROWS + iota(shape, 1) // LANES * ROWS

    def build(t, data_hi, data_lo):
        step_row, step_col = place(patch_ref[t], n_cols)
        row = step_row * height + row_ref[t] + EDGE - HALF
        fill(image, row, step_col, 2, data_hi, data_lo)

    def multiply(t, data_hi, data_lo):
        step_row, step_col = place(patch_ref[t], n_cols)
        which = set_ref[t]
        big = mxu(table_ref[which], data_hi[...])
        terms = big[:per_set] + big[per_set:] + mxu(table_ref[which, 0:per_set, :], data_lo[...])
        terms = terms.reshape(6, PHASES * ROWS, 2 * LANES)
        one_u = columns_of(step_col, n_cols, width)
        u = jnp.concatenate([one_u, one_u], axis=1)
        y = (lax.axis_index("visit") + step_row - 1) * height + row_ref[t] + row_in
        v = 2.0 * (y.astype(F32) + 0.5) / (n_rows * height) - 1.0
        model = terms[0] + u * (terms[1] + u * terms[3] + v * terms[4]) + v * (terms[2] + v * terms[5])
        for half in range(2):
            rows_of = pl.ds(pl.multiple_of(t * strip_rows + half * ROWS, ROWS), ROWS)
            for dx in range(PHASES):
                models[rows_of, dx * LANES : (dx + 1) * LANES] = model[
                    dx * ROWS : (dx + 1) * ROWS, half * LANES : (half + 1) * LANES
                ]

    build(0, hi_a, lo_a)
    copy_table.wait()

    some = 4
    buffers = ((hi_a, lo_a), (hi_b, lo_b))

    def some_strips(i, carry):
        for j in range(some):
            t = some * i + j
            build(jnp.minimum(t + 1, n_strips - 1), *buffers[(j + 1) % 2])
            multiply(t, *buffers[j % 2])
        return carry

    lax.fori_loop(0, n_strips // some, some_strips, 0)

    copy_strips.wait()
    gather = from_phases()
    some = 16
    for c in range(n_strips // some):
        hi, lo = split(models[c * some * strip_rows : (c + 1) * some * strip_rows, :])
        natural = mxu(hi, gather) + mxu(lo, gather)
        part = pl.ds(c * some, some)
        strips_ref[part] = strips_ref[part] - natural.reshape(some, strip_rows, width)
        pltpu.make_async_copy(strips_ref.at[part], diff_hbm.at[part], sems.at[2 + c]).start()
    for c in range(n_strips // some):
        part = pl.ds(c * some, some)
        pltpu.make_async_copy(strips_ref.at[part], diff_hbm.at[part], sems.at[2 + c]).wait()


def coadd_kernel(n_rows, n_cols, flat_ref, centre_ref, mid_ref, even_ref, odd_ref, coadd_ref, taps, wide, models, hi_a, lo_a, hi_b, lo_b):
    height, width = coadd_ref.shape
    total = mid_ref[...] + even_ref[...] + odd_ref[...]
    counts = total[height:, 0:LANES].T.astype(BF16)
    n_sets = counts.shape[1]
    y = lax.axis_index("visit") * height + iota((height, 1), 0)
    v = 2.0 * (y.astype(F32) + 0.5) / (n_rows * height) - 1.0
    parts = []
    for p in range(6):
        hi, lo = split(flat_ref[p * n_sets : (p + 1) * n_sets, :])
        parts.append(mxu(counts, hi) + mxu(counts, lo))
    by_power = (parts[0] + v * (parts[2] + v * parts[5]), parts[1] + v * parts[4], parts[3])
    for a in range(3):
        for c in range(TILES):
            taps[c, a * height : (a + 1) * height, :] = by_power[a][:, c * LANES : (c + 1) * LANES]
    n = 3 * height // ROWS
    for dy in range(ROWS):
        some = jnp.concatenate([taps[c, pl.ds(dy, n, stride=ROWS), :] for c in range(TILES)], axis=1)
        moved = some if dy == 0 else pltpu.roll(some, dy, 1)
        for c in range(TILES):
            wide[c, pl.ds(dy, n, stride=ROWS), :] = moved[:, c * LANES : (c + 1) * LANES]
    one_u = columns_of(1, n_cols, width)

    def build(b, data_hi, data_lo):
        fill(centre_ref, b * ROWS + EDGE - HALF, 0, 1, data_hi, data_lo)

    def multiply(b, data_hi, data_lo):
        row = pl.multiple_of(b * ROWS, ROWS)
        parts = [split(on_phases(wide, a * height + row)) for a in range(3)]
        big = mxu(jnp.concatenate([hi for hi, _ in parts] + [lo for _, lo in parts], axis=0), data_hi[...])
        small = mxu(jnp.concatenate([hi for hi, _ in parts], axis=0), data_lo[...])
        terms = (big[: big.shape[0] // 2] + big[big.shape[0] // 2 :] + small).reshape(3, PHASES * ROWS, LANES)
        model = terms[0] + one_u * (terms[1] + one_u * terms[2])
        for dx in range(PHASES):
            models[pl.ds(row, ROWS), dx * LANES : (dx + 1) * LANES] = model[dx * ROWS : (dx + 1) * ROWS]

    n_blocks = height // ROWS
    build(0, hi_a, lo_a)

    some = 8
    buffers = ((hi_a, lo_a), (hi_b, lo_b))

    def some_blocks(i, carry):
        for j in range(some):
            b = some * i + j
            build(jnp.minimum(b + 1, n_blocks - 1), *buffers[(j + 1) % 2])
            multiply(b, *buffers[j % 2])
        return carry

    lax.fori_loop(0, n_blocks // some, some_blocks, 0)
    hi, lo = split(models[...])
    gather = from_phases()
    coadd_ref[...] = total[:height] - (mxu(hi, gather) + mxu(lo, gather))


def swap(x, axis, apart, first):
    size = lax.axis_size(axis)
    lower = [i for i in range(size - apart) if (i - first) % (2 * apart) < apart]
    pairs = [(i, i + apart) for i in lower] + [(i + apart, i) for i in lower]
    return lax.ppermute(x, axis, pairs)


def per_device(strips, patch_of, box_row, kernel_set, template, row_taps, col_taps, kernel_coef):
    n_rows, n_cols = lax.axis_size("visit"), lax.axis_size("det")
    n_strips, strip_rows, width = strips.shape
    height = template.shape[0]
    n_sets, n_terms, n_basis = kernel_coef.shape
    rows_out = n_terms * PHASES * ROWS
    smem = pl.BlockSpec(memory_space=pltpu.SMEM)
    vmem = pl.BlockSpec(memory_space=pltpu.VMEM)
    hbm = pl.BlockSpec(memory_space=pl.ANY)
    params = pltpu.CompilerParams(vmem_limit_bytes=VMEM)

    patch_of = patch_of.reshape(n_strips)

    v, d = lax.axis_index("visit"), lax.axis_index("det")
    first, last = template[:, :SIDE], template[:, width - SIDE :]
    ahead = d % 4 < 2
    near = swap(jnp.where(ahead, last, first), "det", 2, 0)
    away = swap(jnp.where(ahead, first, last), "det", 2, 2)
    even = swap(template, "det", 1, 0)
    odd = swap(template, "det", 1, 1)
    patch_of, near, away = lax.optimization_barrier((patch_of, near, away))

    sums = jax.ShapeDtypeStruct((3, height + ROWS, width), F32)
    for_even, mid, for_odd, flat, table = pl.pallas_call(
        functools.partial(prepare_kernel, n_cols),
        out_shape=(
            sums,
            sums,
            sums,
            jax.ShapeDtypeStruct((n_sets * n_terms, DEPTH), F32),
            jax.ShapeDtypeStruct((n_sets, 2 * rows_out, DEPTH), BF16),
        ),
        in_specs=[smem] * 3 + [vmem] * 3 + [hbm],
        out_specs=(vmem,) * 5,
        scratch_shapes=[
            pltpu.VMEM(strips.shape, F32),
            pltpu.VMEM((9, PHASES, height + ROWS, LANES), F32),
            pltpu.VMEM((TILES, n_sets * n_terms * ROWS, LANES), F32),
            pltpu.SemaphoreType.DMA,
        ],
        compiler_params=params,
        cost_estimate=pl.CostEstimate(flops=6 << 30, bytes_accessed=10 << 20, transcendentals=0),
        name="prepare",
    )(
        patch_of, box_row, kernel_set, row_taps.T, col_taps.T,
        jnp.swapaxes(kernel_coef, 0, 1).reshape(n_terms * n_sets, n_basis), strips,
    )

    even, odd, for_even, for_odd = lax.optimization_barrier((even, odd, for_even, for_odd))
    far_left, far_right = jnp.where(ahead, away, near), jnp.where(ahead, near, away)
    left, right = jnp.where(d % 2 == 0, odd, even), jnp.where(d % 2 == 0, even, odd)
    blank = jnp.zeros((height, LANES - 2 * SIDE), F32)
    here = jnp.concatenate([far_left, left, template, right, far_right, blank], axis=1)

    first, last = here[:EDGE], here[height - EDGE :]
    ahead = v % 4 < 2
    near_rows = swap(jnp.where(ahead, last, first), "visit", 2, 0)
    away_rows = swap(jnp.where(ahead, first, last), "visit", 2, 2)
    even = swap(here, "visit", 1, 0)
    odd = swap(here, "visit", 1, 1)

    near_rows, away_rows, for_even, for_odd = lax.optimization_barrier((near_rows, away_rows, for_even, for_odd))
    sum_even = swap(for_even, "det", 1, 0)
    sum_odd = swap(for_odd, "det", 1, 1)

    image_rows = 3 * height + 2 * EDGE
    flops = n_strips * 3 * rows_out * DEPTH * 2 * LANES * 2
    difference, centre = pl.pallas_call(
        functools.partial(strips_kernel, n_rows, n_cols),
        out_shape=(
            jax.ShapeDtypeStruct(strips.shape, F32),
            jax.ShapeDtypeStruct((2, PHASES, 2, height + 2 * EDGE, LANES), F32),
        ),
        in_specs=[smem] * 3 + [vmem] * 5 + [hbm] * 2,
        out_specs=(hbm, vmem),
        scratch_shapes=[
            pltpu.VMEM(table.shape, BF16),
            pltpu.VMEM(strips.shape, F32),
            pltpu.VMEM((2, PHASES, 4, image_rows, LANES), F32),
            pltpu.VMEM((n_strips * strip_rows, PHASES * LANES), F32),
        ]
        + [pltpu.VMEM((DEPTH, 2 * LANES), BF16)] * 4
        + [pltpu.SemaphoreType.DMA((6,))],
        compiler_params=params,
        cost_estimate=pl.CostEstimate(flops=flops, bytes_accessed=14 << 20, transcendentals=0),
        name="strip_models",
    )(patch_of, box_row, kernel_set, near_rows, away_rows, here, even, odd, table, strips)

    centre, sum_even, sum_odd = lax.optimization_barrier((centre, sum_even, sum_odd))
    mid = mid + sum_even + sum_odd
    from_even = swap(jnp.where(v % 2 == 0, mid[2], mid[0]), "visit", 1, 0)
    from_odd = swap(jnp.where(v % 2 == 0, mid[0], mid[2]), "visit", 1, 1)

    coadd = pl.pallas_call(
        functools.partial(coadd_kernel, n_rows, n_cols),
        out_shape=jax.ShapeDtypeStruct(template.shape, F32),
        in_specs=[vmem] * 5,
        out_specs=vmem,
        scratch_shapes=[
            pltpu.VMEM((TILES, 3 * height, LANES), F32),
            pltpu.VMEM((TILES, 3 * height, LANES), F32),
            pltpu.VMEM((height, PHASES * LANES), F32),
        ]
        + [pltpu.VMEM((DEPTH, LANES), BF16)] * 4,
        compiler_params=params,
        cost_estimate=pl.CostEstimate(flops=6 << 30, bytes_accessed=3 << 20, transcendentals=0),
        name="coadd_models",
    )(flat, centre, mid[1], from_even, from_odd)
    return difference, coadd


def solution(mesh):
    tiles = ("visit", "det")
    in_specs = (P(tiles, None, None), P(tiles, None), P(tiles), P(tiles), P("visit", "det"), P(), P(), P())
    out_specs = (P(tiles, None, None), P("visit", "det"))
    return jax.shard_map(per_device, mesh=mesh, in_specs=in_specs, out_specs=out_specs, check_vma=False)
```

```python
import functools

import jax
import jax.numpy as jnp
from jax import lax
from jax.experimental import pallas as pl
from jax.experimental.pallas import tpu as pltpu
from jax.sharding import PartitionSpec as P

F32 = jnp.float32
BF16 = jnp.bfloat16
F8 = jnp.float8_e4m3fn
HIGHEST = lax.Precision.HIGHEST

HALF = 10
SIDE = 12
EDGE = 16
PHASES = 4
LANES = 128
ROWS = 8
WIN = 32
SHIFTS = 24
DEPTH = SHIFTS * WIN
TILES = DEPTH // LANES
FINE = 3
SCALE = 2.0**14
TOP = 256.0
MIB = 1024 * 1024


def iota(shape, dim):
    return lax.broadcasted_iota(jnp.int32, shape, dim)


def split(x):
    hi = x.astype(BF16)
    lo = (x - hi.astype(F32)).astype(BF16)
    return hi, lo


def mxu(a, b):
    return jnp.dot(a, b, preferred_element_type=F32)


def exact(a, b):
    return jnp.dot(a, b, precision=HIGHEST, preferred_element_type=F32)


def to_phases(width):
    out = iota((width, PHASES * LANES), 1)
    source = (out % LANES) * PHASES + out // LANES
    return jnp.where(iota((width, PHASES * LANES), 0) == source, 1.0, 0.0).astype(BF16)


def from_phases():
    src = iota((PHASES * LANES, PHASES * LANES), 0)
    target = (src % LANES) * PHASES + src // LANES
    return jnp.where(iota((PHASES * LANES, PHASES * LANES), 1) == target, 1.0, 0.0).astype(BF16)


def place(patch, n_cols):
    step_row = (patch >> (n_cols.bit_length() - 1)) - lax.axis_index("visit") + 1
    step_col = (patch & (n_cols - 1)) - lax.axis_index("det") + 1
    return step_row, step_col


def sums_kernel(n_cols, patch_ref, row_ref, set_ref, strips_ref, even_ref, mid_ref, odd_ref, acc):
    acc[...] = jnp.zeros(acc.shape, F32)
    height = mid_ref.shape[1] - ROWS
    strip_rows = strips_ref.shape[1]
    place_lane = iota((ROWS, LANES), 1)
    place_sub = iota((ROWS, LANES), 0)

    def one_strip(t, carry):
        step_row, step_col = place(patch_ref[t], n_cols)
        top = row_ref[t]
        q = step_col * 3 + step_row
        for c in range(PHASES):
            acc[q, c, pl.ds(top, strip_rows), :] += strips_ref[t, :, c * LANES : (c + 1) * LANES]
        hit = (place_sub == set_ref[t]) & (place_lane >= top) & (place_lane < top + strip_rows)
        acc[q, 0, height:, :] += jnp.where(hit, 1.0, 0.0)
        return carry

    lax.fori_loop(0, strips_ref.shape[0], one_strip, 0, unroll=4)
    parity = lax.axis_index("det") % 2
    for first, out in ((6 - 6 * parity, even_ref), (3, mid_ref), (6 * parity, odd_ref)):
        for c in range(PHASES):
            out[:, :, c * LANES : (c + 1) * LANES] = acc[pl.ds(first, 3), c]


def taps_kernel(
    n_rows, n_cols, row_taps_ref, col_taps_ref, coef_ref, flat_ref, table_ref, table8_ref, top_ref, wide
):
    taps = row_taps_ref.shape[0]
    lane = iota((taps, DEPTH), 1)
    sub = iota((taps, DEPTH), 0)
    row_part = exact(row_taps_ref[...].T, jnp.where(lane % WIN == sub, 1.0, 0.0))
    col_part = exact(col_taps_ref[...].T, jnp.where(lane // WIN == sub, 1.0, 0.0))
    n_sets = table_ref.shape[0]
    one, u, v, uu, uv, vv = [coef_ref[p * n_sets : (p + 1) * n_sets, :] for p in range(6)]
    u0 = (2 * lax.axis_index("det") + 1).astype(F32) / n_cols - 1.0
    v0 = (2 * lax.axis_index("visit") + 1).astype(F32) / n_rows - 1.0
    one, u, v = (
        one + u0 * (u + u0 * uu) + v0 * (v + u0 * uv + v0 * vv),
        u + 2.0 * u0 * uu + v0 * uv,
        v + u0 * uv + 2.0 * v0 * vv,
    )
    flat = exact(jnp.concatenate([one, v, u, uu, uv, vv], axis=0), row_part * col_part)
    flat_ref[...] = flat
    top = jnp.maximum(jnp.max(jnp.max(jnp.abs(flat), axis=1, keepdims=True), axis=0, keepdims=True), 1e-30)
    top_ref[...] = jnp.broadcast_to(top, top_ref.shape)
    scale = TOP / top
    n = flat.shape[0]
    block = PHASES * ROWS
    for dy in range(ROWS):
        moved = flat if dy == 0 else pltpu.roll(flat, dy, 1)
        for c in range(TILES):
            wide[c, pl.ds(dy, n, stride=ROWS), :] = moved[:, c * LANES : (c + 1) * LANES]
    for s in range(n_sets):
        for p in range(6):
            rows = on_phases(wide, (p * n_sets + s) * ROWS)
            hi = rows.astype(BF16)
            table_ref[s, p * block : (p + 1) * block, :] = hi
            if p < FINE:
                table_ref[s, (6 + p) * block : (7 + p) * block, :] = (rows - hi.astype(F32)).astype(BF16)
                table8_ref[s, p * block : (p + 1) * block, :] = (rows * scale).astype(F8)


def on_phases(wide, first):
    rows = jnp.concatenate([wide[c, pl.ds(first, ROWS), :] for c in range(TILES)], axis=1)
    return jnp.concatenate([rows] + [pltpu.roll(rows, dx * WIN, 1) for dx in range(1, PHASES)], axis=0)


def columns_of(step_col, n_cols, width):
    shape = (PHASES * ROWS, LANES)
    col = (step_col - 1) * width - width // 2 + iota(shape, 1) * PHASES + iota(shape, 0) // ROWS
    return 2.0 * (col.astype(F32) + 0.5) / (n_cols * width)


def fill(image_ref, part, row, col, halves, kind, data):
    lane = iota((WIN, LANES), 1)
    for phase in range(PHASES):
        near, far = [image_ref[part, phase, col + i, pl.ds(row, WIN + (halves - 1) * ROWS), :] for i in range(2)]
        for half in range(halves):
            rows = slice(half * ROWS, half * ROWS + WIN)
            a, b = near[rows].astype(kind), far[rows].astype(kind)
            for shift in range((SIDE - HALF + SHIFTS - 1) // PHASES + 1):
                k = shift * PHASES + phase - (SIDE - HALF)
                if 0 <= k < SHIFTS:
                    moved = a if shift == 0 else pltpu.roll(jnp.where(lane < shift, b, a), LANES - shift, 1)
                    data[k * WIN : (k + 1) * WIN, half * LANES : (half + 1) * LANES] = moved


def strips_kernel(
    n_rows, n_cols, patch_ref, row_ref, set_ref, near_rows, away_rows, here_ref, even_ref, odd_ref,
    top_ref, table8_ref, table_hbm, strips_hbm, diff_hbm, centre_ref, table_ref, strips_ref, image, models,
    hi_a, lo_a, hi_b, lo_b, sems,
):
    copy_table = pltpu.make_async_copy(table_hbm, table_ref, sems.at[0])
    copy_strips = pltpu.make_async_copy(strips_hbm, strips_ref, sems.at[1])
    copy_table.start()
    copy_strips.start()
    height = here_ref.shape[0]
    width = PHASES * LANES
    n_strips, strip_rows, _ = strips_ref.shape
    block = PHASES * ROWS
    fine = FINE * block

    scatter = to_phases(width)
    rows = image.shape[3]
    upper = lax.axis_index("visit") % 2 == 0
    ahead = lax.axis_index("visit") % 4 < 2
    for b in range(4):
        cols = slice(b * width, min((b + 1) * width, here_ref.shape[1]))
        near, away, even, odd = [r[:, cols] for r in (near_rows, away_rows, even_ref, odd_ref)]
        pieces = (
            jnp.where(ahead, away, near),
            jnp.where(upper, odd, even),
            here_ref[:, cols],
            jnp.where(upper, even, odd),
            jnp.where(ahead, near, away),
        )
        parts = [split(piece) for piece in pieces]
        both = jnp.concatenate([hi for hi, _ in parts] + [lo for _, lo in parts], axis=0)
        moved = mxu(both, scatter[: cols.stop - cols.start])
        for f in range(PHASES):
            for part in range(2):
                some = moved[part * rows : (part + 1) * rows, f * LANES : (f + 1) * LANES]
                image[part, f, b] = some * SCALE if part else some
    centre_ref[...] = image[:, :, 1:3, height : height + centre_ref.shape[3], :]

    shape = (PHASES * ROWS, 2 * LANES)
    row_in = iota(shape, 0) % ROWS + iota(shape, 1) // LANES * ROWS

    undo = top_ref[0, 0] * (1.0 / (TOP * SCALE))

    def build(t, data_hi, data_lo):
        step_row, step_col = place(patch_ref[t], n_cols)
        row = step_row * height + row_ref[t] + EDGE - HALF
        fill(image, 0, row, step_col, 2, BF16, data_hi)
        fill(image, 1, row, step_col, 2, F8, data_lo)

    def multiply(t, data_hi, data_lo):
        step_row, step_col = place(patch_ref[t], n_cols)
        which = set_ref[t]
        big = mxu(table_ref[which], data_hi[...])
        small = mxu(table8_ref[which], data_lo[...])
        exact_terms = big[:fine] + big[6 * block :] + small * undo
        term_1, term_v, term_u = [exact_terms[p * block : (p + 1) * block] for p in range(FINE)]
        term_uu, term_uv, term_vv = [big[p * block : (p + 1) * block] for p in range(FINE, 6)]
        one_u = columns_of(step_col, n_cols, width)
        u = jnp.concatenate([one_u, one_u], axis=1)
        y = (step_row - 1) * height - height // 2 + row_ref[t] + row_in
        v = 2.0 * (y.astype(F32) + 0.5) / (n_rows * height)
        model = term_1 + u * (term_u + u * term_uu + v * term_uv) + v * (term_v + v * term_vv)
        for half in range(2):
            rows_of = pl.ds(pl.multiple_of(t * strip_rows + half * ROWS, ROWS), ROWS)
            for dx in range(PHASES):
                models[rows_of, dx * LANES : (dx + 1) * LANES] = model[
                    dx * ROWS : (dx + 1) * ROWS, half * LANES : (half + 1) * LANES
                ]

    build(0, hi_a, lo_a)
    copy_table.wait()
    some = 4
    buffers = ((hi_a, lo_a), (hi_b, lo_b))

    def some_strips(i, carry):
        for j in range(some):
            t = some * i + j
            build(jnp.minimum(t + 1, n_strips - 1), *buffers[(j + 1) % 2])
            multiply(t, *buffers[j % 2])
        return carry

    lax.fori_loop(0, n_strips // some, some_strips, 0)

    copy_strips.wait()
    gather = from_phases()
    gather = jnp.concatenate([gather, gather], axis=0)
    some = 16
    for c in range(n_strips // some):
        both = split(models[c * some * strip_rows : (c + 1) * some * strip_rows, :])
        natural = mxu(jnp.concatenate(both, axis=1), gather)
        part = pl.ds(c * some, some)
        strips_ref[part] = strips_ref[part] - natural.reshape(some, strip_rows, width)
        pltpu.make_async_copy(strips_ref.at[part], diff_hbm.at[part], sems.at[2 + c]).start()
    for c in range(n_strips // some):
        part = pl.ds(c * some, some)
        pltpu.make_async_copy(strips_ref.at[part], diff_hbm.at[part], sems.at[2 + c]).wait()


def coadd_kernel(n_rows, n_cols, flat_ref, centre_ref, mid_ref, even_ref, odd_ref, coadd_ref, taps, wide, models, hi_a, lo_a, hi_b, lo_b):
    height, width = coadd_ref.shape
    total = mid_ref[...] + even_ref[...] + odd_ref[...]
    count = total[height:, 0:LANES]
    n_sets = count.shape[0]
    v = 2.0 * ((iota(count.shape, 1) - height // 2).astype(F32) + 0.5) / (n_rows * height)

    def three(x, p):
        taps_of = flat_ref[p * n_sets : (p + 1) * n_sets, :]
        x_hi, t_hi = x.astype(BF16).astype(F32), taps_of.astype(BF16).astype(F32)
        return [(x_hi, t_hi), (x - x_hi, t_hi), (x_hi, taps_of - t_hi)]

    by_power = []
    for terms in ((0, 1, 5), (2, 4), (3,)):
        rows, x = [], count
        for p in terms:
            rows, x = rows + three(x, p), x * v
        sides = [jnp.concatenate(side, axis=0) for side in zip(*rows)]
        by_power.append(mxu(sides[0].T.astype(BF16), sides[1].astype(BF16)))
    for a in range(3):
        for c in range(TILES):
            taps[c, a * height : (a + 1) * height, :] = by_power[a][:, c * LANES : (c + 1) * LANES]
    n = 3 * height // ROWS
    for dy in range(ROWS):
        some = jnp.concatenate([taps[c, pl.ds(dy, n, stride=ROWS), :] for c in range(TILES)], axis=1)
        moved = some if dy == 0 else pltpu.roll(some, dy, 1)
        for c in range(TILES):
            wide[c, pl.ds(dy, n, stride=ROWS), :] = moved[:, c * LANES : (c + 1) * LANES]
    one_u = columns_of(1, n_cols, width)

    def build(b, data_hi, data_lo):
        fill(centre_ref, 0, b * ROWS + EDGE - HALF, 0, 1, BF16, data_hi)
        fill(centre_ref, 1, b * ROWS + EDGE - HALF, 0, 1, BF16, data_lo)

    def multiply(b, data_hi, data_lo):
        row = pl.multiple_of(b * ROWS, ROWS)
        fine_hi, fine_lo = split(on_phases(wide, row))
        rest = [on_phases(wide, a * height + row).astype(BF16) for a in (1, 2)]
        big = mxu(jnp.concatenate([fine_hi] + rest + [fine_lo], axis=0), data_hi[...])
        terms = big.reshape(4, PHASES * ROWS, LANES)
        small = mxu(fine_hi, data_lo[...]) * (1.0 / SCALE)
        model = terms[0] + terms[3] + small + one_u * (terms[1] + one_u * terms[2])
        for dx in range(PHASES):
            models[pl.ds(row, ROWS), dx * LANES : (dx + 1) * LANES] = model[dx * ROWS : (dx + 1) * ROWS]

    n_blocks = height // ROWS
    build(0, hi_a, lo_a)
    some = 8
    buffers = ((hi_a, lo_a), (hi_b, lo_b))

    def some_blocks(i, carry):
        for j in range(some):
            b = some * i + j
            build(jnp.minimum(b + 1, n_blocks - 1), *buffers[(j + 1) % 2])
            multiply(b, *buffers[j % 2])
        return carry

    lax.fori_loop(0, n_blocks // some, some_blocks, 0)
    hi, lo = split(models[...])
    gather = from_phases()
    coadd_ref[...] = total[:height] - (mxu(hi, gather) + mxu(lo, gather))


def swap(x, axis, apart, first):
    size = lax.axis_size(axis)
    lower = [i for i in range(size - apart) if (i - first) % (2 * apart) < apart]
    pairs = [(i, i + apart) for i in lower] + [(i + apart, i) for i in lower]
    return lax.ppermute(x, axis, pairs)


def per_device(strips, patch_of, box_row, kernel_set, template, row_taps, col_taps, kernel_coef):
    n_rows, n_cols = lax.axis_size("visit"), lax.axis_size("det")
    n_strips, strip_rows, width = strips.shape
    height = template.shape[0]
    n_sets, n_terms, n_basis = kernel_coef.shape
    block = PHASES * ROWS
    smem = pl.BlockSpec(memory_space=pltpu.SMEM)
    vmem = pl.BlockSpec(memory_space=pltpu.VMEM)
    hbm = pl.BlockSpec(memory_space=pl.ANY)

    patch_of = patch_of.reshape(n_strips)

    v, d = lax.axis_index("visit"), lax.axis_index("det")
    first, last = template[:, :SIDE], template[:, width - SIDE :]
    ahead = d % 4 < 2
    near = swap(jnp.where(ahead, last, first), "det", 2, 0)
    away = swap(jnp.where(ahead, first, last), "det", 2, 2)
    even = swap(template, "det", 1, 0)
    odd = swap(template, "det", 1, 1)
    patch_of, near, away = lax.optimization_barrier((patch_of, near, away))

    sums = jax.ShapeDtypeStruct((3, height + ROWS, width), F32)
    for_even, mid, for_odd = pl.pallas_call(
        functools.partial(sums_kernel, n_cols),
        out_shape=(sums, sums, sums),
        in_specs=[smem] * 3 + [vmem],
        out_specs=(vmem,) * 3,
        scratch_shapes=[pltpu.VMEM((9, PHASES, height + ROWS, LANES), F32)],
        compiler_params=pltpu.CompilerParams(vmem_limit_bytes=16 * MIB),
        cost_estimate=pl.CostEstimate(flops=3 << 30, bytes_accessed=5 << 20, transcendentals=0),
        name="strip_sums",
    )(patch_of, box_row, kernel_set, strips)

    even, odd, for_even, for_odd, row_taps = lax.optimization_barrier((even, odd, for_even, for_odd, row_taps))
    far_left, far_right = jnp.where(ahead, away, near), jnp.where(ahead, near, away)
    left, right = jnp.where(d % 2 == 0, odd, even), jnp.where(d % 2 == 0, even, odd)
    blank = jnp.zeros((height, LANES - 2 * SIDE), F32)
    here = jnp.concatenate([far_left, left, template, right, far_right, blank], axis=1)

    first, last = here[:EDGE], here[height - EDGE :]
    ahead = v % 4 < 2
    near_rows = swap(jnp.where(ahead, last, first), "visit", 2, 0)
    away_rows = swap(jnp.where(ahead, first, last), "visit", 2, 2)
    flat, table, table8, top = pl.pallas_call(
        functools.partial(taps_kernel, n_rows, n_cols),
        out_shape=(
            jax.ShapeDtypeStruct((n_sets * n_terms, DEPTH), F32),
            jax.ShapeDtypeStruct((n_sets, (n_terms + FINE) * block, DEPTH), BF16),
            jax.ShapeDtypeStruct((n_sets, FINE * block, DEPTH), F8),
            jax.ShapeDtypeStruct((ROWS, LANES), F32),
        ),
        in_specs=[vmem] * 3,
        out_specs=(vmem,) * 4,
        scratch_shapes=[pltpu.VMEM((TILES, n_sets * n_terms * ROWS, LANES), F32)],
        compiler_params=pltpu.CompilerParams(vmem_limit_bytes=16 * MIB),
        cost_estimate=pl.CostEstimate(flops=3 << 30, bytes_accessed=5 << 20, transcendentals=0),
        name="tap_tables",
    )(row_taps.T, col_taps.T, jnp.swapaxes(kernel_coef, 0, 1).reshape(n_terms * n_sets, n_basis))

    near_rows, away_rows, here, for_even, for_odd, flat = lax.optimization_barrier(
        (near_rows, away_rows, here, for_even, for_odd, flat)
    )
    even = swap(here, "visit", 1, 0)
    odd = swap(here, "visit", 1, 1)

    sum_even = swap(for_even, "det", 1, 0)
    sum_odd = swap(for_odd, "det", 1, 1)

    image_rows = 3 * height + 2 * EDGE
    flops = n_strips * 2 * n_terms * block * DEPTH * 2 * LANES * 2
    difference, centre = pl.pallas_call(
        functools.partial(strips_kernel, n_rows, n_cols),
        out_shape=(
            jax.ShapeDtypeStruct(strips.shape, F32),
            jax.ShapeDtypeStruct((2, PHASES, 2, height + 2 * EDGE, LANES), F32),
        ),
        in_specs=[smem] * 3 + [vmem] * 5 + [smem, vmem] + [hbm] * 2,
        out_specs=(hbm, vmem),
        scratch_shapes=[
            pltpu.VMEM(table.shape, BF16),
            pltpu.VMEM(strips.shape, F32),
            pltpu.VMEM((2, PHASES, 4, image_rows, LANES), F32),
            pltpu.VMEM((n_strips * strip_rows, PHASES * LANES), F32),
        ]
        + [pltpu.VMEM((DEPTH, 2 * LANES), kind) for kind in (BF16, F8, BF16, F8)]
        + [pltpu.SemaphoreType.DMA((6,))],
        compiler_params=pltpu.CompilerParams(vmem_limit_bytes=34 * MIB),
        cost_estimate=pl.CostEstimate(flops=flops, bytes_accessed=14 << 20, transcendentals=0),
        name="strip_models",
    )(patch_of, box_row, kernel_set, near_rows, away_rows, here, even, odd, top, table8, table, strips)

    centre, sum_even, sum_odd = lax.optimization_barrier((centre, sum_even, sum_odd))
    mid = mid + sum_even + sum_odd
    from_even = swap(jnp.where(v % 2 == 0, mid[2], mid[0]), "visit", 1, 0)
    from_odd = swap(jnp.where(v % 2 == 0, mid[0], mid[2]), "visit", 1, 1)

    coadd = pl.pallas_call(
        functools.partial(coadd_kernel, n_rows, n_cols),
        out_shape=jax.ShapeDtypeStruct(template.shape, F32),
        in_specs=[vmem] * 5,
        out_specs=vmem,
        scratch_shapes=[
            pltpu.VMEM((TILES, 3 * height, LANES), F32),
            pltpu.VMEM((TILES, 3 * height, LANES), F32),
            pltpu.VMEM((height, PHASES * LANES), F32),
        ]
        + [pltpu.VMEM((DEPTH, LANES), BF16)] * 4,
        compiler_params=pltpu.CompilerParams(vmem_limit_bytes=16 * MIB),
        cost_estimate=pl.CostEstimate(flops=6 << 30, bytes_accessed=3 << 20, transcendentals=0),
        name="coadd_models",
    )(flat, centre, mid[1], from_even, from_odd)
    return difference, coadd


def solution(mesh):
    tiles = ("visit", "det")
    in_specs = (P(tiles, None, None), P(tiles, None), P(tiles), P(tiles), P("visit", "det"), P(), P(), P())
    out_specs = (P(tiles, None, None), P("visit", "det"))
    return jax.shard_map(per_device, mesh=mesh, in_specs=in_specs, out_specs=out_specs, check_vma=False)
```

```python
import functools

import jax
import jax.numpy as jnp
from jax import lax
from jax.experimental import pallas as pl
from jax.experimental.pallas import tpu as pltpu
from jax.sharding import PartitionSpec as P

F32 = jnp.float32
BF16 = jnp.bfloat16
F8 = jnp.float8_e4m3fn
HIGHEST = lax.Precision.HIGHEST

HALF = 10
SIDE = 12
EDGE = 16
PHASES = 4
LANES = 128
ROWS = 8
WIN = 32
SHIFTS = 24
DEPTH = SHIFTS * WIN
TILES = DEPTH // LANES
FINE = 3
SCALE = 2.0**14
TOP = 256.0
MIB = 1024 * 1024


def iota(shape, dim):
    return lax.broadcasted_iota(jnp.int32, shape, dim)


def split(x):
    hi = x.astype(BF16)
    lo = (x - hi.astype(F32)).astype(BF16)
    return hi, lo


def mxu(a, b):
    return jnp.dot(a, b, preferred_element_type=F32)


def exact(a, b):
    return jnp.dot(a, b, precision=HIGHEST, preferred_element_type=F32)


def to_phases(width):
    out = iota((width, PHASES * LANES), 1)
    source = (out % LANES) * PHASES + out // LANES
    return jnp.where(iota((width, PHASES * LANES), 0) == source, 1.0, 0.0).astype(BF16)


def from_phases():
    src = iota((PHASES * LANES, PHASES * LANES), 0)
    target = (src % LANES) * PHASES + src // LANES
    return jnp.where(iota((PHASES * LANES, PHASES * LANES), 1) == target, 1.0, 0.0).astype(BF16)


def place(patch, n_cols):
    step_row = (patch >> (n_cols.bit_length() - 1)) - lax.axis_index("visit") + 1
    step_col = (patch & (n_cols - 1)) - lax.axis_index("det") + 1
    return step_row, step_col


def sums_kernel(n_cols, patch_ref, row_ref, set_ref, strips_hbm, even_ref, mid_ref, odd_ref, strips_ref, acc, sems):
    n_strips, strip_rows, _ = strips_ref.shape
    n_parts = 4
    some = n_strips // n_parts
    copies = []
    for i in range(n_parts):
        part = pl.ds(i * some, some)
        copies.append(pltpu.make_async_copy(strips_hbm.at[part], strips_ref.at[part], sems.at[i]))
        copies[i].start()
    acc[...] = jnp.zeros(acc.shape, F32)
    height = acc.shape[2] - ROWS
    place_lane = iota((ROWS, LANES), 1)
    place_sub = iota((ROWS, LANES), 0)

    def one_strip(t, carry):
        step_row, step_col = place(patch_ref[t], n_cols)
        top = row_ref[t]
        q = step_col * 3 + step_row
        for c in range(PHASES):
            acc[q, c, pl.ds(top, strip_rows), :] += strips_ref[t, :, c * LANES : (c + 1) * LANES]
        hit = (place_sub == set_ref[t]) & (place_lane >= top) & (place_lane < top + strip_rows)
        acc[q, 0, height:, :] += jnp.where(hit, 1.0, 0.0)
        return carry

    for i in range(n_parts):
        copies[i].wait()
        lax.fori_loop(i * some, (i + 1) * some, one_strip, 0, unroll=4)
    parity = lax.axis_index("det") % 2
    for first, out in ((6 - 6 * parity, even_ref), (3, mid_ref), (6 * parity, odd_ref)):
        out[...] = acc[pl.ds(first, 3)]


def taps_kernel(
    n_rows, n_cols, row_taps_ref, col_taps_ref, coef_ref, flat_ref, table_ref, table8_ref, top_ref, wide
):
    taps = row_taps_ref.shape[0]
    lane = iota((taps, DEPTH), 1)
    sub = iota((taps, DEPTH), 0)
    row_part = exact(row_taps_ref[...].T, jnp.where(lane % WIN == sub, 1.0, 0.0))
    col_part = exact(col_taps_ref[...].T, jnp.where(lane // WIN == sub, 1.0, 0.0))
    n_sets = table_ref.shape[0]
    one, u, v, uu, uv, vv = [coef_ref[p * n_sets : (p + 1) * n_sets, :] for p in range(6)]
    u0 = (2 * lax.axis_index("det") + 1).astype(F32) / n_cols - 1.0
    v0 = (2 * lax.axis_index("visit") + 1).astype(F32) / n_rows - 1.0
    one, u, v = (
        one + u0 * (u + u0 * uu) + v0 * (v + u0 * uv + v0 * vv),
        u + 2.0 * u0 * uu + v0 * uv,
        v + u0 * uv + 2.0 * v0 * vv,
    )
    flat = exact(jnp.concatenate([one, v, u, uu, uv, vv], axis=0), row_part * col_part)
    flat_ref[...] = flat
    top = jnp.maximum(jnp.max(jnp.max(jnp.abs(flat), axis=1, keepdims=True), axis=0, keepdims=True), 1e-30)
    top_ref[...] = jnp.broadcast_to(top, top_ref.shape)
    scale = TOP / top
    n = flat.shape[0]
    block = PHASES * ROWS
    for dy in range(ROWS):
        moved = flat if dy == 0 else pltpu.roll(flat, dy, 1)
        for c in range(TILES):
            wide[c, pl.ds(dy, n, stride=ROWS), :] = moved[:, c * LANES : (c + 1) * LANES]
    for s in range(n_sets):
        for p in range(6):
            rows = on_phases(wide, (p * n_sets + s) * ROWS)
            hi = rows.astype(BF16)
            table_ref[s, p * block : (p + 1) * block, :] = hi
            if p < FINE:
                table_ref[s, (6 + p) * block : (7 + p) * block, :] = (rows - hi.astype(F32)).astype(BF16)
                table8_ref[s, p * block : (p + 1) * block, :] = (rows * scale).astype(F8)


def on_phases(wide, first):
    rows = jnp.concatenate([wide[c, pl.ds(first, ROWS), :] for c in range(TILES)], axis=1)
    return jnp.concatenate([rows] + [pltpu.roll(rows, dx * WIN, 1) for dx in range(1, PHASES)], axis=0)


def columns_of(step_col, n_cols, width):
    shape = (PHASES * ROWS, LANES)
    col = (step_col - 1) * width - width // 2 + iota(shape, 1) * PHASES + iota(shape, 0) // ROWS
    return 2.0 * (col.astype(F32) + 0.5) / (n_cols * width)


def fill(image_ref, part, row, col, halves, kind, data):
    lane = iota((WIN, LANES), 1)
    for phase in range(PHASES):
        near, far = [image_ref[part, phase, col + i, pl.ds(row, WIN + (halves - 1) * ROWS), :] for i in range(2)]
        for half in range(halves):
            rows = slice(half * ROWS, half * ROWS + WIN)
            a, b = near[rows].astype(kind), far[rows].astype(kind)
            for shift in range((SIDE - HALF + SHIFTS - 1) // PHASES + 1):
                k = shift * PHASES + phase - (SIDE - HALF)
                if 0 <= k < SHIFTS:
                    moved = a if shift == 0 else pltpu.roll(jnp.where(lane < shift, b, a), LANES - shift, 1)
                    data[k * WIN : (k + 1) * WIN, half * LANES : (half + 1) * LANES] = moved


def strips_kernel(
    n_rows, n_cols, patch_ref, row_ref, set_ref, top_ref, near_hbm, away_hbm, here_hbm, even_hbm, odd_hbm,
    table8_ref, table_ref, strips_hbm, diff_hbm, centre_hbm,
    near_rows, away_rows, here_ref, even_ref, odd_ref, strips_ref, centre_ref, image, models,
    hi_a, lo_a, hi_b, lo_b, in_sems, sems,
):
    inputs = [
        pltpu.make_async_copy(source, target, in_sems.at[i])
        for i, (source, target) in enumerate(
            (
                (here_hbm, here_ref),
                (even_hbm, even_ref),
                (odd_hbm, odd_ref),
                (near_hbm, near_rows),
                (away_hbm, away_rows),
                (strips_hbm, strips_ref),
            )
        )
    ]
    for copy in inputs:
        copy.start()
    height = here_ref.shape[0]
    width = PHASES * LANES
    n_strips, strip_rows, _ = strips_ref.shape
    block = PHASES * ROWS
    fine = FINE * block

    scatter = to_phases(width)
    rows = image.shape[3]
    upper = lax.axis_index("visit") % 2 == 0
    ahead = lax.axis_index("visit") % 4 < 2
    for copy in inputs[:5]:
        copy.wait()
    for b in range(4):
        cols = slice(b * width, min((b + 1) * width, here_ref.shape[1]))
        near, away, even, odd = [r[:, cols] for r in (near_rows, away_rows, even_ref, odd_ref)]
        pieces = (
            jnp.where(ahead, away, near),
            jnp.where(upper, odd, even),
            here_ref[:, cols],
            jnp.where(upper, even, odd),
            jnp.where(ahead, near, away),
        )
        parts = [split(piece) for piece in pieces]
        both = jnp.concatenate([hi for hi, _ in parts] + [lo for _, lo in parts], axis=0)
        moved = mxu(both, scatter[: cols.stop - cols.start])
        for f in range(PHASES):
            for part in range(2):
                some = moved[part * rows : (part + 1) * rows, f * LANES : (f + 1) * LANES]
                image[part, f, b] = some * SCALE if part else some
    centre_ref[...] = image[:, :, 1:3, height : height + centre_ref.shape[3], :]
    copy_centre = pltpu.make_async_copy(centre_ref, centre_hbm, sems.at[4])
    copy_centre.start()

    shape = (PHASES * ROWS, 2 * LANES)
    row_in = iota(shape, 0) % ROWS + iota(shape, 1) // LANES * ROWS

    undo = top_ref[0:1, 0:1] * (1.0 / (TOP * SCALE))

    def build(t, data_hi, data_lo):
        step_row, step_col = place(patch_ref[t], n_cols)
        row = step_row * height + row_ref[t] + EDGE - HALF
        fill(image, 0, row, step_col, 2, BF16, data_hi)
        fill(image, 1, row, step_col, 2, F8, data_lo)

    def multiply(t, data_hi, data_lo):
        step_row, step_col = place(patch_ref[t], n_cols)
        which = set_ref[t]
        big = mxu(table_ref[which], data_hi[...])
        small = mxu(table8_ref[which], data_lo[...])
        exact_terms = big[:fine] + big[6 * block :] + small * undo
        term_1, term_v, term_u = [exact_terms[p * block : (p + 1) * block] for p in range(FINE)]
        term_uu, term_uv, term_vv = [big[p * block : (p + 1) * block] for p in range(FINE, 6)]
        one_u = columns_of(step_col, n_cols, width)
        u = jnp.concatenate([one_u, one_u], axis=1)
        y = (step_row - 1) * height - height // 2 + row_ref[t] + row_in
        v = 2.0 * (y.astype(F32) + 0.5) / (n_rows * height)
        model = term_1 + u * (term_u + u * term_uu + v * term_uv) + v * (term_v + v * term_vv)
        for half in range(2):
            rows_of = pl.ds(pl.multiple_of(t * strip_rows + half * ROWS, ROWS), ROWS)
            for dx in range(PHASES):
                models[rows_of, dx * LANES : (dx + 1) * LANES] = model[
                    dx * ROWS : (dx + 1) * ROWS, half * LANES : (half + 1) * LANES
                ]

    build(0, hi_a, lo_a)
    some = 4
    buffers = ((hi_a, lo_a), (hi_b, lo_b))

    def some_strips(i, carry):
        for j in range(some):
            t = some * i + j
            build(jnp.minimum(t + 1, n_strips - 1), *buffers[(j + 1) % 2])
            multiply(t, *buffers[j % 2])
        return carry

    lax.fori_loop(0, n_strips // some, some_strips, 0)

    inputs[5].wait()
    gather = from_phases()
    gather = jnp.concatenate([gather, gather], axis=0)
    some = 16
    for c in range(n_strips // some):
        both = split(models[c * some * strip_rows : (c + 1) * some * strip_rows, :])
        natural = mxu(jnp.concatenate(both, axis=1), gather)
        part = pl.ds(c * some, some)
        strips_ref[part] = strips_ref[part] - natural.reshape(some, strip_rows, width)
        pltpu.make_async_copy(strips_ref.at[part], diff_hbm.at[part], sems.at[c]).start()
    for c in range(n_strips // some):
        part = pl.ds(c * some, some)
        pltpu.make_async_copy(strips_ref.at[part], diff_hbm.at[part], sems.at[c]).wait()
    copy_centre.wait()


def coadd_kernel(
    n_rows, n_cols, flat_ref, centre_hbm, mid_any, even_any, odd_any, coadd_ref,
    centre_ref, mid_ref, even_ref, odd_ref, taps, wide, models, hi_a, lo_a, hi_b, lo_b, sems,
):
    height, width = coadd_ref.shape
    sources = (mid_any, even_any, odd_any, centre_hbm)
    targets = (mid_ref, even_ref, odd_ref, centre_ref)
    copies = [pltpu.make_async_copy(source, target, sems.at[i]) for i, (source, target) in enumerate(zip(sources, targets))]
    for copy in copies:
        copy.start()
    for copy in copies[:3]:
        copy.wait()
    count = mid_ref[0, height:, :] + even_ref[0, height:, :] + odd_ref[0, height:, :]
    n_sets = count.shape[0]
    v = 2.0 * ((iota(count.shape, 1) - height // 2).astype(F32) + 0.5) / (n_rows * height)

    def three(x, p):
        taps_of = flat_ref[p * n_sets : (p + 1) * n_sets, :]
        x_hi, t_hi = x.astype(BF16).astype(F32), taps_of.astype(BF16).astype(F32)
        return [(x_hi, t_hi), (x - x_hi, t_hi), (x_hi, taps_of - t_hi)]

    by_power = []
    for terms in ((0, 1, 5), (2, 4), (3,)):
        rows, x = [], count
        for p in terms:
            rows, x = rows + three(x, p), x * v
        sides = [jnp.concatenate(side, axis=0) for side in zip(*rows)]
        by_power.append(mxu(sides[0].T.astype(BF16), sides[1].astype(BF16)))
    for a in range(3):
        for c in range(TILES):
            taps[c, a * height : (a + 1) * height, :] = by_power[a][:, c * LANES : (c + 1) * LANES]
    n = 3 * height // ROWS
    for dy in range(ROWS):
        some = jnp.concatenate([taps[c, pl.ds(dy, n, stride=ROWS), :] for c in range(TILES)], axis=1)
        moved = some if dy == 0 else pltpu.roll(some, dy, 1)
        for c in range(TILES):
            wide[c, pl.ds(dy, n, stride=ROWS), :] = moved[:, c * LANES : (c + 1) * LANES]
    one_u = columns_of(1, n_cols, width)

    def build(b, data_hi, data_lo):
        fill(centre_ref, 0, b * ROWS + EDGE - HALF, 0, 1, BF16, data_hi)
        fill(centre_ref, 1, b * ROWS + EDGE - HALF, 0, 1, BF16, data_lo)

    def multiply(b, data_hi, data_lo):
        row = pl.multiple_of(b * ROWS, ROWS)
        fine_hi, fine_lo = split(on_phases(wide, row))
        rest = [on_phases(wide, a * height + row).astype(BF16) for a in (1, 2)]
        big = mxu(jnp.concatenate([fine_hi] + rest + [fine_lo], axis=0), data_hi[...])
        terms = big.reshape(4, PHASES * ROWS, LANES)
        small = mxu(fine_hi, data_lo[...]) * (1.0 / SCALE)
        model = terms[0] + terms[3] + small + one_u * (terms[1] + one_u * terms[2])
        for dx in range(PHASES):
            models[pl.ds(row, ROWS), dx * LANES : (dx + 1) * LANES] = model[dx * ROWS : (dx + 1) * ROWS]

    n_blocks = height // ROWS
    copies[3].wait()
    build(0, hi_a, lo_a)
    some = 8
    buffers = ((hi_a, lo_a), (hi_b, lo_b))

    def some_blocks(i, carry):
        for j in range(some):
            b = some * i + j
            build(jnp.minimum(b + 1, n_blocks - 1), *buffers[(j + 1) % 2])
            multiply(b, *buffers[j % 2])
        return carry

    lax.fori_loop(0, n_blocks // some, some_blocks, 0)
    gather = from_phases()
    gather = jnp.concatenate([gather, gather], axis=0)
    natural = mxu(jnp.concatenate(split(models[...]), axis=1), gather)
    for c in range(PHASES):
        total = mid_ref[c, 0:height, :] + even_ref[c, 0:height, :] + odd_ref[c, 0:height, :]
        coadd_ref[:, c * LANES : (c + 1) * LANES] = total - natural[:, c * LANES : (c + 1) * LANES]


def swap(x, axis, apart, first):
    size = lax.axis_size(axis)
    lower = [i for i in range(size - apart) if (i - first) % (2 * apart) < apart]
    pairs = [(i, i + apart) for i in lower] + [(i + apart, i) for i in lower]
    return lax.ppermute(x, axis, pairs)


def per_device(strips, patch_of, box_row, kernel_set, template, row_taps, col_taps, kernel_coef):
    n_rows, n_cols = lax.axis_size("visit"), lax.axis_size("det")
    n_strips, strip_rows, width = strips.shape
    height = template.shape[0]
    n_sets, n_terms, n_basis = kernel_coef.shape
    block = PHASES * ROWS
    smem = pl.BlockSpec(memory_space=pltpu.SMEM)
    vmem = pl.BlockSpec(memory_space=pltpu.VMEM)
    hbm = pl.BlockSpec(memory_space=pltpu.HBM)
    free = pl.BlockSpec(memory_space=pl.ANY)

    patch_of = patch_of.reshape(n_strips)

    v, d = lax.axis_index("visit"), lax.axis_index("det")
    first, last = template[:, :SIDE], template[:, width - SIDE :]
    ahead = d % 4 < 2
    near = swap(jnp.where(ahead, last, first), "det", 2, 0)
    away = swap(jnp.where(ahead, first, last), "det", 2, 2)
    even = swap(template, "det", 1, 0)
    odd = swap(template, "det", 1, 1)

    sums = jax.ShapeDtypeStruct((3, PHASES, height + ROWS, LANES), F32)
    far_left, far_right = jnp.where(ahead, away, near), jnp.where(ahead, near, away)
    left, right = jnp.where(d % 2 == 0, odd, even), jnp.where(d % 2 == 0, even, odd)
    blank = jnp.zeros((height, LANES - 2 * SIDE), F32)
    here = jnp.concatenate([far_left, left, template, right, far_right, blank], axis=1)

    patch_of, row_taps, here = lax.optimization_barrier((patch_of, row_taps, here))
    odd = swap(here, "visit", 1, 1)
    even = swap(here, "visit", 1, 0)
    first, last = here[:EDGE], here[height - EDGE :]
    ahead = v % 4 < 2
    near_rows = swap(jnp.where(ahead, last, first), "visit", 2, 0)
    away_rows = swap(jnp.where(ahead, first, last), "visit", 2, 2)

    for_even, mid, for_odd = pl.pallas_call(
        functools.partial(sums_kernel, n_cols),
        out_shape=(sums, sums, sums),
        in_specs=[smem] * 3 + [hbm],
        out_specs=(vmem,) * 3,
        scratch_shapes=[
            pltpu.VMEM(strips.shape, F32),
            pltpu.VMEM((9, PHASES, height + ROWS, LANES), F32),
            pltpu.SemaphoreType.DMA((4,)),
        ],
        compiler_params=pltpu.CompilerParams(vmem_limit_bytes=56 * MIB),
        cost_estimate=pl.CostEstimate(flops=3 << 30, bytes_accessed=5 << 20, transcendentals=0),
        name="strip_sums",
    )(patch_of, box_row, kernel_set, strips)

    sum_even = swap(for_even, "det", 1, 0)
    sum_odd = swap(for_odd, "det", 1, 1)

    flat, table, table8, top = pl.pallas_call(
        functools.partial(taps_kernel, n_rows, n_cols),
        out_shape=(
            pltpu.VMEM((n_sets * n_terms, DEPTH), F32),
            pltpu.VMEM((n_sets, (n_terms + FINE) * block, DEPTH), BF16),
            pltpu.VMEM((n_sets, FINE * block, DEPTH), F8),
            pltpu.VMEM((ROWS, LANES), F32),
        ),
        in_specs=[vmem] * 3,
        out_specs=(vmem,) * 4,
        scratch_shapes=[pltpu.VMEM((TILES, n_sets * n_terms * ROWS, LANES), F32)],
        compiler_params=pltpu.CompilerParams(vmem_limit_bytes=56 * MIB),
        cost_estimate=pl.CostEstimate(flops=3 << 30, bytes_accessed=5 << 20, transcendentals=0),
        name="tap_tables",
    )(row_taps.T, col_taps.T, jnp.swapaxes(kernel_coef, 0, 1).reshape(n_terms * n_sets, n_basis))

    flat, table, table8, top = [
        pltpu.with_memory_space_constraint(x, pltpu.VMEM) for x in (flat, table, table8, top)
    ]

    image_rows = 3 * height + 2 * EDGE
    flops = n_strips * 2 * n_terms * block * DEPTH * 2 * LANES * 2
    difference, centre = pl.pallas_call(
        functools.partial(strips_kernel, n_rows, n_cols),
        out_shape=(
            jax.ShapeDtypeStruct(strips.shape, F32),
            jax.ShapeDtypeStruct((2, PHASES, 2, height + 2 * EDGE, LANES), F32),
        ),
        in_specs=[smem] * 3 + [vmem] + [free] * 5 + [vmem] * 2 + [hbm],
        out_specs=(hbm, hbm),
        scratch_shapes=[pltpu.VMEM(x.shape, F32) for x in (near_rows, away_rows, here, even, odd)]
        + [
            pltpu.VMEM(strips.shape, F32),
            pltpu.VMEM((2, PHASES, 2, height + 2 * EDGE, LANES), F32),
            pltpu.VMEM((2, PHASES, 4, image_rows, LANES), F32),
            pltpu.VMEM((n_strips * strip_rows, PHASES * LANES), F32),
        ]
        + [pltpu.VMEM((DEPTH, 2 * LANES), kind) for kind in (BF16, F8, BF16, F8)]
        + [pltpu.SemaphoreType.DMA((6,)), pltpu.SemaphoreType.DMA((5,))],
        compiler_params=pltpu.CompilerParams(vmem_limit_bytes=40 * MIB),
        cost_estimate=pl.CostEstimate(flops=flops, bytes_accessed=14 << 20, transcendentals=0),
        name="strip_models",
    )(patch_of, box_row, kernel_set, top, near_rows, away_rows, here, even, odd, table8, table, strips)

    centre, sum_even, sum_odd = lax.optimization_barrier((centre, sum_even, sum_odd))
    mid = mid + sum_even + sum_odd
    from_even = swap(jnp.where(v % 2 == 0, mid[2], mid[0]), "visit", 1, 0)
    from_odd = swap(jnp.where(v % 2 == 0, mid[0], mid[2]), "visit", 1, 1)

    coadd = pl.pallas_call(
        functools.partial(coadd_kernel, n_rows, n_cols),
        out_shape=jax.ShapeDtypeStruct(template.shape, F32),
        in_specs=[vmem, hbm] + [free] * 3,
        out_specs=vmem,
        scratch_shapes=[pltpu.VMEM(x.shape, F32) for x in (centre, from_even, from_even, from_odd)]
        + [
            pltpu.VMEM((TILES, 3 * height, LANES), F32),
            pltpu.VMEM((TILES, 3 * height, LANES), F32),
            pltpu.VMEM((height, PHASES * LANES), F32),
        ]
        + [pltpu.VMEM((DEPTH, LANES), BF16)] * 4
        + [pltpu.SemaphoreType.DMA((4,))],
        compiler_params=pltpu.CompilerParams(vmem_limit_bytes=32 * MIB),
        cost_estimate=pl.CostEstimate(flops=6 << 30, bytes_accessed=3 << 20, transcendentals=0),
        name="coadd_models",
    )(flat, centre, mid[1], from_even, from_odd)
    return difference, coadd


def solution(mesh):
    tiles = ("visit", "det")
    in_specs = (P(tiles, None, None), P(tiles, None), P(tiles), P(tiles), P("visit", "det"), P(), P(), P())
    out_specs = (P(tiles, None, None), P("visit", "det"))
    return jax.shard_map(per_device, mesh=mesh, in_specs=in_specs, out_specs=out_specs, check_vma=False)
```

```python
import functools

import jax
import jax.numpy as jnp
from jax import lax
from jax.experimental import pallas as pl
from jax.experimental.pallas import tpu as pltpu
from jax.sharding import PartitionSpec as P

F32 = jnp.float32
BF16 = jnp.bfloat16
F8 = jnp.float8_e4m3fn
HIGHEST = lax.Precision.HIGHEST

HALF = 10
SIDE = 12
EDGE = 16
PHASES = 4
LANES = 128
ROWS = 8
WIN = 32
SHIFTS = 24
DEPTH = SHIFTS * WIN
TILES = DEPTH // LANES
LATER = 8
FINE = 3
SCALE = 2.0**14
TOP = 256.0
MIB = 1024 * 1024


def iota(shape, dim):
    return lax.broadcasted_iota(jnp.int32, shape, dim)


def split(x):
    hi = x.astype(BF16)
    lo = (x - hi.astype(F32)).astype(BF16)
    return hi, lo


def mxu(a, b):
    return jnp.dot(a, b, preferred_element_type=F32)


def exact(a, b):
    return jnp.dot(a, b, precision=HIGHEST, preferred_element_type=F32)


def to_phases(width):
    out = iota((width, PHASES * LANES), 1)
    source = (out % LANES) * PHASES + out // LANES
    return jnp.where(iota((width, PHASES * LANES), 0) == source, 1.0, 0.0).astype(BF16)


def from_phases():
    src = iota((PHASES * LANES, PHASES * LANES), 0)
    target = (src % LANES) * PHASES + src // LANES
    return jnp.where(iota((PHASES * LANES, PHASES * LANES), 1) == target, 1.0, 0.0).astype(BF16)


def place(patch, n_cols):
    step_row = (patch >> (n_cols.bit_length() - 1)) - lax.axis_index("visit") + 1
    step_col = (patch & (n_cols - 1)) - lax.axis_index("det") + 1
    return step_row, step_col


def sums_kernel(n_cols, patch_ref, row_ref, set_ref, strips_hbm, even_ref, mid_ref, odd_ref, strips_ref, acc, sems):
    n_strips, strip_rows, _ = strips_ref.shape
    n_parts = 4
    some = n_strips // n_parts
    copies = []
    for i in range(n_parts):
        part = pl.ds(i * some, some)
        copies.append(pltpu.make_async_copy(strips_hbm.at[part], strips_ref.at[part], sems.at[i]))
        copies[i].start()
    acc[...] = jnp.zeros(acc.shape, F32)
    height = acc.shape[2] - ROWS
    place_lane = iota((ROWS, LANES), 1)
    place_sub = iota((ROWS, LANES), 0)

    def one_strip(t, carry):
        step_row, step_col = place(patch_ref[t], n_cols)
        top = row_ref[t]
        q = step_col * 3 + step_row
        for c in range(PHASES):
            acc[q, c, pl.ds(top, strip_rows), :] += strips_ref[t, :, c * LANES : (c + 1) * LANES]
        hit = (place_sub == set_ref[t]) & (place_lane >= top) & (place_lane < top + strip_rows)
        acc[q, 0, height:, :] += jnp.where(hit, 1.0, 0.0)
        return carry

    for i in range(n_parts):
        copies[i].wait()
        lax.fori_loop(i * some, (i + 1) * some, one_strip, 0, unroll=4)
    parity = lax.axis_index("det") % 2
    for first, out in ((6 - 6 * parity, even_ref), (3, mid_ref), (6 * parity, odd_ref)):
        out[...] = acc[pl.ds(first, 3)]


def taps_kernel(
    n_rows, n_cols, row_taps_ref, col_taps_ref, coef_ref, flat_ref, table_ref, table8_ref, top_ref, wide
):
    taps = row_taps_ref.shape[0]
    lane = iota((taps, DEPTH), 1)
    sub = iota((taps, DEPTH), 0)
    row_part = exact(row_taps_ref[...].T, jnp.where(lane % WIN == sub, 1.0, 0.0))
    col_part = exact(col_taps_ref[...].T, jnp.where(lane // WIN == sub, 1.0, 0.0))
    n_sets = table_ref.shape[0]
    one, u, v, uu, uv, vv = [coef_ref[p * n_sets : (p + 1) * n_sets, :] for p in range(6)]
    u0 = (2 * lax.axis_index("det") + 1).astype(F32) / n_cols - 1.0
    v0 = (2 * lax.axis_index("visit") + 1).astype(F32) / n_rows - 1.0
    one, u, v = (
        one + u0 * (u + u0 * uu) + v0 * (v + u0 * uv + v0 * vv),
        u + 2.0 * u0 * uu + v0 * uv,
        v + u0 * uv + 2.0 * v0 * vv,
    )
    flat = exact(jnp.concatenate([one, v, u, uu, uv, vv], axis=0), row_part * col_part)
    flat_ref[...] = flat
    top = jnp.maximum(jnp.max(jnp.max(jnp.abs(flat), axis=1, keepdims=True), axis=0, keepdims=True), 1e-30)
    top_ref[...] = jnp.broadcast_to(top, top_ref.shape)
    scale = TOP / top
    n = flat.shape[0]
    block = PHASES * ROWS
    for dy in range(ROWS):
        moved = flat if dy == 0 else pltpu.roll(flat, dy, 1)
        for c in range(TILES):
            wide[c, pl.ds(dy, n, stride=ROWS), :] = moved[:, c * LANES : (c + 1) * LANES]
    for s in range(n_sets):
        for p in range(6):
            rows = on_phases(wide, (p * n_sets + s) * ROWS)
            hi = rows.astype(BF16)
            table_ref[s, p * block : (p + 1) * block, :] = hi
            if p < FINE:
                table_ref[s, (6 + p) * block : (7 + p) * block, :] = (rows - hi.astype(F32)).astype(BF16)
                table8_ref[s, p * block : (p + 1) * block, :] = (rows * scale).astype(F8)


def on_phases(wide, first):
    rows = jnp.concatenate([wide[c, pl.ds(first, ROWS), :] for c in range(TILES)], axis=1)
    return jnp.concatenate([rows] + [pltpu.roll(rows, dx * WIN, 1) for dx in range(1, PHASES)], axis=0)


def columns_of(step_col, n_cols, width):
    shape = (PHASES * ROWS, LANES)
    col = (step_col - 1) * width - width // 2 + iota(shape, 1) * PHASES + iota(shape, 0) // ROWS
    return 2.0 * (col.astype(F32) + 0.5) / (n_cols * width)


def fill(image_ref, part, row, col, halves, kind, data):
    lane = iota((WIN, LANES), 1)
    for phase in range(PHASES):
        near, far = [image_ref[part, phase, col + i, pl.ds(row, WIN + (halves - 1) * ROWS), :] for i in range(2)]
        for half in range(halves):
            rows = slice(half * ROWS, half * ROWS + WIN)
            a, b = near[rows].astype(kind), far[rows].astype(kind)
            for shift in range((SIDE - HALF + SHIFTS - 1) // PHASES + 1):
                k = shift * PHASES + phase - (SIDE - HALF)
                if 0 <= k < SHIFTS:
                    moved = a if shift == 0 else pltpu.roll(jnp.where(lane < shift, b, a), LANES - shift, 1)
                    data[k * WIN : (k + 1) * WIN, half * LANES : (half + 1) * LANES] = moved


def model_loop(
    n_rows, n_cols, height, patch_ref, row_ref, set_ref, top_ref, table8_ref, table_ref, image, buffers, first, last, store
):
    width = PHASES * LANES
    block = PHASES * ROWS
    fine = FINE * block
    shape = (block, 2 * LANES)
    row_in = iota(shape, 0) % ROWS + iota(shape, 1) // LANES * ROWS
    undo = top_ref[0:1, 0:1] * (1.0 / (TOP * SCALE))

    def build(t, data_hi, data_lo):
        step_row, step_col = place(patch_ref[t], n_cols)
        row = step_row * height + row_ref[t] + EDGE - HALF
        fill(image, 0, row, step_col, 2, BF16, data_hi)
        fill(image, 1, row, step_col, 2, F8, data_lo)

    def multiply(t, data_hi, data_lo):
        step_row, step_col = place(patch_ref[t], n_cols)
        which = set_ref[t]
        big = mxu(table_ref[which], data_hi[...])
        small = mxu(table8_ref[which], data_lo[...])
        exact_terms = big[:fine] + big[6 * block :] + small * undo
        term_1, term_v, term_u = [exact_terms[p * block : (p + 1) * block] for p in range(FINE)]
        term_uu, term_uv, term_vv = [big[p * block : (p + 1) * block] for p in range(FINE, 6)]
        one_u = columns_of(step_col, n_cols, width)
        u = jnp.concatenate([one_u, one_u], axis=1)
        y = (step_row - 1) * height - height // 2 + row_ref[t] + row_in
        v = 2.0 * (y.astype(F32) + 0.5) / (n_rows * height)
        store(t, term_1 + u * (term_u + u * term_uu + v * term_uv) + v * (term_v + v * term_vv))

    build(first, *buffers[0])
    some = 4

    def some_strips(i, carry):
        for j in range(some):
            t = first + some * i + j
            build(jnp.minimum(t + 1, last - 1), *buffers[(j + 1) % 2])
            multiply(t, *buffers[j % 2])
        return carry

    lax.fori_loop(0, (last - first) // some, some_strips, 0)


def store_model(models, first, strip_rows, t, model):
    for half in range(2):
        rows_of = pl.ds(pl.multiple_of((t - first) * strip_rows + half * ROWS, ROWS), ROWS)
        for dx in range(PHASES):
            models[rows_of, dx * LANES : (dx + 1) * LANES] = model[
                dx * ROWS : (dx + 1) * ROWS, half * LANES : (half + 1) * LANES
            ]


def strips_kernel(
    n_rows, n_cols, patch_ref, row_ref, set_ref, top_ref, near_rows, away_rows, here_ref, even_ref, odd_ref,
    table8_ref, table_ref, image, models, hi_a, lo_a, hi_b, lo_b,
):
    height = here_ref.shape[0]
    width = PHASES * LANES
    scatter = to_phases(width)
    rows = image.shape[3]
    upper = lax.axis_index("visit") % 2 == 0
    ahead = lax.axis_index("visit") % 4 < 2
    for b in range(4):
        cols = slice(b * width, min((b + 1) * width, here_ref.shape[1]))
        near, away, even, odd = [r[:, cols] for r in (near_rows, away_rows, even_ref, odd_ref)]
        pieces = (
            jnp.where(ahead, away, near),
            jnp.where(upper, odd, even),
            here_ref[:, cols],
            jnp.where(upper, even, odd),
            jnp.where(ahead, near, away),
        )
        parts = [split(piece) for piece in pieces]
        both = jnp.concatenate([hi for hi, _ in parts] + [lo for _, lo in parts], axis=0)
        moved = mxu(both, scatter[: cols.stop - cols.start])
        for f in range(PHASES):
            for part in range(2):
                some = moved[part * rows : (part + 1) * rows, f * LANES : (f + 1) * LANES]
                image[part, f, b] = some * SCALE if part else some

    strip_rows = models.shape[0] // (patch_ref.shape[0] - LATER)
    model_loop(
        n_rows, n_cols, height, patch_ref, row_ref, set_ref, top_ref, table8_ref, table_ref, image,
        ((hi_a, lo_a), (hi_b, lo_b)), 0, patch_ref.shape[0] - LATER,
        functools.partial(store_model, models, 0, strip_rows),
    )


def finish_kernel(
    n_rows, n_cols, height, patch_ref, row_ref, set_ref, top_ref, table8_ref, table_ref, image, models, strips_hbm, diff_hbm,
    strips_ref, rest, hi_a, lo_a, hi_b, lo_b, sems,
):
    n_strips, strip_rows, width = strips_ref.shape
    copy_strips = pltpu.make_async_copy(strips_hbm, strips_ref, sems.at[4])
    copy_strips.start()
    model_loop(
        n_rows, n_cols, height, patch_ref, row_ref, set_ref, top_ref, table8_ref, table_ref, image,
        ((hi_a, lo_a), (hi_b, lo_b)), n_strips - LATER, n_strips,
        functools.partial(store_model, rest, n_strips - LATER, strip_rows),
    )
    gather = from_phases()
    gather = jnp.concatenate([gather, gather], axis=0)
    copy_strips.wait()
    some = 16
    ready = models.shape[0]
    for c in range(n_strips // some):
        rows = slice(c * some * strip_rows, (c + 1) * some * strip_rows)
        found = models[rows] if rows.stop <= ready else jnp.concatenate([models[rows.start : ready], rest[...]], axis=0)
        natural = mxu(jnp.concatenate(split(found), axis=1), gather)
        part = pl.ds(c * some, some)
        strips_ref[part] = strips_ref[part] - natural.reshape(some, strip_rows, width)
        pltpu.make_async_copy(strips_ref.at[part], diff_hbm.at[part], sems.at[c]).start()
    for c in range(n_strips // some):
        part = pl.ds(c * some, some)
        pltpu.make_async_copy(strips_ref.at[part], diff_hbm.at[part], sems.at[c]).wait()


def coadd_kernel(
    n_rows, n_cols, flat_ref, image, mid_any, even_any, odd_any, coadd_ref,
    mid_ref, even_ref, odd_ref, taps, wide, models, hi_a, lo_a, hi_b, lo_b, sems,
):
    height, width = coadd_ref.shape
    sources = (mid_any, even_any, odd_any)
    targets = (mid_ref, even_ref, odd_ref)
    copies = [pltpu.make_async_copy(source, target, sems.at[i]) for i, (source, target) in enumerate(zip(sources, targets))]
    for copy in copies:
        copy.start()
    for copy in copies:
        copy.wait()
    count = mid_ref[0, height:, :] + even_ref[0, height:, :] + odd_ref[0, height:, :]
    n_sets = count.shape[0]
    v = 2.0 * ((iota(count.shape, 1) - height // 2).astype(F32) + 0.5) / (n_rows * height)

    def three(x, p):
        taps_of = flat_ref[p * n_sets : (p + 1) * n_sets, :]
        x_hi, t_hi = x.astype(BF16).astype(F32), taps_of.astype(BF16).astype(F32)
        return [(x_hi, t_hi), (x - x_hi, t_hi), (x_hi, taps_of - t_hi)]

    by_power = []
    for terms in ((0, 1, 5), (2, 4), (3,)):
        rows, x = [], count
        for p in terms:
            rows, x = rows + three(x, p), x * v
        sides = [jnp.concatenate(side, axis=0) for side in zip(*rows)]
        by_power.append(mxu(sides[0].T.astype(BF16), sides[1].astype(BF16)))
    for a in range(3):
        for c in range(TILES):
            taps[c, a * height : (a + 1) * height, :] = by_power[a][:, c * LANES : (c + 1) * LANES]
    n = 3 * height // ROWS
    for dy in range(ROWS):
        some = jnp.concatenate([taps[c, pl.ds(dy, n, stride=ROWS), :] for c in range(TILES)], axis=1)
        moved = some if dy == 0 else pltpu.roll(some, dy, 1)
        for c in range(TILES):
            wide[c, pl.ds(dy, n, stride=ROWS), :] = moved[:, c * LANES : (c + 1) * LANES]
    one_u = columns_of(1, n_cols, width)

    def build(b, data_hi, data_lo):
        fill(image, 0, height + b * ROWS + EDGE - HALF, 1, 1, BF16, data_hi)
        fill(image, 1, height + b * ROWS + EDGE - HALF, 1, 1, BF16, data_lo)

    def multiply(b, data_hi, data_lo):
        row = pl.multiple_of(b * ROWS, ROWS)
        fine_hi, fine_lo = split(on_phases(wide, row))
        rest = [on_phases(wide, a * height + row).astype(BF16) for a in (1, 2)]
        big = mxu(jnp.concatenate([fine_hi] + rest + [fine_lo], axis=0), data_hi[...])
        terms = big.reshape(4, PHASES * ROWS, LANES)
        small = mxu(fine_hi, data_lo[...]) * (1.0 / SCALE)
        model = terms[0] + terms[3] + small + one_u * (terms[1] + one_u * terms[2])
        for dx in range(PHASES):
            models[pl.ds(row, ROWS), dx * LANES : (dx + 1) * LANES] = model[dx * ROWS : (dx + 1) * ROWS]

    n_blocks = height // ROWS
    build(0, hi_a, lo_a)
    some = 8
    buffers = ((hi_a, lo_a), (hi_b, lo_b))

    def some_blocks(i, carry):
        for j in range(some):
            b = some * i + j
            build(jnp.minimum(b + 1, n_blocks - 1), *buffers[(j + 1) % 2])
            multiply(b, *buffers[j % 2])
        return carry

    lax.fori_loop(0, n_blocks // some, some_blocks, 0)
    gather = from_phases()
    gather = jnp.concatenate([gather, gather], axis=0)
    natural = mxu(jnp.concatenate(split(models[...]), axis=1), gather)
    for c in range(PHASES):
        total = mid_ref[c, 0:height, :] + even_ref[c, 0:height, :] + odd_ref[c, 0:height, :]
        coadd_ref[:, c * LANES : (c + 1) * LANES] = total - natural[:, c * LANES : (c + 1) * LANES]


def swap(x, axis, apart, first):
    size = lax.axis_size(axis)
    lower = [i for i in range(size - apart) if (i - first) % (2 * apart) < apart]
    pairs = [(i, i + apart) for i in lower] + [(i + apart, i) for i in lower]
    return lax.ppermute(x, axis, pairs)


def per_device(strips, patch_of, box_row, kernel_set, template, row_taps, col_taps, kernel_coef):
    n_rows, n_cols = lax.axis_size("visit"), lax.axis_size("det")
    n_strips, strip_rows, width = strips.shape
    height = template.shape[0]
    n_sets, n_terms, n_basis = kernel_coef.shape
    block = PHASES * ROWS
    smem = pl.BlockSpec(memory_space=pltpu.SMEM)
    vmem = pl.BlockSpec(memory_space=pltpu.VMEM)
    hbm = pl.BlockSpec(memory_space=pltpu.HBM)
    free = pl.BlockSpec(memory_space=pl.ANY)

    patch_of = patch_of.reshape(n_strips)

    v, d = lax.axis_index("visit"), lax.axis_index("det")
    first, last = template[:, :SIDE], template[:, width - SIDE :]
    ahead = d % 4 < 2
    near = swap(jnp.where(ahead, last, first), "det", 2, 0)
    away = swap(jnp.where(ahead, first, last), "det", 2, 2)
    even = swap(template, "det", 1, 0)
    odd = swap(template, "det", 1, 1)

    sums = jax.ShapeDtypeStruct((3, PHASES, height + ROWS, LANES), F32)
    far_left, far_right = jnp.where(ahead, away, near), jnp.where(ahead, near, away)
    left, right = jnp.where(d % 2 == 0, odd, even), jnp.where(d % 2 == 0, even, odd)
    blank = jnp.zeros((height, LANES - 2 * SIDE), F32)
    here = jnp.concatenate([far_left, left, template, right, far_right, blank], axis=1)

    patch_of, row_taps, here = lax.optimization_barrier((patch_of, row_taps, here))
    odd = swap(here, "visit", 1, 1)
    even = swap(here, "visit", 1, 0)
    first, last = here[:EDGE], here[height - EDGE :]
    ahead = v % 4 < 2
    near_rows = swap(jnp.where(ahead, last, first), "visit", 2, 0)
    away_rows = swap(jnp.where(ahead, first, last), "visit", 2, 2)

    for_even, mid, for_odd = pl.pallas_call(
        functools.partial(sums_kernel, n_cols),
        out_shape=(sums, sums, sums),
        in_specs=[smem] * 3 + [hbm],
        out_specs=(vmem,) * 3,
        scratch_shapes=[
            pltpu.VMEM(strips.shape, F32),
            pltpu.VMEM((9, PHASES, height + ROWS, LANES), F32),
            pltpu.SemaphoreType.DMA((4,)),
        ],
        compiler_params=pltpu.CompilerParams(vmem_limit_bytes=56 * MIB),
        cost_estimate=pl.CostEstimate(flops=3 << 30, bytes_accessed=5 << 20, transcendentals=0),
        name="strip_sums",
    )(patch_of, box_row, kernel_set, strips)

    for_odd, even = lax.optimization_barrier((for_odd, even))
    sum_even = swap(for_even, "det", 1, 0)
    sum_odd = swap(for_odd, "det", 1, 1)

    flat, table, table8, top = pl.pallas_call(
        functools.partial(taps_kernel, n_rows, n_cols),
        out_shape=(
            pltpu.VMEM((n_sets * n_terms, DEPTH), F32),
            pltpu.VMEM((n_sets, (n_terms + FINE) * block, DEPTH), BF16),
            pltpu.VMEM((n_sets, FINE * block, DEPTH), F8),
            pltpu.VMEM((ROWS, LANES), F32),
        ),
        in_specs=[vmem] * 3,
        out_specs=(vmem,) * 4,
        scratch_shapes=[pltpu.VMEM((TILES, n_sets * n_terms * ROWS, LANES), F32)],
        compiler_params=pltpu.CompilerParams(vmem_limit_bytes=56 * MIB),
        cost_estimate=pl.CostEstimate(flops=3 << 30, bytes_accessed=5 << 20, transcendentals=0),
        name="tap_tables",
    )(row_taps.T, col_taps.T, jnp.swapaxes(kernel_coef, 0, 1).reshape(n_terms * n_sets, n_basis))

    flat, table, table8, top = [
        pltpu.with_memory_space_constraint(x, pltpu.VMEM) for x in (flat, table, table8, top)
    ]

    even, odd, near_rows, away_rows, here = [
        pltpu.with_memory_space_constraint(x, pltpu.VMEM) for x in (even, odd, near_rows, away_rows, here)
    ]

    flops = n_strips * 2 * n_terms * block * DEPTH * 2 * LANES * 2
    buffers = [pltpu.VMEM((DEPTH, 2 * LANES), kind) for kind in (BF16, F8, BF16, F8)]
    image, models = pl.pallas_call(
        functools.partial(strips_kernel, n_rows, n_cols),
        out_shape=(
            pltpu.VMEM((2, PHASES, 4, 3 * height + 2 * EDGE, LANES), F32),
            pltpu.VMEM(((n_strips - LATER) * strip_rows, width), F32),
        ),
        in_specs=[smem] * 3 + [vmem] * 8,
        out_specs=(vmem, vmem),
        scratch_shapes=buffers,
        compiler_params=pltpu.CompilerParams(vmem_limit_bytes=32 * MIB),
        cost_estimate=pl.CostEstimate(flops=flops, bytes_accessed=14 << 20, transcendentals=0),
        name="strip_models",
    )(patch_of, box_row, kernel_set, top, near_rows, away_rows, here, even, odd, table8, table)

    image, models, sum_even, sum_odd = lax.optimization_barrier((image, models, sum_even, sum_odd))
    mid = mid + sum_even + sum_odd
    image, models = [pltpu.with_memory_space_constraint(x, pltpu.VMEM) for x in (image, models)]
    from_even = swap(jnp.where(v % 2 == 0, mid[2], mid[0]), "visit", 1, 0)
    from_odd = swap(jnp.where(v % 2 == 0, mid[0], mid[2]), "visit", 1, 1)

    patch_of, mid = lax.optimization_barrier((patch_of, mid))
    difference = pl.pallas_call(
        functools.partial(finish_kernel, n_rows, n_cols, height),
        out_shape=jax.ShapeDtypeStruct(strips.shape, F32),
        in_specs=[smem] * 3 + [vmem] * 5 + [hbm],
        out_specs=hbm,
        scratch_shapes=[pltpu.VMEM(strips.shape, F32), pltpu.VMEM((LATER * strip_rows, width), F32)]
        + buffers
        + [pltpu.SemaphoreType.DMA((5,))],
        compiler_params=pltpu.CompilerParams(vmem_limit_bytes=32 * MIB),
        cost_estimate=pl.CostEstimate(flops=flops // 4, bytes_accessed=4 << 20, transcendentals=0),
        name="finish",
    )(patch_of, box_row, kernel_set, top, table8, table, image, models, strips)

    coadd = pl.pallas_call(
        functools.partial(coadd_kernel, n_rows, n_cols),
        out_shape=jax.ShapeDtypeStruct(template.shape, F32),
        in_specs=[vmem, vmem] + [free] * 3,
        out_specs=vmem,
        scratch_shapes=[pltpu.VMEM(x.shape, F32) for x in (from_even, from_even, from_odd)]
        + [
            pltpu.VMEM((TILES, 3 * height, LANES), F32),
            pltpu.VMEM((TILES, 3 * height, LANES), F32),
            pltpu.VMEM((height, PHASES * LANES), F32),
        ]
        + [pltpu.VMEM((DEPTH, LANES), BF16)] * 4
        + [pltpu.SemaphoreType.DMA((3,))],
        compiler_params=pltpu.CompilerParams(vmem_limit_bytes=32 * MIB),
        cost_estimate=pl.CostEstimate(flops=6 << 30, bytes_accessed=3 << 20, transcendentals=0),
        name="coadd_models",
    )(flat, image, mid[1], from_even, from_odd)
    return difference, coadd


def solution(mesh):
    tiles = ("visit", "det")
    in_specs = (P(tiles, None, None), P(tiles, None), P(tiles), P(tiles), P("visit", "det"), P(), P(), P())
    out_specs = (P(tiles, None, None), P("visit", "det"))
    return jax.shard_map(per_device, mesh=mesh, in_specs=in_specs, out_specs=out_specs, check_vma=False)
```

```python
import functools

import jax
import jax.numpy as jnp
from jax import lax
from jax.experimental import pallas as pl
from jax.experimental.pallas import tpu as pltpu
from jax.sharding import PartitionSpec as P

F32 = jnp.float32
BF16 = jnp.bfloat16
F8 = jnp.float8_e4m3fn
HIGHEST = lax.Precision.HIGHEST

HALF = 10
SIDE = 12
EDGE = 16
PHASES = 4
LANES = 128
ROWS = 8
WIN = 32
SHIFTS = 24
DEPTH = SHIFTS * WIN
TILES = DEPTH // LANES
LATER = 8
FINE = 3
SCALE = 2.0**14
TOP = 256.0
MIB = 1024 * 1024


def iota(shape, dim):
    return lax.broadcasted_iota(jnp.int32, shape, dim)


def split(x):
    hi = x.astype(BF16)
    lo = (x - hi.astype(F32)).astype(BF16)
    return hi, lo


def mxu(a, b):
    return jnp.dot(a, b, preferred_element_type=F32)


def exact(a, b):
    return jnp.dot(a, b, precision=HIGHEST, preferred_element_type=F32)


def to_phases(width):
    out = iota((width, PHASES * LANES), 1)
    source = (out % LANES) * PHASES + out // LANES
    return jnp.where(iota((width, PHASES * LANES), 0) == source, 1.0, 0.0).astype(BF16)


def from_phases():
    src = iota((PHASES * LANES, PHASES * LANES), 0)
    target = (src % LANES) * PHASES + src // LANES
    return jnp.where(iota((PHASES * LANES, PHASES * LANES), 1) == target, 1.0, 0.0).astype(BF16)


def place(patch, n_cols):
    step_row = (patch >> (n_cols.bit_length() - 1)) - lax.axis_index("visit") + 1
    step_col = (patch & (n_cols - 1)) - lax.axis_index("det") + 1
    return step_row, step_col


def sums_kernel(n_cols, patch_ref, row_ref, set_ref, strips_hbm, even_ref, mid_ref, odd_ref, strips_ref, acc, sems):
    n_strips, strip_rows, _ = strips_ref.shape
    n_parts = 4
    some = n_strips // n_parts
    copies = []
    for i in range(n_parts):
        part = pl.ds(i * some, some)
        copies.append(pltpu.make_async_copy(strips_hbm.at[part], strips_ref.at[part], sems.at[i]))
        copies[i].start()
    acc[...] = jnp.zeros(acc.shape, F32)
    height = acc.shape[2] - ROWS
    place_lane = iota((ROWS, LANES), 1)
    place_sub = iota((ROWS, LANES), 0)

    def one_strip(t, carry):
        step_row, step_col = place(patch_ref[t], n_cols)
        top = row_ref[t]
        q = step_col * 3 + step_row
        for c in range(PHASES):
            acc[q, c, pl.ds(top, strip_rows), :] += strips_ref[t, :, c * LANES : (c + 1) * LANES]
        hit = (place_sub == set_ref[t]) & (place_lane >= top) & (place_lane < top + strip_rows)
        acc[q, 0, height:, :] += jnp.where(hit, 1.0, 0.0)
        return carry

    for i in range(n_parts):
        copies[i].wait()
        lax.fori_loop(i * some, (i + 1) * some, one_strip, 0, unroll=4)
    parity = lax.axis_index("det") % 2
    for first, out in ((6 - 6 * parity, even_ref), (3, mid_ref), (6 * parity, odd_ref)):
        out[...] = acc[pl.ds(first, 3)]


def taps_kernel(
    n_rows, n_cols, row_taps_ref, col_taps_ref, coef_ref, flat_ref, table_ref, table8_ref, top_ref, wide
):
    taps = row_taps_ref.shape[0]
    lane = iota((taps, DEPTH), 1)
    sub = iota((taps, DEPTH), 0)
    row_part = exact(row_taps_ref[...].T, jnp.where(lane % WIN == sub, 1.0, 0.0))
    col_part = exact(col_taps_ref[...].T, jnp.where(lane // WIN == sub, 1.0, 0.0))
    n_sets = table_ref.shape[0]
    one, u, v, uu, uv, vv = [coef_ref[p * n_sets : (p + 1) * n_sets, :] for p in range(6)]
    u0 = (2 * lax.axis_index("det") + 1).astype(F32) / n_cols - 1.0
    v0 = (2 * lax.axis_index("visit") + 1).astype(F32) / n_rows - 1.0
    one, u, v = (
        one + u0 * (u + u0 * uu) + v0 * (v + u0 * uv + v0 * vv),
        u + 2.0 * u0 * uu + v0 * uv,
        v + u0 * uv + 2.0 * v0 * vv,
    )
    flat = exact(jnp.concatenate([one, v, u, uu, uv, vv], axis=0), row_part * col_part)
    flat_ref[...] = flat
    top = jnp.maximum(jnp.max(jnp.max(jnp.abs(flat), axis=1, keepdims=True), axis=0, keepdims=True), 1e-30)
    top_ref[...] = jnp.broadcast_to(top, top_ref.shape)
    scale = TOP / top
    n = flat.shape[0]
    block = PHASES * ROWS
    for dy in range(ROWS):
        moved = flat if dy == 0 else pltpu.roll(flat, dy, 1)
        for c in range(TILES):
            wide[c, pl.ds(dy, n, stride=ROWS), :] = moved[:, c * LANES : (c + 1) * LANES]
    for s in range(n_sets):
        for p in range(6):
            rows = on_phases(wide, (p * n_sets + s) * ROWS)
            hi = rows.astype(BF16)
            table_ref[s, p * block : (p + 1) * block, :] = hi
            if p < FINE:
                table_ref[s, (6 + p) * block : (7 + p) * block, :] = (rows - hi.astype(F32)).astype(BF16)
                table8_ref[s, p * block : (p + 1) * block, :] = (rows * scale).astype(F8)


def on_phases(wide, first):
    rows = jnp.concatenate([wide[c, pl.ds(first, ROWS), :] for c in range(TILES)], axis=1)
    return jnp.concatenate([rows] + [pltpu.roll(rows, dx * WIN, 1) for dx in range(1, PHASES)], axis=0)


def columns_of(step_col, n_cols, width):
    shape = (PHASES * ROWS, LANES)
    col = (step_col - 1) * width - width // 2 + iota(shape, 1) * PHASES + iota(shape, 0) // ROWS
    return 2.0 * (col.astype(F32) + 0.5) / (n_cols * width)


def fill(image_ref, part, row, col, halves, kind, data):
    lane = iota((WIN, LANES), 1)
    for phase in range(PHASES):
        near, far = [image_ref[part, phase, col + i, pl.ds(row, WIN + (halves - 1) * ROWS), :] for i in range(2)]
        for half in range(halves):
            rows = slice(half * ROWS, half * ROWS + WIN)
            a, b = near[rows].astype(kind), far[rows].astype(kind)
            for shift in range((SIDE - HALF + SHIFTS - 1) // PHASES + 1):
                k = shift * PHASES + phase - (SIDE - HALF)
                if 0 <= k < SHIFTS:
                    moved = a if shift == 0 else pltpu.roll(jnp.where(lane < shift, b, a), LANES - shift, 1)
                    data[k * WIN : (k + 1) * WIN, half * LANES : (half + 1) * LANES] = moved


def model_loop(
    n_rows, n_cols, height, patch_ref, row_ref, set_ref, top_ref, table8_ref, table_ref, image, buffers, first, last, store
):
    width = PHASES * LANES
    block = PHASES * ROWS
    fine = FINE * block
    shape = (block, 2 * LANES)
    row_in = iota(shape, 0) % ROWS + iota(shape, 1) // LANES * ROWS
    undo = top_ref[0:1, 0:1] * (1.0 / (TOP * SCALE))

    def build(t, data_hi, data_lo):
        step_row, step_col = place(patch_ref[t], n_cols)
        row = step_row * height + row_ref[t] + EDGE - HALF
        fill(image, 0, row, step_col, 2, BF16, data_hi)
        fill(image, 1, row, step_col, 2, F8, data_lo)

    def multiply(t, data_hi, data_lo):
        step_row, step_col = place(patch_ref[t], n_cols)
        which = set_ref[t]
        big = mxu(table_ref[which], data_hi[...])
        small = mxu(table8_ref[which], data_lo[...])
        exact_terms = big[:fine] + big[6 * block :] + small * undo
        term_1, term_v, term_u = [exact_terms[p * block : (p + 1) * block] for p in range(FINE)]
        term_uu, term_uv, term_vv = [big[p * block : (p + 1) * block] for p in range(FINE, 6)]
        one_u = columns_of(step_col, n_cols, width)
        u = jnp.concatenate([one_u, one_u], axis=1)
        y = (step_row - 1) * height - height // 2 + row_ref[t] + row_in
        v = 2.0 * (y.astype(F32) + 0.5) / (n_rows * height)
        store(t, term_1 + u * (term_u + u * term_uu + v * term_uv) + v * (term_v + v * term_vv))

    build(first, *buffers[0])
    some = 4

    def some_strips(i, carry):
        for j in range(some):
            t = first + some * i + j
            build(jnp.minimum(t + 1, last - 1), *buffers[(j + 1) % 2])
            multiply(t, *buffers[j % 2])
        return carry

    lax.fori_loop(0, (last - first) // some, some_strips, 0)


def store_model(models, first, strip_rows, t, model):
    for half in range(2):
        rows_of = pl.ds(pl.multiple_of((t - first) * strip_rows + half * ROWS, ROWS), ROWS)
        for dx in range(PHASES):
            models[rows_of, dx * LANES : (dx + 1) * LANES] = model[
                dx * ROWS : (dx + 1) * ROWS, half * LANES : (half + 1) * LANES
            ]


def strips_kernel(
    n_rows, n_cols, patch_ref, row_ref, set_ref, top_ref, near_rows, away_rows, here_ref, even_ref, odd_ref,
    table8_ref, table_ref, image, models, hi_a, lo_a, hi_b, lo_b,
):
    height = here_ref.shape[0]
    width = PHASES * LANES
    scatter = to_phases(width)
    rows = image.shape[3]
    upper = lax.axis_index("visit") % 2 == 0
    ahead = lax.axis_index("visit") % 4 < 2
    for b in range(4):
        cols = slice(b * width, min((b + 1) * width, here_ref.shape[1]))
        near, away, even, odd = [r[:, cols] for r in (near_rows, away_rows, even_ref, odd_ref)]
        pieces = (
            jnp.where(ahead, away, near),
            jnp.where(upper, odd, even),
            here_ref[:, cols],
            jnp.where(upper, even, odd),
            jnp.where(ahead, near, away),
        )
        parts = [split(piece) for piece in pieces]
        both = jnp.concatenate([hi for hi, _ in parts] + [lo for _, lo in parts], axis=0)
        moved = mxu(both, scatter[: cols.stop - cols.start])
        for f in range(PHASES):
            for part in range(2):
                some = moved[part * rows : (part + 1) * rows, f * LANES : (f + 1) * LANES]
                image[part, f, b] = some * SCALE if part else some

    strip_rows = models.shape[0] // (patch_ref.shape[0] - LATER)
    model_loop(
        n_rows, n_cols, height, patch_ref, row_ref, set_ref, top_ref, table8_ref, table_ref, image,
        ((hi_a, lo_a), (hi_b, lo_b)), 0, patch_ref.shape[0] - LATER,
        functools.partial(store_model, models, 0, strip_rows),
    )


def finish_kernel(
    n_rows, n_cols, height, patch_ref, row_ref, set_ref, top_ref, table8_ref, table_ref, image, models, strips_hbm, diff_hbm,
    strips_ref, rest, hi_a, lo_a, hi_b, lo_b, sems,
):
    n_strips, strip_rows, width = strips_ref.shape
    copy_strips = pltpu.make_async_copy(strips_hbm, strips_ref, sems.at[4])
    copy_strips.start()
    model_loop(
        n_rows, n_cols, height, patch_ref, row_ref, set_ref, top_ref, table8_ref, table_ref, image,
        ((hi_a, lo_a), (hi_b, lo_b)), n_strips - LATER, n_strips,
        functools.partial(store_model, rest, n_strips - LATER, strip_rows),
    )
    gather = from_phases()
    gather = jnp.concatenate([gather, gather], axis=0)
    copy_strips.wait()
    some = 16
    ready = models.shape[0]
    for c in range(n_strips // some):
        rows = slice(c * some * strip_rows, (c + 1) * some * strip_rows)
        found = models[rows] if rows.stop <= ready else jnp.concatenate([models[rows.start : ready], rest[...]], axis=0)
        natural = mxu(jnp.concatenate(split(found), axis=1), gather)
        part = pl.ds(c * some, some)
        strips_ref[part] = strips_ref[part] - natural.reshape(some, strip_rows, width)
        pltpu.make_async_copy(strips_ref.at[part], diff_hbm.at[part], sems.at[c]).start()
    for c in range(n_strips // some):
        part = pl.ds(c * some, some)
        pltpu.make_async_copy(strips_ref.at[part], diff_hbm.at[part], sems.at[c]).wait()


def coadd_kernel(
    n_rows, n_cols, flat_ref, image, mid_any, even_any, odd_any, coadd_ref,
    mid_ref, even_ref, odd_ref, taps, wide, models, hi_a, lo_a, hi_b, lo_b, sems,
):
    height, width = coadd_ref.shape
    sources = (mid_any, even_any, odd_any)
    targets = (mid_ref, even_ref, odd_ref)
    copies = [pltpu.make_async_copy(source, target, sems.at[i]) for i, (source, target) in enumerate(zip(sources, targets))]
    for copy in copies:
        copy.start()
    for copy in copies:
        copy.wait()
    count = mid_ref[0, height:, :] + even_ref[0, height:, :] + odd_ref[0, height:, :]
    n_sets = count.shape[0]
    v = 2.0 * ((iota(count.shape, 1) - height // 2).astype(F32) + 0.5) / (n_rows * height)

    def three(x, p):
        taps_of = flat_ref[p * n_sets : (p + 1) * n_sets, :]
        x_hi, t_hi = x.astype(BF16).astype(F32), taps_of.astype(BF16).astype(F32)
        return [(x_hi, t_hi), (x - x_hi, t_hi), (x_hi, taps_of - t_hi)]

    by_power = []
    for terms in ((0, 1, 5), (2, 4), (3,)):
        rows, x = [], count
        for p in terms:
            rows, x = rows + three(x, p), x * v
        sides = [jnp.concatenate(side, axis=0) for side in zip(*rows)]
        by_power.append(mxu(sides[0].T.astype(BF16), sides[1].astype(BF16)))
    for a in range(3):
        for c in range(TILES):
            taps[c, a * height : (a + 1) * height, :] = by_power[a][:, c * LANES : (c + 1) * LANES]
    n = 3 * height // ROWS
    for dy in range(ROWS):
        some = jnp.concatenate([taps[c, pl.ds(dy, n, stride=ROWS), :] for c in range(TILES)], axis=1)
        moved = some if dy == 0 else pltpu.roll(some, dy, 1)
        for c in range(TILES):
            wide[c, pl.ds(dy, n, stride=ROWS), :] = moved[:, c * LANES : (c + 1) * LANES]
    one_u = columns_of(1, n_cols, width)

    def build(b, data_hi, data_lo):
        fill(image, 0, height + b * ROWS + EDGE - HALF, 1, 1, BF16, data_hi)
        fill(image, 1, height + b * ROWS + EDGE - HALF, 1, 1, BF16, data_lo)

    def multiply(b, data_hi, data_lo):
        row = pl.multiple_of(b * ROWS, ROWS)
        fine_hi, fine_lo = split(on_phases(wide, row))
        rest = [on_phases(wide, a * height + row).astype(BF16) for a in (1, 2)]
        big = mxu(jnp.concatenate([fine_hi] + rest + [fine_lo], axis=0), data_hi[...])
        terms = big.reshape(4, PHASES * ROWS, LANES)
        small = mxu(fine_hi, data_lo[...]) * (1.0 / SCALE)
        model = terms[0] + terms[3] + small + one_u * (terms[1] + one_u * terms[2])
        for dx in range(PHASES):
            models[pl.ds(row, ROWS), dx * LANES : (dx + 1) * LANES] = model[dx * ROWS : (dx + 1) * ROWS]

    n_blocks = height // ROWS
    build(0, hi_a, lo_a)
    some = 8
    buffers = ((hi_a, lo_a), (hi_b, lo_b))

    def some_blocks(i, carry):
        for j in range(some):
            b = some * i + j
            build(jnp.minimum(b + 1, n_blocks - 1), *buffers[(j + 1) % 2])
            multiply(b, *buffers[j % 2])
        return carry

    lax.fori_loop(0, n_blocks // some, some_blocks, 0)
    gather = from_phases()
    gather = jnp.concatenate([gather, gather], axis=0)
    natural = mxu(jnp.concatenate(split(models[...]), axis=1), gather)
    for c in range(PHASES):
        total = mid_ref[c, 0:height, :] + even_ref[c, 0:height, :] + odd_ref[c, 0:height, :]
        coadd_ref[:, c * LANES : (c + 1) * LANES] = total - natural[:, c * LANES : (c + 1) * LANES]


def swap(x, axis, apart, first):
    size = lax.axis_size(axis)
    lower = [i for i in range(size - apart) if (i - first) % (2 * apart) < apart]
    pairs = [(i, i + apart) for i in lower] + [(i + apart, i) for i in lower]
    return lax.ppermute(x, axis, pairs)


def per_device(strips, patch_of, box_row, kernel_set, template, row_taps, col_taps, kernel_coef):
    n_rows, n_cols = lax.axis_size("visit"), lax.axis_size("det")
    n_strips, strip_rows, width = strips.shape
    height = template.shape[0]
    n_sets, n_terms, n_basis = kernel_coef.shape
    block = PHASES * ROWS
    smem = pl.BlockSpec(memory_space=pltpu.SMEM)
    vmem = pl.BlockSpec(memory_space=pltpu.VMEM)
    hbm = pl.BlockSpec(memory_space=pltpu.HBM)
    free = pl.BlockSpec(memory_space=pl.ANY)

    patch_of = patch_of.reshape(n_strips)

    v, d = lax.axis_index("visit"), lax.axis_index("det")
    first, last = template[:, :SIDE], template[:, width - SIDE :]
    ahead = d % 4 < 2
    even = swap(template, "det", 1, 0)
    odd = swap(template, "det", 1, 1)
    for_near, for_away = jnp.where(ahead, last, first), jnp.where(ahead, first, last)
    patch_of, for_near, for_away = lax.optimization_barrier((patch_of, for_near, for_away))
    near = swap(for_near, "det", 2, 0)
    away = swap(for_away, "det", 2, 2)

    sums = jax.ShapeDtypeStruct((3, PHASES, height + ROWS, LANES), F32)
    for_even, mid, for_odd = pl.pallas_call(
        functools.partial(sums_kernel, n_cols),
        out_shape=(sums, sums, sums),
        in_specs=[smem] * 3 + [hbm],
        out_specs=(vmem,) * 3,
        scratch_shapes=[
            pltpu.VMEM(strips.shape, F32),
            pltpu.VMEM((9, PHASES, height + ROWS, LANES), F32),
            pltpu.SemaphoreType.DMA((4,)),
        ],
        compiler_params=pltpu.CompilerParams(vmem_limit_bytes=56 * MIB),
        cost_estimate=pl.CostEstimate(flops=3 << 30, bytes_accessed=5 << 20, transcendentals=0),
        name="strip_sums",
    )(patch_of, box_row, kernel_set, strips)

    far_left, far_right = jnp.where(ahead, away, near), jnp.where(ahead, near, away)
    left, right = jnp.where(d % 2 == 0, odd, even), jnp.where(d % 2 == 0, even, odd)
    blank = jnp.zeros((height, LANES - 2 * SIDE), F32)
    here = jnp.concatenate([far_left, left, template, right, far_right, blank], axis=1)

    for_even, for_odd, here = lax.optimization_barrier((for_even, for_odd, here))
    odd = swap(here, "visit", 1, 1)
    even = swap(here, "visit", 1, 0)
    first, last = here[:EDGE], here[height - EDGE :]
    ahead = v % 4 < 2
    near_rows = swap(jnp.where(ahead, last, first), "visit", 2, 0)
    away_rows = swap(jnp.where(ahead, first, last), "visit", 2, 2)

    for_odd, even, row_taps = lax.optimization_barrier((for_odd, even, row_taps))
    sum_even = swap(for_even, "det", 1, 0)
    sum_odd = swap(for_odd, "det", 1, 1)

    flat, table, table8, top = pl.pallas_call(
        functools.partial(taps_kernel, n_rows, n_cols),
        out_shape=(
            pltpu.VMEM((n_sets * n_terms, DEPTH), F32),
            pltpu.VMEM((n_sets, (n_terms + FINE) * block, DEPTH), BF16),
            pltpu.VMEM((n_sets, FINE * block, DEPTH), F8),
            pltpu.VMEM((ROWS, LANES), F32),
        ),
        in_specs=[vmem] * 3,
        out_specs=(vmem,) * 4,
        scratch_shapes=[pltpu.VMEM((TILES, n_sets * n_terms * ROWS, LANES), F32)],
        compiler_params=pltpu.CompilerParams(vmem_limit_bytes=56 * MIB),
        cost_estimate=pl.CostEstimate(flops=3 << 30, bytes_accessed=5 << 20, transcendentals=0),
        name="tap_tables",
    )(row_taps.T, col_taps.T, jnp.swapaxes(kernel_coef, 0, 1).reshape(n_terms * n_sets, n_basis))

    flat, table, table8, top = [
        pltpu.with_memory_space_constraint(x, pltpu.VMEM) for x in (flat, table, table8, top)
    ]

    even, odd, near_rows, away_rows, here = [
        pltpu.with_memory_space_constraint(x, pltpu.VMEM) for x in (even, odd, near_rows, away_rows, here)
    ]

    flops = n_strips * 2 * n_terms * block * DEPTH * 2 * LANES * 2
    buffers = [pltpu.VMEM((DEPTH, 2 * LANES), kind) for kind in (BF16, F8, BF16, F8)]
    image, models = pl.pallas_call(
        functools.partial(strips_kernel, n_rows, n_cols),
        out_shape=(
            pltpu.VMEM((2, PHASES, 4, 3 * height + 2 * EDGE, LANES), F32),
            pltpu.VMEM(((n_strips - LATER) * strip_rows, width), F32),
        ),
        in_specs=[smem] * 3 + [vmem] * 8,
        out_specs=(vmem, vmem),
        scratch_shapes=buffers,
        compiler_params=pltpu.CompilerParams(vmem_limit_bytes=32 * MIB),
        cost_estimate=pl.CostEstimate(flops=flops, bytes_accessed=14 << 20, transcendentals=0),
        name="strip_models",
    )(patch_of, box_row, kernel_set, top, near_rows, away_rows, here, even, odd, table8, table)

    image, models, sum_even, sum_odd = lax.optimization_barrier((image, models, sum_even, sum_odd))
    mid = mid + sum_even + sum_odd
    image, models = [pltpu.with_memory_space_constraint(x, pltpu.VMEM) for x in (image, models)]
    from_even = swap(jnp.where(v % 2 == 0, mid[2], mid[0]), "visit", 1, 0)
    from_odd = swap(jnp.where(v % 2 == 0, mid[0], mid[2]), "visit", 1, 1)

    patch_of, mid = lax.optimization_barrier((patch_of, mid))
    difference = pl.pallas_call(
        functools.partial(finish_kernel, n_rows, n_cols, height),
        out_shape=jax.ShapeDtypeStruct(strips.shape, F32),
        in_specs=[smem] * 3 + [vmem] * 5 + [hbm],
        out_specs=hbm,
        scratch_shapes=[pltpu.VMEM(strips.shape, F32), pltpu.VMEM((LATER * strip_rows, width), F32)]
        + buffers
        + [pltpu.SemaphoreType.DMA((5,))],
        compiler_params=pltpu.CompilerParams(vmem_limit_bytes=32 * MIB),
        cost_estimate=pl.CostEstimate(flops=flops // 4, bytes_accessed=4 << 20, transcendentals=0),
        name="finish",
    )(patch_of, box_row, kernel_set, top, table8, table, image, models, strips)

    coadd = pl.pallas_call(
        functools.partial(coadd_kernel, n_rows, n_cols),
        out_shape=jax.ShapeDtypeStruct(template.shape, F32),
        in_specs=[vmem, vmem] + [free] * 3,
        out_specs=vmem,
        scratch_shapes=[pltpu.VMEM(x.shape, F32) for x in (from_even, from_even, from_odd)]
        + [
            pltpu.VMEM((TILES, 3 * height, LANES), F32),
            pltpu.VMEM((TILES, 3 * height, LANES), F32),
            pltpu.VMEM((height, PHASES * LANES), F32),
        ]
        + [pltpu.VMEM((DEPTH, LANES), BF16)] * 4
        + [pltpu.SemaphoreType.DMA((3,))],
        compiler_params=pltpu.CompilerParams(vmem_limit_bytes=32 * MIB),
        cost_estimate=pl.CostEstimate(flops=6 << 30, bytes_accessed=3 << 20, transcendentals=0),
        name="coadd_models",
    )(flat, image, mid[1], from_even, from_odd)
    return difference, coadd


def solution(mesh):
    tiles = ("visit", "det")
    in_specs = (P(tiles, None, None), P(tiles, None), P(tiles), P(tiles), P("visit", "det"), P(), P(), P())
    out_specs = (P(tiles, None, None), P("visit", "det"))
    return jax.shard_map(per_device, mesh=mesh, in_specs=in_specs, out_specs=out_specs, check_vma=False)
```

```python
import functools

import jax
import jax.numpy as jnp
from jax import lax
from jax.experimental import pallas as pl
from jax.experimental.pallas import tpu as pltpu
from jax.sharding import PartitionSpec as P

F32 = jnp.float32
BF16 = jnp.bfloat16
F8 = jnp.float8_e4m3fn
HIGHEST = lax.Precision.HIGHEST

HALF = 10
SIDE = 12
EDGE = 16
PHASES = 4
LANES = 128
ROWS = 8
WIN = 32
SHIFTS = 24
DEPTH = SHIFTS * WIN
TILES = DEPTH // LANES
LATER = 8
FINE = 3
SCALE = 2.0**14
TOP = 256.0
MIB = 1024 * 1024


def iota(shape, dim):
    return lax.broadcasted_iota(jnp.int32, shape, dim)


def split(x):
    hi = x.astype(BF16)
    lo = (x - hi.astype(F32)).astype(BF16)
    return hi, lo


def mxu(a, b):
    return jnp.dot(a, b, preferred_element_type=F32)


def exact(a, b):
    return jnp.dot(a, b, precision=HIGHEST, preferred_element_type=F32)


def to_phases(width):
    out = iota((width, PHASES * LANES), 1)
    source = (out % LANES) * PHASES + out // LANES
    return jnp.where(iota((width, PHASES * LANES), 0) == source, 1.0, 0.0).astype(BF16)


def from_phases():
    src = iota((PHASES * LANES, PHASES * LANES), 0)
    target = (src % LANES) * PHASES + src // LANES
    return jnp.where(iota((PHASES * LANES, PHASES * LANES), 1) == target, 1.0, 0.0).astype(BF16)


def place(patch, n_cols):
    step_row = (patch >> (n_cols.bit_length() - 1)) - lax.axis_index("visit") + 1
    step_col = (patch & (n_cols - 1)) - lax.axis_index("det") + 1
    return step_row, step_col


def sums_kernel(
    n_cols, patch_ref, row_ref, set_ref, strips_hbm, even_ref, mid_ref, odd_ref, order_ref, strips_ref, acc, sems
):
    n_strips, strip_rows, _ = strips_ref.shape
    n_parts = 4
    some = n_strips // n_parts
    copies = []
    for i in range(n_parts):
        part = pl.ds(i * some, some)
        copies.append(pltpu.make_async_copy(strips_hbm.at[part], strips_ref.at[part], sems.at[i]))
        copies[i].start()
    acc[...] = jnp.zeros(acc.shape, F32)
    height = acc.shape[2] - ROWS
    place_lane = iota((ROWS, LANES), 1)
    place_sub = iota((ROWS, LANES), 0)

    def one_strip(t, carry):
        step_row, step_col = place(patch_ref[t], n_cols)
        top = row_ref[t]
        q = step_col * 3 + step_row
        for c in range(PHASES):
            acc[q, c, pl.ds(top, strip_rows), :] += strips_ref[t, :, c * LANES : (c + 1) * LANES]
        hit = (place_sub == set_ref[t]) & (place_lane >= top) & (place_lane < top + strip_rows)
        acc[q, 0, height:, :] += jnp.where(hit, 1.0, 0.0)
        far_above = (step_row == 0) & (top < HALF)
        far_below = (step_row == 2) & (top + strip_rows + HALF > height)
        n_plain, n_far = carry
        far = (far_above | far_below).astype(jnp.int32)
        order_ref[jnp.where(far == 1, n_strips - 1 - n_far, n_plain)] = t
        return n_plain + 1 - far, n_far + far

    carry = (jnp.int32(0), jnp.int32(0))
    for i in range(n_parts):
        copies[i].wait()
        carry = lax.fori_loop(i * some, (i + 1) * some, one_strip, carry, unroll=4)
    order_ref[n_strips] = carry[0]
    parity = lax.axis_index("det") % 2
    for first, out in ((6 - 6 * parity, even_ref), (3, mid_ref), (6 * parity, odd_ref)):
        out[...] = acc[pl.ds(first, 3)]


def taps_kernel(
    n_rows, n_cols, row_taps_ref, col_taps_ref, coef_ref, flat_ref, table_ref, table8_ref, top_ref, wide
):
    taps = row_taps_ref.shape[0]
    lane = iota((taps, DEPTH), 1)
    sub = iota((taps, DEPTH), 0)
    row_part = exact(row_taps_ref[...].T, jnp.where(lane % WIN == sub, 1.0, 0.0))
    col_part = exact(col_taps_ref[...].T, jnp.where(lane // WIN == sub, 1.0, 0.0))
    n_sets = table_ref.shape[0]
    one, u, v, uu, uv, vv = [coef_ref[p * n_sets : (p + 1) * n_sets, :] for p in range(6)]
    u0 = (2 * lax.axis_index("det") + 1).astype(F32) / n_cols - 1.0
    v0 = (2 * lax.axis_index("visit") + 1).astype(F32) / n_rows - 1.0
    one, u, v = (
        one + u0 * (u + u0 * uu) + v0 * (v + u0 * uv + v0 * vv),
        u + 2.0 * u0 * uu + v0 * uv,
        v + u0 * uv + 2.0 * v0 * vv,
    )
    flat = exact(jnp.concatenate([one, v, u, uu, uv, vv], axis=0), row_part * col_part)
    flat_ref[...] = flat
    top = jnp.maximum(jnp.max(jnp.max(jnp.abs(flat), axis=1, keepdims=True), axis=0, keepdims=True), 1e-30)
    top_ref[...] = jnp.broadcast_to(top, top_ref.shape)
    scale = TOP / top
    n = flat.shape[0]
    block = PHASES * ROWS
    for dy in range(ROWS):
        moved = flat if dy == 0 else pltpu.roll(flat, dy, 1)
        for c in range(TILES):
            wide[c, pl.ds(dy, n, stride=ROWS), :] = moved[:, c * LANES : (c + 1) * LANES]
    for s in range(n_sets):
        for p in range(6):
            rows = on_phases(wide, (p * n_sets + s) * ROWS)
            hi = rows.astype(BF16)
            table_ref[s, p * block : (p + 1) * block, :] = hi
            if p < FINE:
                table_ref[s, (6 + p) * block : (7 + p) * block, :] = (rows - hi.astype(F32)).astype(BF16)
                table8_ref[s, p * block : (p + 1) * block, :] = (rows * scale).astype(F8)


def on_phases(wide, first):
    rows = jnp.concatenate([wide[c, pl.ds(first, ROWS), :] for c in range(TILES)], axis=1)
    return jnp.concatenate([rows] + [pltpu.roll(rows, dx * WIN, 1) for dx in range(1, PHASES)], axis=0)


def columns_of(step_col, n_cols, width):
    shape = (PHASES * ROWS, LANES)
    col = (step_col - 1) * width - width // 2 + iota(shape, 1) * PHASES + iota(shape, 0) // ROWS
    return 2.0 * (col.astype(F32) + 0.5) / (n_cols * width)


def fill(image_ref, part, row, col, halves, kind, data):
    lane = iota((WIN, LANES), 1)
    for phase in range(PHASES):
        near, far = [image_ref[part, phase, col + i, pl.ds(row, WIN + (halves - 1) * ROWS), :] for i in range(2)]
        for half in range(halves):
            rows = slice(half * ROWS, half * ROWS + WIN)
            a, b = near[rows].astype(kind), far[rows].astype(kind)
            for shift in range((SIDE - HALF + SHIFTS - 1) // PHASES + 1):
                k = shift * PHASES + phase - (SIDE - HALF)
                if 0 <= k < SHIFTS:
                    moved = a if shift == 0 else pltpu.roll(jnp.where(lane < shift, b, a), LANES - shift, 1)
                    data[k * WIN : (k + 1) * WIN, half * LANES : (half + 1) * LANES] = moved


def model_loop(
    n_rows, n_cols, height, order_ref, patch_ref, row_ref, set_ref, top_ref, table8_ref, table_ref, image, image_row,
    buffers, first, last, models,
):
    width = PHASES * LANES
    block = PHASES * ROWS
    fine = FINE * block
    shape = (block, 2 * LANES)
    row_in = iota(shape, 0) % ROWS + iota(shape, 1) // LANES * ROWS
    undo = top_ref[0:1, 0:1] * (1.0 / (TOP * SCALE))

    def build(t, data_hi, data_lo):
        step_row, step_col = place(patch_ref[t], n_cols)
        row = step_row * height + row_ref[t] + EDGE - HALF
        fill(image, 0, image_row(row), step_col, 2, BF16, data_hi)
        fill(image, 1, image_row(row), step_col, 2, F8, data_lo)

    def multiply(t, data_hi, data_lo):
        step_row, step_col = place(patch_ref[t], n_cols)
        which = set_ref[t]
        big = mxu(table_ref[which], data_hi[...])
        small = mxu(table8_ref[which], data_lo[...])
        exact_terms = big[:fine] + big[6 * block :] + small * undo
        term_1, term_v, term_u = [exact_terms[p * block : (p + 1) * block] for p in range(FINE)]
        term_uu, term_uv, term_vv = [big[p * block : (p + 1) * block] for p in range(FINE, 6)]
        one_u = columns_of(step_col, n_cols, width)
        u = jnp.concatenate([one_u, one_u], axis=1)
        y = (step_row - 1) * height - height // 2 + row_ref[t] + row_in
        v = 2.0 * (y.astype(F32) + 0.5) / (n_rows * height)
        model = term_1 + u * (term_u + u * term_uu + v * term_uv) + v * (term_v + v * term_vv)
        for half in range(2):
            rows_of = pl.ds(pl.multiple_of(t * 2 * ROWS + half * ROWS, ROWS), ROWS)
            for dx in range(PHASES):
                models[rows_of, dx * LANES : (dx + 1) * LANES] = model[
                    dx * ROWS : (dx + 1) * ROWS, half * LANES : (half + 1) * LANES
                ]

    def strip(i):
        return order_ref[jnp.minimum(i, last - 1)]

    some = 4

    def some_strips(i, carry):
        for j in range(some):
            build(strip(first + some * i + j + 1), *buffers[(j + 1) % 2])
            multiply(strip(first + some * i + j), *buffers[j % 2])
        return carry

    @pl.when(last > first)
    def _():
        build(strip(first), *buffers[0])
        lax.fori_loop(0, (last - first + some - 1) // some, some_strips, 0)


def plain_count(order_ref, n_strips):
    n_plain = order_ref[n_strips]
    return jnp.minimum(n_plain, n_strips - LATER), n_plain


def phases_of(pieces, cols, store):
    parts = [split(piece) for piece in pieces]
    both = jnp.concatenate([hi for hi, _ in parts] + [lo for _, lo in parts], axis=0)
    rows = both.shape[0] // 2
    moved = mxu(both, to_phases(PHASES * LANES)[: cols.stop - cols.start])
    for f in range(PHASES):
        for part in range(2):
            some = moved[part * rows : (part + 1) * rows, f * LANES : (f + 1) * LANES]
            store(part, f, some * SCALE if part else some)


def strips_kernel(
    n_rows, n_cols, order_ref, patch_ref, row_ref, set_ref, top_ref, here_ref, even_ref, odd_ref,
    table8_ref, table_ref, image, models, hi_a, lo_a, hi_b, lo_b,
):
    height = here_ref.shape[0]
    width = PHASES * LANES
    blank = jnp.zeros(image.shape[:3] + (EDGE, LANES), F32)
    image[:, :, :, 0:EDGE, :] = blank
    image[:, :, :, EDGE + 3 * height :, :] = blank
    upper = lax.axis_index("visit") % 2 == 0
    for b in range(4):
        cols = slice(b * width, min((b + 1) * width, here_ref.shape[1]))
        here, even, odd = [r[:, cols] for r in (here_ref, even_ref, odd_ref)]

        def store(part, f, some):
            image[part, f, b, EDGE : EDGE + 3 * height, :] = some

        phases_of((jnp.where(upper, odd, even), here, jnp.where(upper, even, odd)), cols, store)

    count, _ = plain_count(order_ref, patch_ref.shape[0])
    model_loop(
        n_rows, n_cols, height, order_ref, patch_ref, row_ref, set_ref, top_ref, table8_ref, table_ref, image,
        lambda row: row, ((hi_a, lo_a), (hi_b, lo_b)), 0, count, models,
    )


def finish_kernel(
    n_rows, n_cols, height, order_ref, patch_ref, row_ref, set_ref, top_ref, near_rows, away_rows,
    table8_ref, table_ref, image, models_ref, strips_hbm, diff_hbm,
    strips_ref, models, ends, hi_a, lo_a, hi_b, lo_b, sems,
):
    n_strips, strip_rows, width = strips_ref.shape
    copy_strips = pltpu.make_async_copy(strips_hbm, strips_ref, sems.at[4])
    copy_strips.start()
    models[...] = models_ref[...]

    half = ends.shape[3] // 2
    rows = image.shape[3]
    ends[:, :, :, EDGE:half, :] = image[:, :, :, EDGE:half, :]
    ends[:, :, :, half : 2 * half - EDGE, :] = image[:, :, :, rows - half : rows - EDGE, :]
    ahead = lax.axis_index("visit") % 4 < 2
    for b in range(4):
        cols = slice(b * width, min((b + 1) * width, near_rows.shape[1]))
        near, away = near_rows[:, cols], away_rows[:, cols]

        def store(part, f, some):
            ends[part, f, b, 0:EDGE, :] = some[0:EDGE]
            ends[part, f, b, 2 * half - EDGE :, :] = some[EDGE:]

        phases_of((jnp.where(ahead, away, near), jnp.where(ahead, near, away)), cols, store)

    count, n_plain = plain_count(order_ref, n_strips)
    buffers = ((hi_a, lo_a), (hi_b, lo_b))
    model_loop(
        n_rows, n_cols, height, order_ref, patch_ref, row_ref, set_ref, top_ref, table8_ref, table_ref, image,
        lambda row: row, buffers, count, n_plain, models,
    )
    model_loop(
        n_rows, n_cols, height, order_ref, patch_ref, row_ref, set_ref, top_ref, table8_ref, table_ref, ends,
        lambda row: jnp.where(row < half, row, row - (rows - 2 * half)), buffers, n_plain, n_strips, models,
    )
    gather = from_phases()
    gather = jnp.concatenate([gather, gather], axis=0)
    copy_strips.wait()
    some = 16
    for c in range(n_strips // some):
        natural = mxu(jnp.concatenate(split(models[c * some * strip_rows : (c + 1) * some * strip_rows]), axis=1), gather)
        part = pl.ds(c * some, some)
        strips_ref[part] = strips_ref[part] - natural.reshape(some, strip_rows, width)
        pltpu.make_async_copy(strips_ref.at[part], diff_hbm.at[part], sems.at[c]).start()
    for c in range(n_strips // some):
        part = pl.ds(c * some, some)
        pltpu.make_async_copy(strips_ref.at[part], diff_hbm.at[part], sems.at[c]).wait()


def coadd_kernel(
    n_rows, n_cols, flat_ref, image, mid_any, even_any, odd_any, coadd_ref,
    mid_ref, even_ref, odd_ref, taps, wide, models, hi_a, lo_a, hi_b, lo_b, sems,
):
    height, width = coadd_ref.shape
    sources = (mid_any, even_any, odd_any)
    targets = (mid_ref, even_ref, odd_ref)
    copies = [pltpu.make_async_copy(source, target, sems.at[i]) for i, (source, target) in enumerate(zip(sources, targets))]
    for copy in copies:
        copy.start()
    for copy in copies:
        copy.wait()
    count = mid_ref[0, height:, :] + even_ref[0, height:, :] + odd_ref[0, height:, :]
    n_sets = count.shape[0]
    v = 2.0 * ((iota(count.shape, 1) - height // 2).astype(F32) + 0.5) / (n_rows * height)

    def three(x, p):
        taps_of = flat_ref[p * n_sets : (p + 1) * n_sets, :]
        x_hi, t_hi = x.astype(BF16).astype(F32), taps_of.astype(BF16).astype(F32)
        return [(x_hi, t_hi), (x - x_hi, t_hi), (x_hi, taps_of - t_hi)]

    by_power = []
    for terms in ((0, 1, 5), (2, 4), (3,)):
        rows, x = [], count
        for p in terms:
            rows, x = rows + three(x, p), x * v
        sides = [jnp.concatenate(side, axis=0) for side in zip(*rows)]
        by_power.append(mxu(sides[0].T.astype(BF16), sides[1].astype(BF16)))
    for a in range(3):
        for c in range(TILES):
            taps[c, a * height : (a + 1) * height, :] = by_power[a][:, c * LANES : (c + 1) * LANES]
    n = 3 * height // ROWS
    for dy in range(ROWS):
        some = jnp.concatenate([taps[c, pl.ds(dy, n, stride=ROWS), :] for c in range(TILES)], axis=1)
        moved = some if dy == 0 else pltpu.roll(some, dy, 1)
        for c in range(TILES):
            wide[c, pl.ds(dy, n, stride=ROWS), :] = moved[:, c * LANES : (c + 1) * LANES]
    one_u = columns_of(1, n_cols, width)

    def build(b, data_hi, data_lo):
        fill(image, 0, height + b * ROWS + EDGE - HALF, 1, 1, BF16, data_hi)
        fill(image, 1, height + b * ROWS + EDGE - HALF, 1, 1, BF16, data_lo)

    def multiply(b, data_hi, data_lo):
        row = pl.multiple_of(b * ROWS, ROWS)
        fine_hi, fine_lo = split(on_phases(wide, row))
        rest = [on_phases(wide, a * height + row).astype(BF16) for a in (1, 2)]
        big = mxu(jnp.concatenate([fine_hi] + rest + [fine_lo], axis=0), data_hi[...])
        terms = big.reshape(4, PHASES * ROWS, LANES)
        small = mxu(fine_hi, data_lo[...]) * (1.0 / SCALE)
        model = terms[0] + terms[3] + small + one_u * (terms[1] + one_u * terms[2])
        for dx in range(PHASES):
            models[pl.ds(row, ROWS), dx * LANES : (dx + 1) * LANES] = model[dx * ROWS : (dx + 1) * ROWS]

    n_blocks = height // ROWS
    build(0, hi_a, lo_a)
    some = 8
    buffers = ((hi_a, lo_a), (hi_b, lo_b))

    def some_blocks(i, carry):
        for j in range(some):
            b = some * i + j
            build(jnp.minimum(b + 1, n_blocks - 1), *buffers[(j + 1) % 2])
            multiply(b, *buffers[j % 2])
        return carry

    lax.fori_loop(0, n_blocks // some, some_blocks, 0)
    gather = from_phases()
    gather = jnp.concatenate([gather, gather], axis=0)
    natural = mxu(jnp.concatenate(split(models[...]), axis=1), gather)
    for c in range(PHASES):
        total = mid_ref[c, 0:height, :] + even_ref[c, 0:height, :] + odd_ref[c, 0:height, :]
        coadd_ref[:, c * LANES : (c + 1) * LANES] = total - natural[:, c * LANES : (c + 1) * LANES]


def swap(x, axis, apart, first):
    size = lax.axis_size(axis)
    lower = [i for i in range(size - apart) if (i - first) % (2 * apart) < apart]
    pairs = [(i, i + apart) for i in lower] + [(i + apart, i) for i in lower]
    return lax.ppermute(x, axis, pairs)


def per_device(strips, patch_of, box_row, kernel_set, template, row_taps, col_taps, kernel_coef):
    n_rows, n_cols = lax.axis_size("visit"), lax.axis_size("det")
    n_strips, strip_rows, width = strips.shape
    height = template.shape[0]
    n_sets, n_terms, n_basis = kernel_coef.shape
    block = PHASES * ROWS
    smem = pl.BlockSpec(memory_space=pltpu.SMEM)
    vmem = pl.BlockSpec(memory_space=pltpu.VMEM)
    hbm = pl.BlockSpec(memory_space=pltpu.HBM)
    free = pl.BlockSpec(memory_space=pl.ANY)

    patch_of = patch_of.reshape(n_strips)

    v, d = lax.axis_index("visit"), lax.axis_index("det")
    first, last = template[:, :SIDE], template[:, width - SIDE :]
    ahead = d % 4 < 2
    even = swap(template, "det", 1, 0)
    odd = swap(template, "det", 1, 1)
    for_near, for_away = jnp.where(ahead, last, first), jnp.where(ahead, first, last)
    patch_of, for_near, for_away = lax.optimization_barrier((patch_of, for_near, for_away))
    near = swap(for_near, "det", 2, 0)
    away = swap(for_away, "det", 2, 2)

    sums = jax.ShapeDtypeStruct((3, PHASES, height + ROWS, LANES), F32)
    for_even, mid, for_odd, order = pl.pallas_call(
        functools.partial(sums_kernel, n_cols),
        out_shape=(sums, sums, sums, jax.ShapeDtypeStruct((n_strips + 1,), jnp.int32)),
        in_specs=[smem] * 3 + [hbm],
        out_specs=(vmem,) * 3 + (smem,),
        scratch_shapes=[
            pltpu.VMEM(strips.shape, F32),
            pltpu.VMEM((9, PHASES, height + ROWS, LANES), F32),
            pltpu.SemaphoreType.DMA((4,)),
        ],
        compiler_params=pltpu.CompilerParams(vmem_limit_bytes=56 * MIB),
        cost_estimate=pl.CostEstimate(flops=3 << 30, bytes_accessed=5 << 20, transcendentals=0),
        name="strip_sums",
    )(patch_of, box_row, kernel_set, strips)

    far_left, far_right = jnp.where(ahead, away, near), jnp.where(ahead, near, away)
    left, right = jnp.where(d % 2 == 0, odd, even), jnp.where(d % 2 == 0, even, odd)
    blank = jnp.zeros((height, LANES - 2 * SIDE), F32)
    here = jnp.concatenate([far_left, left, template, right, far_right, blank], axis=1)

    for_even, for_odd, here = lax.optimization_barrier((for_even, for_odd, here))
    odd = swap(here, "visit", 1, 1)
    even = swap(here, "visit", 1, 0)
    first, last = here[:EDGE], here[height - EDGE :]
    ahead = v % 4 < 2
    near_rows = swap(jnp.where(ahead, last, first), "visit", 2, 0)
    away_rows = swap(jnp.where(ahead, first, last), "visit", 2, 2)

    for_odd, even, row_taps = lax.optimization_barrier((for_odd, even, row_taps))
    sum_even = swap(for_even, "det", 1, 0)
    sum_odd = swap(for_odd, "det", 1, 1)

    flat, table, table8, top = pl.pallas_call(
        functools.partial(taps_kernel, n_rows, n_cols),
        out_shape=(
            pltpu.VMEM((n_sets * n_terms, DEPTH), F32),
            pltpu.VMEM((n_sets, (n_terms + FINE) * block, DEPTH), BF16),
            pltpu.VMEM((n_sets, FINE * block, DEPTH), F8),
            pltpu.VMEM((ROWS, LANES), F32),
        ),
        in_specs=[vmem] * 3,
        out_specs=(vmem,) * 4,
        scratch_shapes=[pltpu.VMEM((TILES, n_sets * n_terms * ROWS, LANES), F32)],
        compiler_params=pltpu.CompilerParams(vmem_limit_bytes=56 * MIB),
        cost_estimate=pl.CostEstimate(flops=3 << 30, bytes_accessed=5 << 20, transcendentals=0),
        name="tap_tables",
    )(row_taps.T, col_taps.T, jnp.swapaxes(kernel_coef, 0, 1).reshape(n_terms * n_sets, n_basis))

    flat, table, table8, top = [
        pltpu.with_memory_space_constraint(x, pltpu.VMEM) for x in (flat, table, table8, top)
    ]

    even, odd, here = [pltpu.with_memory_space_constraint(x, pltpu.VMEM) for x in (even, odd, here)]

    flops = n_strips * 2 * n_terms * block * DEPTH * 2 * LANES * 2
    buffers = [pltpu.VMEM((DEPTH, 2 * LANES), kind) for kind in (BF16, F8, BF16, F8)]
    image, models = pl.pallas_call(
        functools.partial(strips_kernel, n_rows, n_cols),
        out_shape=(
            pltpu.VMEM((2, PHASES, 4, 3 * height + 2 * EDGE, LANES), F32),
            pltpu.VMEM((n_strips * strip_rows, width), F32),
        ),
        in_specs=[smem] * 4 + [vmem] * 6,
        out_specs=(vmem, vmem),
        scratch_shapes=buffers,
        compiler_params=pltpu.CompilerParams(vmem_limit_bytes=32 * MIB),
        cost_estimate=pl.CostEstimate(flops=flops, bytes_accessed=14 << 20, transcendentals=0),
        name="strip_models",
    )(order, patch_of, box_row, kernel_set, top, here, even, odd, table8, table)

    image, models, sum_even, sum_odd = lax.optimization_barrier((image, models, sum_even, sum_odd))
    mid = mid + sum_even + sum_odd
    image, models = [pltpu.with_memory_space_constraint(x, pltpu.VMEM) for x in (image, models)]
    from_even = swap(jnp.where(v % 2 == 0, mid[2], mid[0]), "visit", 1, 0)
    from_odd = swap(jnp.where(v % 2 == 0, mid[0], mid[2]), "visit", 1, 1)

    patch_of, mid = lax.optimization_barrier((patch_of, mid))
    difference = pl.pallas_call(
        functools.partial(finish_kernel, n_rows, n_cols, height),
        out_shape=jax.ShapeDtypeStruct(strips.shape, F32),
        in_specs=[smem] * 4 + [vmem] * 7 + [hbm],
        out_specs=hbm,
        scratch_shapes=[
            pltpu.VMEM(strips.shape, F32),
            pltpu.VMEM((n_strips * strip_rows, width), F32),
            pltpu.VMEM((2, PHASES, 4, 2 * (EDGE + 5 * ROWS), LANES), F32),
        ]
        + buffers
        + [pltpu.SemaphoreType.DMA((5,))],
        compiler_params=pltpu.CompilerParams(vmem_limit_bytes=32 * MIB),
        cost_estimate=pl.CostEstimate(flops=flops // 4, bytes_accessed=4 << 20, transcendentals=0),
        name="finish",
    )(order, patch_of, box_row, kernel_set, top, near_rows, away_rows, table8, table, image, models, strips)

    coadd = pl.pallas_call(
        functools.partial(coadd_kernel, n_rows, n_cols),
        out_shape=jax.ShapeDtypeStruct(template.shape, F32),
        in_specs=[vmem, vmem] + [free] * 3,
        out_specs=vmem,
        scratch_shapes=[pltpu.VMEM(x.shape, F32) for x in (from_even, from_even, from_odd)]
        + [
            pltpu.VMEM((TILES, 3 * height, LANES), F32),
            pltpu.VMEM((TILES, 3 * height, LANES), F32),
            pltpu.VMEM((height, PHASES * LANES), F32),
        ]
        + [pltpu.VMEM((DEPTH, LANES), BF16)] * 4
        + [pltpu.SemaphoreType.DMA((3,))],
        compiler_params=pltpu.CompilerParams(vmem_limit_bytes=32 * MIB),
        cost_estimate=pl.CostEstimate(flops=6 << 30, bytes_accessed=3 << 20, transcendentals=0),
        name="coadd_models",
    )(flat, image, mid[1], from_even, from_odd)
    return difference, coadd


def solution(mesh):
    tiles = ("visit", "det")
    in_specs = (P(tiles, None, None), P(tiles, None), P(tiles), P(tiles), P("visit", "det"), P(), P(), P())
    out_specs = (P(tiles, None, None), P("visit", "det"))
    return jax.shard_map(per_device, mesh=mesh, in_specs=in_specs, out_specs=out_specs, check_vma=False)
```

```python
import functools

import jax
import jax.numpy as jnp
from jax import lax
from jax.experimental import pallas as pl
from jax.experimental.pallas import tpu as pltpu
from jax.sharding import PartitionSpec as P

F32 = jnp.float32
BF16 = jnp.bfloat16
F8 = jnp.float8_e4m3fn
HIGHEST = lax.Precision.HIGHEST

HALF = 10
SIDE = 12
EDGE = 16
PHASES = 4
LANES = 128
ROWS = 8
WIN = 32
SHIFTS = 24
DEPTH = SHIFTS * WIN
TILES = DEPTH // LANES
LATER = 8
FINE = 3
SCALE = 2.0**14
TOP = 256.0
MIB = 1024 * 1024


def iota(shape, dim):
    return lax.broadcasted_iota(jnp.int32, shape, dim)


def split(x):
    hi = x.astype(BF16)
    lo = (x - hi.astype(F32)).astype(BF16)
    return hi, lo


def mxu(a, b):
    return jnp.dot(a, b, preferred_element_type=F32)


def exact(a, b):
    return jnp.dot(a, b, precision=HIGHEST, preferred_element_type=F32)


def to_phases(width):
    out = iota((width, PHASES * LANES), 1)
    source = (out % LANES) * PHASES + out // LANES
    return jnp.where(iota((width, PHASES * LANES), 0) == source, 1.0, 0.0).astype(BF16)


def from_phases():
    src = iota((PHASES * LANES, PHASES * LANES), 0)
    target = (src % LANES) * PHASES + src // LANES
    return jnp.where(iota((PHASES * LANES, PHASES * LANES), 1) == target, 1.0, 0.0).astype(BF16)


def place(patch, n_cols):
    step_row = (patch >> (n_cols.bit_length() - 1)) - lax.axis_index("visit") + 1
    step_col = (patch & (n_cols - 1)) - lax.axis_index("det") + 1
    return step_row, step_col


def sums_kernel(n_cols, patch_ref, row_ref, set_ref, strips_hbm, even_ref, mid_ref, odd_ref, strips_ref, acc, sems):
    n_strips, strip_rows, _ = strips_ref.shape
    n_parts = 4
    some = n_strips // n_parts
    copies = []
    for i in range(n_parts):
        part = pl.ds(i * some, some)
        copies.append(pltpu.make_async_copy(strips_hbm.at[part], strips_ref.at[part], sems.at[i]))
        copies[i].start()
    acc[...] = jnp.zeros(acc.shape, F32)
    height = acc.shape[2] - ROWS
    place_lane = iota((ROWS, LANES), 1)
    place_sub = iota((ROWS, LANES), 0)

    def one_strip(t, carry):
        step_row, step_col = place(patch_ref[t], n_cols)
        top = row_ref[t]
        q = step_col * 3 + step_row
        for c in range(PHASES):
            acc[q, c, pl.ds(top, strip_rows), :] += strips_ref[t, :, c * LANES : (c + 1) * LANES]
        hit = (place_sub == set_ref[t]) & (place_lane >= top) & (place_lane < top + strip_rows)
        acc[q, 0, height:, :] += jnp.where(hit, 1.0, 0.0)
        return carry

    for i in range(n_parts):
        copies[i].wait()
        lax.fori_loop(i * some, (i + 1) * some, one_strip, 0, unroll=4)
    parity = lax.axis_index("det") % 2
    for first, out in ((6 - 6 * parity, even_ref), (3, mid_ref), (6 * parity, odd_ref)):
        out[...] = acc[pl.ds(first, 3)]


def taps_kernel(
    n_rows, n_cols, row_taps_ref, col_taps_ref, coef_ref, flat_ref, table_ref, table8_ref, top_ref, wide
):
    taps = row_taps_ref.shape[0]
    lane = iota((taps, DEPTH), 1)
    sub = iota((taps, DEPTH), 0)
    row_part = exact(row_taps_ref[...].T, jnp.where(lane % WIN == sub, 1.0, 0.0))
    col_part = exact(col_taps_ref[...].T, jnp.where(lane // WIN == sub, 1.0, 0.0))
    n_sets = table_ref.shape[0]
    one, u, v, uu, uv, vv = [coef_ref[p * n_sets : (p + 1) * n_sets, :] for p in range(6)]
    u0 = (2 * lax.axis_index("det") + 1).astype(F32) / n_cols - 1.0
    v0 = (2 * lax.axis_index("visit") + 1).astype(F32) / n_rows - 1.0
    one, u, v = (
        one + u0 * (u + u0 * uu) + v0 * (v + u0 * uv + v0 * vv),
        u + 2.0 * u0 * uu + v0 * uv,
        v + u0 * uv + 2.0 * v0 * vv,
    )
    flat = exact(jnp.concatenate([one, v, u, uu, uv, vv], axis=0), row_part * col_part)
    flat_ref[...] = flat
    top = jnp.maximum(jnp.max(jnp.max(jnp.abs(flat), axis=1, keepdims=True), axis=0, keepdims=True), 1e-30)
    top_ref[...] = jnp.broadcast_to(top, top_ref.shape)
    scale = TOP / top
    n = flat.shape[0]
    block = PHASES * ROWS
    for dy in range(ROWS):
        moved = flat if dy == 0 else pltpu.roll(flat, dy, 1)
        for c in range(TILES):
            wide[c, pl.ds(dy, n, stride=ROWS), :] = moved[:, c * LANES : (c + 1) * LANES]
    for s in range(n_sets):
        for p in range(6):
            rows = on_phases(wide, (p * n_sets + s) * ROWS)
            hi = rows.astype(BF16)
            table_ref[s, p * block : (p + 1) * block, :] = hi
            if p < FINE:
                table_ref[s, (6 + p) * block : (7 + p) * block, :] = (rows - hi.astype(F32)).astype(BF16)
                table8_ref[s, p * block : (p + 1) * block, :] = (rows * scale).astype(F8)


def on_phases(wide, first):
    rows = jnp.concatenate([wide[c, pl.ds(first, ROWS), :] for c in range(TILES)], axis=1)
    return jnp.concatenate([rows] + [pltpu.roll(rows, dx * WIN, 1) for dx in range(1, PHASES)], axis=0)


def columns_of(step_col, n_cols, width):
    shape = (PHASES * ROWS, LANES)
    col = (step_col - 1) * width - width // 2 + iota(shape, 1) * PHASES + iota(shape, 0) // ROWS
    return 2.0 * (col.astype(F32) + 0.5) / (n_cols * width)


def fill(shifted_ref, row, col, halves, data_hi, data_lo):
    for k in range(SHIFTS):
        x = shifted_ref[k, col, pl.ds(row, WIN + (halves - 1) * ROWS), :]
        lo = (x - x.astype(BF16).astype(F32)) * SCALE
        for half in range(halves):
            rows = slice(half * ROWS, half * ROWS + WIN)
            place_in = (slice(k * WIN, (k + 1) * WIN), slice(half * LANES, (half + 1) * LANES))
            data_hi[place_in] = x[rows].astype(BF16)
            data_lo[place_in] = lo[rows].astype(data_lo.dtype)


def model_loop(
    n_rows, n_cols, height, patch_ref, row_ref, set_ref, top_ref, table8_ref, table_ref, shifted_ref, buffers, first, last, store
):
    width = PHASES * LANES
    block = PHASES * ROWS
    fine = FINE * block
    shape = (block, 2 * LANES)
    row_in = iota(shape, 0) % ROWS + iota(shape, 1) // LANES * ROWS
    undo = top_ref[0:1, 0:1] * (1.0 / (TOP * SCALE))

    def build(t, data_hi, data_lo):
        step_row, step_col = place(patch_ref[t], n_cols)
        row = step_row * height + row_ref[t] + EDGE - HALF
        fill(shifted_ref, row, step_col, 2, data_hi, data_lo)

    def multiply(t, data_hi, data_lo):
        step_row, step_col = place(patch_ref[t], n_cols)
        which = set_ref[t]
        big = mxu(table_ref[which], data_hi[...])
        small = mxu(table8_ref[which], data_lo[...])
        exact_terms = big[:fine] + big[6 * block :] + small * undo
        term_1, term_v, term_u = [exact_terms[p * block : (p + 1) * block] for p in range(FINE)]
        term_uu, term_uv, term_vv = [big[p * block : (p + 1) * block] for p in range(FINE, 6)]
        one_u = columns_of(step_col, n_cols, width)
        u = jnp.concatenate([one_u, one_u], axis=1)
        y = (step_row - 1) * height - height // 2 + row_ref[t] + row_in
        v = 2.0 * (y.astype(F32) + 0.5) / (n_rows * height)
        store(t, term_1 + u * (term_u + u * term_uu + v * term_uv) + v * (term_v + v * term_vv))

    build(first, *buffers[0])
    some = 4

    def some_strips(i, carry):
        for j in range(some):
            t = first + some * i + j
            build(jnp.minimum(t + 1, last - 1), *buffers[(j + 1) % 2])
            multiply(t, *buffers[j % 2])
        return carry

    lax.fori_loop(0, (last - first) // some, some_strips, 0)


def store_model(models, first, strip_rows, t, model):
    for half in range(2):
        rows_of = pl.ds(pl.multiple_of((t - first) * strip_rows + half * ROWS, ROWS), ROWS)
        for dx in range(PHASES):
            models[rows_of, dx * LANES : (dx + 1) * LANES] = model[
                dx * ROWS : (dx + 1) * ROWS, half * LANES : (half + 1) * LANES
            ]


def strips_kernel(
    n_rows, n_cols, patch_ref, row_ref, set_ref, top_ref, near_rows, away_rows, here_ref, even_ref, odd_ref,
    table8_ref, table_ref, shifted_ref, models, image, hi_a, lo_a, hi_b, lo_b,
):
    height = here_ref.shape[0]
    width = PHASES * LANES
    scatter = to_phases(width)
    rows = image.shape[2]
    upper = lax.axis_index("visit") % 2 == 0
    ahead = lax.axis_index("visit") % 4 < 2
    for b in range(4):
        cols = slice(b * width, min((b + 1) * width, here_ref.shape[1]))
        near, away, even, odd = [r[:, cols] for r in (near_rows, away_rows, even_ref, odd_ref)]
        pieces = (
            jnp.where(ahead, away, near),
            jnp.where(upper, odd, even),
            here_ref[:, cols],
            jnp.where(upper, even, odd),
            jnp.where(ahead, near, away),
        )
        parts = [split(piece) for piece in pieces]
        both = jnp.concatenate([hi for hi, _ in parts] + [lo for _, lo in parts], axis=0)
        moved = mxu(both, scatter[: cols.stop - cols.start])
        for f in range(PHASES):
            lanes = slice(f * LANES, (f + 1) * LANES)
            image[f, b] = moved[:rows, lanes] + moved[rows:, lanes]

    lane = iota((WIN, LANES), 1)

    def shift_rows(i, carry):
        at = pl.ds(pl.multiple_of(i * WIN, WIN), WIN)
        for phase in range(PHASES):
            tiles = [image[phase, b, at, :] for b in range(4)]
            for k in range(SHIFTS):
                if (k + SIDE - HALF) % PHASES == phase:
                    shift = (k + SIDE - HALF) // PHASES
                    for b in range(3):
                        a, c = tiles[b], tiles[b + 1]
                        moved = a if shift == 0 else pltpu.roll(jnp.where(lane < shift, c, a), LANES - shift, 1)
                        shifted_ref[k, b, at, :] = moved
        return carry

    lax.fori_loop(0, rows // WIN, shift_rows, 0)

    strip_rows = models.shape[0] // (patch_ref.shape[0] - LATER)
    model_loop(
        n_rows, n_cols, height, patch_ref, row_ref, set_ref, top_ref, table8_ref, table_ref, shifted_ref,
        ((hi_a, lo_a), (hi_b, lo_b)), 0, patch_ref.shape[0] - LATER,
        functools.partial(store_model, models, 0, strip_rows),
    )


def finish_kernel(
    n_rows, n_cols, height, patch_ref, row_ref, set_ref, top_ref, table8_ref, table_ref, shifted_ref, models, strips_hbm, diff_hbm,
    strips_ref, rest, hi_a, lo_a, hi_b, lo_b, sems,
):
    n_strips, strip_rows, width = strips_ref.shape
    copy_strips = pltpu.make_async_copy(strips_hbm, strips_ref, sems.at[4])
    copy_strips.start()
    model_loop(
        n_rows, n_cols, height, patch_ref, row_ref, set_ref, top_ref, table8_ref, table_ref, shifted_ref,
        ((hi_a, lo_a), (hi_b, lo_b)), n_strips - LATER, n_strips,
        functools.partial(store_model, rest, n_strips - LATER, strip_rows),
    )
    gather = from_phases()
    gather = jnp.concatenate([gather, gather], axis=0)
    copy_strips.wait()
    some = 32
    ready = models.shape[0]
    for c in range(n_strips // some):
        rows = slice(c * some * strip_rows, (c + 1) * some * strip_rows)
        found = models[rows] if rows.stop <= ready else jnp.concatenate([models[rows.start : ready], rest[...]], axis=0)
        natural = mxu(jnp.concatenate(split(found), axis=1), gather)
        part = pl.ds(c * some, some)
        strips_ref[part] = strips_ref[part] - natural.reshape(some, strip_rows, width)
        pltpu.make_async_copy(strips_ref.at[part], diff_hbm.at[part], sems.at[c]).start()
    for c in range(n_strips // some):
        part = pl.ds(c * some, some)
        pltpu.make_async_copy(strips_ref.at[part], diff_hbm.at[part], sems.at[c]).wait()


def coadd_kernel(
    n_rows, n_cols, flat_ref, shifted_ref, mid_any, left_any, right_any, even_any, odd_any, coadd_ref,
    parts_ref, taps, wide, models, hi_a, lo_a, hi_b, lo_b, sems,
):
    height, width = coadd_ref.shape
    sources = (mid_any, left_any, right_any, even_any, odd_any)
    copies = [pltpu.make_async_copy(source, parts_ref.at[i], sems.at[i]) for i, source in enumerate(sources)]
    for copy in copies:
        copy.start()
    for copy in copies:
        copy.wait()
    count = jnp.sum(parts_ref[:, 0, height:, :], axis=0)
    n_sets = count.shape[0]
    v = 2.0 * ((iota(count.shape, 1) - height // 2).astype(F32) + 0.5) / (n_rows * height)

    def three(x, p):
        taps_of = flat_ref[p * n_sets : (p + 1) * n_sets, :]
        x_hi, t_hi = x.astype(BF16).astype(F32), taps_of.astype(BF16).astype(F32)
        return [(x_hi, t_hi), (x - x_hi, t_hi), (x_hi, taps_of - t_hi)]

    by_power = []
    for terms in ((0, 1, 5), (2, 4), (3,)):
        rows, x = [], count
        for p in terms:
            rows, x = rows + three(x, p), x * v
        sides = [jnp.concatenate(side, axis=0) for side in zip(*rows)]
        by_power.append(mxu(sides[0].T.astype(BF16), sides[1].astype(BF16)))
    for a in range(3):
        for c in range(TILES):
            taps[c, a * height : (a + 1) * height, :] = by_power[a][:, c * LANES : (c + 1) * LANES]
    n = 3 * height // ROWS
    for dy in range(ROWS):
        some = jnp.concatenate([taps[c, pl.ds(dy, n, stride=ROWS), :] for c in range(TILES)], axis=1)
        moved = some if dy == 0 else pltpu.roll(some, dy, 1)
        for c in range(TILES):
            wide[c, pl.ds(dy, n, stride=ROWS), :] = moved[:, c * LANES : (c + 1) * LANES]
    one_u = columns_of(1, n_cols, width)

    def build(b, data_hi, data_lo):
        fill(shifted_ref, height + b * ROWS + EDGE - HALF, 1, 1, data_hi, data_lo)

    def multiply(b, data_hi, data_lo):
        row = pl.multiple_of(b * ROWS, ROWS)
        fine_hi, fine_lo = split(on_phases(wide, row))
        rest = [on_phases(wide, a * height + row).astype(BF16) for a in (1, 2)]
        big = mxu(jnp.concatenate([fine_hi] + rest + [fine_lo], axis=0), data_hi[...])
        terms = big.reshape(4, PHASES * ROWS, LANES)
        small = mxu(fine_hi, data_lo[...]) * (1.0 / SCALE)
        model = terms[0] + terms[3] + small + one_u * (terms[1] + one_u * terms[2])
        for dx in range(PHASES):
            models[pl.ds(row, ROWS), dx * LANES : (dx + 1) * LANES] = model[dx * ROWS : (dx + 1) * ROWS]

    n_blocks = height // ROWS
    build(0, hi_a, lo_a)
    some = 8
    buffers = ((hi_a, lo_a), (hi_b, lo_b))

    def some_blocks(i, carry):
        for j in range(some):
            b = some * i + j
            build(jnp.minimum(b + 1, n_blocks - 1), *buffers[(j + 1) % 2])
            multiply(b, *buffers[j % 2])
        return carry

    lax.fori_loop(0, n_blocks // some, some_blocks, 0)
    gather = from_phases()
    gather = jnp.concatenate([gather, gather], axis=0)
    natural = mxu(jnp.concatenate(split(models[...]), axis=1), gather)
    for c in range(PHASES):
        total = jnp.sum(parts_ref[:, c, 0:height, :], axis=0)
        coadd_ref[:, c * LANES : (c + 1) * LANES] = total - natural[:, c * LANES : (c + 1) * LANES]


def swap(x, axis, apart, first):
    size = lax.axis_size(axis)
    lower = [i for i in range(size - apart) if (i - first) % (2 * apart) < apart]
    pairs = [(i, i + apart) for i in lower] + [(i + apart, i) for i in lower]
    return lax.ppermute(x, axis, pairs)


def per_device(strips, patch_of, box_row, kernel_set, template, row_taps, col_taps, kernel_coef):
    n_rows, n_cols = lax.axis_size("visit"), lax.axis_size("det")
    n_strips, strip_rows, width = strips.shape
    height = template.shape[0]
    n_sets, n_terms, n_basis = kernel_coef.shape
    block = PHASES * ROWS
    smem = pl.BlockSpec(memory_space=pltpu.SMEM)
    vmem = pl.BlockSpec(memory_space=pltpu.VMEM)
    hbm = pl.BlockSpec(memory_space=pltpu.HBM)
    free = pl.BlockSpec(memory_space=pl.ANY)

    patch_of = patch_of.reshape(n_strips)

    v, d = lax.axis_index("visit"), lax.axis_index("det")
    first, last = template[:, :SIDE], template[:, width - SIDE :]
    ahead = d % 4 < 2
    even = swap(template, "det", 1, 0)
    odd = swap(template, "det", 1, 1)
    for_near, for_away = jnp.where(ahead, last, first), jnp.where(ahead, first, last)
    patch_of, for_near, for_away = lax.optimization_barrier((patch_of, for_near, for_away))
    near = swap(for_near, "det", 2, 0)
    away = swap(for_away, "det", 2, 2)

    sums = jax.ShapeDtypeStruct((3, PHASES, height + ROWS, LANES), F32)
    for_even, mid, for_odd = pl.pallas_call(
        functools.partial(sums_kernel, n_cols),
        out_shape=(sums, sums, sums),
        in_specs=[smem] * 3 + [hbm],
        out_specs=(vmem,) * 3,
        scratch_shapes=[
            pltpu.VMEM(strips.shape, F32),
            pltpu.VMEM((9, PHASES, height + ROWS, LANES), F32),
            pltpu.SemaphoreType.DMA((4,)),
        ],
        compiler_params=pltpu.CompilerParams(vmem_limit_bytes=56 * MIB),
        cost_estimate=pl.CostEstimate(flops=3 << 30, bytes_accessed=5 << 20, transcendentals=0),
        name="strip_sums",
    )(patch_of, box_row, kernel_set, strips)

    far_left, far_right = jnp.where(ahead, away, near), jnp.where(ahead, near, away)
    left, right = jnp.where(d % 2 == 0, odd, even), jnp.where(d % 2 == 0, even, odd)
    blank = jnp.zeros((height, LANES - 2 * SIDE), F32)
    here = jnp.concatenate([far_left, left, template, right, far_right, blank], axis=1)

    for_even, for_odd, here = lax.optimization_barrier((for_even, for_odd, here))
    odd = swap(here, "visit", 1, 1)
    even = swap(here, "visit", 1, 0)
    first, last = here[:EDGE], here[height - EDGE :]
    ahead = v % 4 < 2
    near_rows = swap(jnp.where(ahead, last, first), "visit", 2, 0)
    away_rows = swap(jnp.where(ahead, first, last), "visit", 2, 2)

    for_odd, even, row_taps = lax.optimization_barrier((for_odd, even, row_taps))
    sum_even = swap(for_even, "det", 1, 0)
    sum_odd = swap(for_odd, "det", 1, 1)

    flat, table, table8, top = pl.pallas_call(
        functools.partial(taps_kernel, n_rows, n_cols),
        out_shape=(
            pltpu.VMEM((n_sets * n_terms, DEPTH), F32),
            pltpu.VMEM((n_sets, (n_terms + FINE) * block, DEPTH), BF16),
            pltpu.VMEM((n_sets, FINE * block, DEPTH), F8),
            pltpu.VMEM((ROWS, LANES), F32),
        ),
        in_specs=[vmem] * 3,
        out_specs=(vmem,) * 4,
        scratch_shapes=[pltpu.VMEM((TILES, n_sets * n_terms * ROWS, LANES), F32)],
        compiler_params=pltpu.CompilerParams(vmem_limit_bytes=56 * MIB),
        cost_estimate=pl.CostEstimate(flops=3 << 30, bytes_accessed=5 << 20, transcendentals=0),
        name="tap_tables",
    )(row_taps.T, col_taps.T, jnp.swapaxes(kernel_coef, 0, 1).reshape(n_terms * n_sets, n_basis))

    flat, table, table8, top = [
        pltpu.with_memory_space_constraint(x, pltpu.VMEM) for x in (flat, table, table8, top)
    ]

    even, odd, near_rows, away_rows, here = [
        pltpu.with_memory_space_constraint(x, pltpu.VMEM) for x in (even, odd, near_rows, away_rows, here)
    ]

    flops = n_strips * 2 * n_terms * block * DEPTH * 2 * LANES * 2
    buffers = [pltpu.VMEM((DEPTH, 2 * LANES), kind) for kind in (BF16, F8, BF16, F8)]
    shifted, models = pl.pallas_call(
        functools.partial(strips_kernel, n_rows, n_cols),
        out_shape=(
            pltpu.VMEM((SHIFTS, 3, 3 * height + 2 * EDGE, LANES), F32),
            pltpu.VMEM(((n_strips - LATER) * strip_rows, width), F32),
        ),
        in_specs=[smem] * 3 + [vmem] * 8,
        out_specs=(vmem, vmem),
        scratch_shapes=[pltpu.VMEM((PHASES, 4, 3 * height + 2 * EDGE, LANES), F32)] + buffers,
        compiler_params=pltpu.CompilerParams(vmem_limit_bytes=16 * MIB),
        cost_estimate=pl.CostEstimate(flops=flops, bytes_accessed=14 << 20, transcendentals=0),
        name="strip_models",
    )(patch_of, box_row, kernel_set, top, near_rows, away_rows, here, even, odd, table8, table)

    shifted, models, sum_even, sum_odd = lax.optimization_barrier((shifted, models, sum_even, sum_odd))
    shifted, models = [pltpu.with_memory_space_constraint(x, pltpu.VMEM) for x in (shifted, models)]
    above, below = [mid[i] + sum_even[i] + sum_odd[i] for i in (0, 2)]
    for_even, for_odd = jnp.where(v % 2 == 0, below, above), jnp.where(v % 2 == 0, above, below)
    from_even = swap(for_even, "visit", 1, 0)
    from_odd = swap(for_odd, "visit", 1, 1)

    patch_of, for_even = lax.optimization_barrier((patch_of, for_even))
    difference = pl.pallas_call(
        functools.partial(finish_kernel, n_rows, n_cols, height),
        out_shape=jax.ShapeDtypeStruct(strips.shape, F32),
        in_specs=[smem] * 3 + [vmem] * 5 + [hbm],
        out_specs=hbm,
        scratch_shapes=[pltpu.VMEM(strips.shape, F32), pltpu.VMEM((LATER * strip_rows, width), F32)]
        + buffers
        + [pltpu.SemaphoreType.DMA((5,))],
        compiler_params=pltpu.CompilerParams(vmem_limit_bytes=16 * MIB),
        cost_estimate=pl.CostEstimate(flops=flops // 4, bytes_accessed=4 << 20, transcendentals=0),
        name="finish",
    )(patch_of, box_row, kernel_set, top, table8, table, shifted, models, strips)

    coadd = pl.pallas_call(
        functools.partial(coadd_kernel, n_rows, n_cols),
        out_shape=jax.ShapeDtypeStruct(template.shape, F32),
        in_specs=[vmem, vmem] + [free] * 5,
        out_specs=vmem,
        scratch_shapes=[
            pltpu.VMEM((5,) + from_even.shape, F32),
            pltpu.VMEM((TILES, 3 * height, LANES), F32),
            pltpu.VMEM((TILES, 3 * height, LANES), F32),
            pltpu.VMEM((height, PHASES * LANES), F32),
        ]
        + [pltpu.VMEM((DEPTH, LANES), BF16)] * 4
        + [pltpu.SemaphoreType.DMA((5,))],
        compiler_params=pltpu.CompilerParams(vmem_limit_bytes=16 * MIB),
        cost_estimate=pl.CostEstimate(flops=6 << 30, bytes_accessed=3 << 20, transcendentals=0),
        name="coadd_models",
    )(flat, shifted, mid[1], sum_even[1], sum_odd[1], from_even, from_odd)
    return difference, coadd


def solution(mesh):
    tiles = ("visit", "det")
    in_specs = (P(tiles, None, None), P(tiles, None), P(tiles), P(tiles), P("visit", "det"), P(), P(), P())
    out_specs = (P(tiles, None, None), P("visit", "det"))
    return jax.shard_map(per_device, mesh=mesh, in_specs=in_specs, out_specs=out_specs, check_vma=False)
```

```python
import functools

import jax
import jax.numpy as jnp
from jax import lax
from jax.experimental import pallas as pl
from jax.experimental.pallas import tpu as pltpu
from jax.sharding import PartitionSpec as P

F32 = jnp.float32
BF16 = jnp.bfloat16
F8 = jnp.float8_e4m3fn
HIGHEST = lax.Precision.HIGHEST

HALF = 10
SIDE = 12
EDGE = 16
PHASES = 4
LANES = 128
ROWS = 8
WIN = 32
SHIFTS = 24
DEPTH = SHIFTS * WIN
TILES = DEPTH // LANES
LATER = 8
FINE = 3
SCALE = 2.0**14
TOP = 256.0
MIB = 1024 * 1024


def iota(shape, dim):
    return lax.broadcasted_iota(jnp.int32, shape, dim)


def split(x):
    hi = x.astype(BF16)
    lo = (x - hi.astype(F32)).astype(BF16)
    return hi, lo


def mxu(a, b):
    return jnp.dot(a, b, preferred_element_type=F32)


def exact(a, b):
    return jnp.dot(a, b, precision=HIGHEST, preferred_element_type=F32)


def to_phases(width):
    out = iota((width, PHASES * LANES), 1)
    source = (out % LANES) * PHASES + out // LANES
    return jnp.where(iota((width, PHASES * LANES), 0) == source, 1.0, 0.0).astype(BF16)


def from_phases():
    src = iota((PHASES * LANES, PHASES * LANES), 0)
    target = (src % LANES) * PHASES + src // LANES
    return jnp.where(iota((PHASES * LANES, PHASES * LANES), 1) == target, 1.0, 0.0).astype(BF16)


def place(patch, n_cols):
    step_row = (patch >> (n_cols.bit_length() - 1)) - lax.axis_index("visit") + 1
    step_col = (patch & (n_cols - 1)) - lax.axis_index("det") + 1
    return step_row, step_col


def sums_kernel(n_cols, patch_ref, row_ref, set_ref, strips_hbm, even_ref, mid_ref, odd_ref, strips_ref, acc, sems):
    n_strips, strip_rows, _ = strips_ref.shape
    n_parts = 4
    some = n_strips // n_parts
    copies = []
    for i in range(n_parts):
        part = pl.ds(i * some, some)
        copies.append(pltpu.make_async_copy(strips_hbm.at[part], strips_ref.at[part], sems.at[i]))
        copies[i].start()
    acc[...] = jnp.zeros(acc.shape, F32)
    height = acc.shape[2] - ROWS
    place_lane = iota((ROWS, LANES), 1)
    place_sub = iota((ROWS, LANES), 0)

    def one_strip(t, carry):
        step_row, step_col = place(patch_ref[t], n_cols)
        top = row_ref[t]
        q = step_col * 3 + step_row
        for c in range(PHASES):
            acc[q, c, pl.ds(top, strip_rows), :] += strips_ref[t, :, c * LANES : (c + 1) * LANES]
        hit = (place_sub == set_ref[t]) & (place_lane >= top) & (place_lane < top + strip_rows)
        acc[q, 0, height:, :] += jnp.where(hit, 1.0, 0.0)
        return carry

    for i in range(n_parts):
        copies[i].wait()
        lax.fori_loop(i * some, (i + 1) * some, one_strip, 0, unroll=4)
    parity = lax.axis_index("det") % 2
    for first, out in ((6 - 6 * parity, even_ref), (3, mid_ref), (6 * parity, odd_ref)):
        out[...] = acc[pl.ds(first, 3)]


def taps_kernel(
    n_rows, n_cols, row_taps_ref, col_taps_ref, coef_ref, flat_ref, table_ref, table8_ref, top_ref, wide
):
    taps = row_taps_ref.shape[0]
    lane = iota((taps, DEPTH), 1)
    sub = iota((taps, DEPTH), 0)
    row_part = exact(row_taps_ref[...].T, jnp.where(lane % WIN == sub, 1.0, 0.0))
    col_part = exact(col_taps_ref[...].T, jnp.where(lane // WIN == sub, 1.0, 0.0))
    n_sets = table_ref.shape[0]
    one, u, v, uu, uv, vv = [coef_ref[p * n_sets : (p + 1) * n_sets, :] for p in range(6)]
    u0 = (2 * lax.axis_index("det") + 1).astype(F32) / n_cols - 1.0
    v0 = (2 * lax.axis_index("visit") + 1).astype(F32) / n_rows - 1.0
    one, u, v = (
        one + u0 * (u + u0 * uu) + v0 * (v + u0 * uv + v0 * vv),
        u + 2.0 * u0 * uu + v0 * uv,
        v + u0 * uv + 2.0 * v0 * vv,
    )
    flat = exact(jnp.concatenate([one, v, u, uu, uv, vv], axis=0), row_part * col_part)
    flat_ref[...] = flat
    top = jnp.maximum(jnp.max(jnp.max(jnp.abs(flat), axis=1, keepdims=True), axis=0, keepdims=True), 1e-30)
    top_ref[...] = jnp.broadcast_to(top, top_ref.shape)
    scale = TOP / top
    n = flat.shape[0]
    block = PHASES * ROWS
    for dy in range(ROWS):
        moved = flat if dy == 0 else pltpu.roll(flat, dy, 1)
        for c in range(TILES):
            wide[c, pl.ds(dy, n, stride=ROWS), :] = moved[:, c * LANES : (c + 1) * LANES]
    for s in range(n_sets):
        for p in range(6):
            rows = on_phases(wide, (p * n_sets + s) * ROWS)
            hi = rows.astype(BF16)
            table_ref[s, p * block : (p + 1) * block, :] = hi
            if p < FINE:
                table_ref[s, (6 + p) * block : (7 + p) * block, :] = (rows - hi.astype(F32)).astype(BF16)
                table8_ref[s, p * block : (p + 1) * block, :] = (rows * scale).astype(F8)


def on_phases(wide, first):
    rows = jnp.concatenate([wide[c, pl.ds(first, ROWS), :] for c in range(TILES)], axis=1)
    return jnp.concatenate([rows] + [pltpu.roll(rows, dx * WIN, 1) for dx in range(1, PHASES)], axis=0)


def columns_of(step_col, n_cols, width):
    shape = (PHASES * ROWS, LANES)
    col = (step_col - 1) * width - width // 2 + iota(shape, 1) * PHASES + iota(shape, 0) // ROWS
    return 2.0 * (col.astype(F32) + 0.5) / (n_cols * width)


def fill(image_ref, part, row, col, halves, kind, data):
    lane = iota((WIN, LANES), 1)
    for phase in range(PHASES):
        near, far = [image_ref[part, phase, col + i, pl.ds(row, WIN + (halves - 1) * ROWS), :] for i in range(2)]
        for half in range(halves):
            rows = slice(half * ROWS, half * ROWS + WIN)
            a, b = near[rows].astype(kind), far[rows].astype(kind)
            for shift in range((SIDE - HALF + SHIFTS - 1) // PHASES + 1):
                k = shift * PHASES + phase - (SIDE - HALF)
                if 0 <= k < SHIFTS:
                    moved = a if shift == 0 else pltpu.roll(jnp.where(lane < shift, b, a), LANES - shift, 1)
                    data[k * WIN : (k + 1) * WIN, half * LANES : (half + 1) * LANES] = moved


def model_loop(
    n_rows, n_cols, height, patch_ref, row_ref, set_ref, top_ref, table8_ref, table_ref, image, buffers, first, last, store
):
    width = PHASES * LANES
    block = PHASES * ROWS
    fine = FINE * block
    shape = (block, 2 * LANES)
    row_in = iota(shape, 0) % ROWS + iota(shape, 1) // LANES * ROWS
    undo = top_ref[0:1, 0:1] * (1.0 / (TOP * SCALE))

    def build(t, data_hi, data_lo):
        step_row, step_col = place(patch_ref[t], n_cols)
        row = step_row * height + row_ref[t] + EDGE - HALF
        fill(image, 0, row, step_col, 2, BF16, data_hi)
        fill(image, 1, row, step_col, 2, F8, data_lo)

    def multiply(t, data_hi, data_lo):
        step_row, step_col = place(patch_ref[t], n_cols)
        which = set_ref[t]
        big = mxu(table_ref[which], data_hi[...])
        small = mxu(table8_ref[which], data_lo[...])
        exact_terms = big[:fine] + big[6 * block :] + small * undo
        term_1, term_v, term_u = [exact_terms[p * block : (p + 1) * block] for p in range(FINE)]
        term_uu, term_uv, term_vv = [big[p * block : (p + 1) * block] for p in range(FINE, 6)]
        one_u = columns_of(step_col, n_cols, width)
        u = jnp.concatenate([one_u, one_u], axis=1)
        y = (step_row - 1) * height - height // 2 + row_ref[t] + row_in
        v = 2.0 * (y.astype(F32) + 0.5) / (n_rows * height)
        store(t, term_1 + u * (term_u + u * term_uu + v * term_uv) + v * (term_v + v * term_vv))

    build(first, *buffers[0])
    some = 8

    def some_strips(i, carry):
        for j in range(some):
            t = first + some * i + j
            build(jnp.minimum(t + 1, last - 1), *buffers[(j + 1) % 2])
            multiply(t, *buffers[j % 2])
        return carry

    lax.fori_loop(0, (last - first) // some, some_strips, 0)


def store_model(models, first, strip_rows, t, model):
    for half in range(2):
        rows_of = pl.ds(pl.multiple_of((t - first) * strip_rows + half * ROWS, ROWS), ROWS)
        for dx in range(PHASES):
            models[rows_of, dx * LANES : (dx + 1) * LANES] = model[
                dx * ROWS : (dx + 1) * ROWS, half * LANES : (half + 1) * LANES
            ]


def strips_kernel(
    n_rows, n_cols, patch_ref, row_ref, set_ref, top_ref, near_rows, away_rows, here_ref, even_ref, odd_ref,
    table8_ref, table_ref, image, models, hi_a, lo_a, hi_b, lo_b,
):
    height = here_ref.shape[0]
    width = PHASES * LANES
    scatter = to_phases(width)
    rows = image.shape[3]
    upper = lax.axis_index("visit") % 2 == 0
    ahead = lax.axis_index("visit") % 4 < 2
    for b in range(4):
        cols = slice(b * width, min((b + 1) * width, here_ref.shape[1]))
        near, away, even, odd = [r[:, cols] for r in (near_rows, away_rows, even_ref, odd_ref)]
        pieces = (
            jnp.where(ahead, away, near),
            jnp.where(upper, odd, even),
            here_ref[:, cols],
            jnp.where(upper, even, odd),
            jnp.where(ahead, near, away),
        )
        parts = [split(piece) for piece in pieces]
        both = jnp.concatenate([hi for hi, _ in parts] + [lo for _, lo in parts], axis=0)
        moved = mxu(both, scatter[: cols.stop - cols.start])
        for f in range(PHASES):
            for part in range(2):
                some = moved[part * rows : (part + 1) * rows, f * LANES : (f + 1) * LANES]
                image[part, f, b] = some * SCALE if part else some

    strip_rows = models.shape[0] // (patch_ref.shape[0] - LATER)
    model_loop(
        n_rows, n_cols, height, patch_ref, row_ref, set_ref, top_ref, table8_ref, table_ref, image,
        ((hi_a, lo_a), (hi_b, lo_b)), 0, patch_ref.shape[0] - LATER,
        functools.partial(store_model, models, 0, strip_rows),
    )


def finish_kernel(
    n_rows, n_cols, height, patch_ref, row_ref, set_ref, top_ref, table8_ref, table_ref, image, models, strips_hbm, diff_hbm,
    strips_ref, rest, hi_a, lo_a, hi_b, lo_b, sems,
):
    n_strips, strip_rows, width = strips_ref.shape
    copy_strips = pltpu.make_async_copy(strips_hbm, strips_ref, sems.at[4])
    copy_strips.start()
    model_loop(
        n_rows, n_cols, height, patch_ref, row_ref, set_ref, top_ref, table8_ref, table_ref, image,
        ((hi_a, lo_a), (hi_b, lo_b)), n_strips - LATER, n_strips,
        functools.partial(store_model, rest, n_strips - LATER, strip_rows),
    )
    gather = from_phases()
    gather = jnp.concatenate([gather, gather], axis=0)
    copy_strips.wait()
    some = 16
    ready = models.shape[0]
    for c in range(n_strips // some):
        rows = slice(c * some * strip_rows, (c + 1) * some * strip_rows)
        found = models[rows] if rows.stop <= ready else jnp.concatenate([models[rows.start : ready], rest[...]], axis=0)
        natural = mxu(jnp.concatenate(split(found), axis=1), gather)
        part = pl.ds(c * some, some)
        strips_ref[part] = strips_ref[part] - natural.reshape(some, strip_rows, width)
        pltpu.make_async_copy(strips_ref.at[part], diff_hbm.at[part], sems.at[c]).start()
    for c in range(n_strips // some):
        part = pl.ds(c * some, some)
        pltpu.make_async_copy(strips_ref.at[part], diff_hbm.at[part], sems.at[c]).wait()


def coadd_kernel(
    n_rows, n_cols, flat_ref, image, mid_any, even_any, odd_any, coadd_ref,
    mid_ref, even_ref, odd_ref, taps, wide, models, hi_a, lo_a, hi_b, lo_b, sems,
):
    height, width = coadd_ref.shape
    sources = (mid_any, even_any, odd_any)
    targets = (mid_ref, even_ref, odd_ref)
    copies = [pltpu.make_async_copy(source, target, sems.at[i]) for i, (source, target) in enumerate(zip(sources, targets))]
    for copy in copies:
        copy.start()
    for copy in copies:
        copy.wait()
    count = mid_ref[0, height:, :] + even_ref[0, height:, :] + odd_ref[0, height:, :]
    n_sets = count.shape[0]
    v = 2.0 * ((iota(count.shape, 1) - height // 2).astype(F32) + 0.5) / (n_rows * height)

    def three(x, p):
        taps_of = flat_ref[p * n_sets : (p + 1) * n_sets, :]
        x_hi, t_hi = x.astype(BF16).astype(F32), taps_of.astype(BF16).astype(F32)
        return [(x_hi, t_hi), (x - x_hi, t_hi), (x_hi, taps_of - t_hi)]

    by_power = []
    for terms in ((0, 1, 5), (2, 4), (3,)):
        rows, x = [], count
        for p in terms:
            rows, x = rows + three(x, p), x * v
        sides = [jnp.concatenate(side, axis=0) for side in zip(*rows)]
        by_power.append(mxu(sides[0].T.astype(BF16), sides[1].astype(BF16)))
    for a in range(3):
        for c in range(TILES):
            taps[c, a * height : (a + 1) * height, :] = by_power[a][:, c * LANES : (c + 1) * LANES]
    n = 3 * height // ROWS
    for dy in range(ROWS):
        some = jnp.concatenate([taps[c, pl.ds(dy, n, stride=ROWS), :] for c in range(TILES)], axis=1)
        moved = some if dy == 0 else pltpu.roll(some, dy, 1)
        for c in range(TILES):
            wide[c, pl.ds(dy, n, stride=ROWS), :] = moved[:, c * LANES : (c + 1) * LANES]
    one_u = columns_of(1, n_cols, width)

    def build(b, data_hi, data_lo):
        fill(image, 0, height + b * ROWS + EDGE - HALF, 1, 1, BF16, data_hi)
        fill(image, 1, height + b * ROWS + EDGE - HALF, 1, 1, BF16, data_lo)

    def multiply(b, data_hi, data_lo):
        row = pl.multiple_of(b * ROWS, ROWS)
        fine_hi, fine_lo = split(on_phases(wide, row))
        rest = [on_phases(wide, a * height + row).astype(BF16) for a in (1, 2)]
        big = mxu(jnp.concatenate([fine_hi] + rest + [fine_lo], axis=0), data_hi[...])
        terms = big.reshape(4, PHASES * ROWS, LANES)
        small = mxu(fine_hi, data_lo[...]) * (1.0 / SCALE)
        model = terms[0] + terms[3] + small + one_u * (terms[1] + one_u * terms[2])
        for dx in range(PHASES):
            models[pl.ds(row, ROWS), dx * LANES : (dx + 1) * LANES] = model[dx * ROWS : (dx + 1) * ROWS]

    n_blocks = height // ROWS
    build(0, hi_a, lo_a)
    some = 8
    buffers = ((hi_a, lo_a), (hi_b, lo_b))

    def some_blocks(i, carry):
        for j in range(some):
            b = some * i + j
            build(jnp.minimum(b + 1, n_blocks - 1), *buffers[(j + 1) % 2])
            multiply(b, *buffers[j % 2])
        return carry

    lax.fori_loop(0, n_blocks // some, some_blocks, 0)
    gather = from_phases()
    gather = jnp.concatenate([gather, gather], axis=0)
    natural = mxu(jnp.concatenate(split(models[...]), axis=1), gather)
    for c in range(PHASES):
        total = mid_ref[c, 0:height, :] + even_ref[c, 0:height, :] + odd_ref[c, 0:height, :]
        coadd_ref[:, c * LANES : (c + 1) * LANES] = total - natural[:, c * LANES : (c + 1) * LANES]


def swap(x, axis, apart, first):
    size = lax.axis_size(axis)
    lower = [i for i in range(size - apart) if (i - first) % (2 * apart) < apart]
    pairs = [(i, i + apart) for i in lower] + [(i + apart, i) for i in lower]
    return lax.ppermute(x, axis, pairs)


def per_device(strips, patch_of, box_row, kernel_set, template, row_taps, col_taps, kernel_coef):
    n_rows, n_cols = lax.axis_size("visit"), lax.axis_size("det")
    n_strips, strip_rows, width = strips.shape
    height = template.shape[0]
    n_sets, n_terms, n_basis = kernel_coef.shape
    block = PHASES * ROWS
    smem = pl.BlockSpec(memory_space=pltpu.SMEM)
    vmem = pl.BlockSpec(memory_space=pltpu.VMEM)
    hbm = pl.BlockSpec(memory_space=pltpu.HBM)
    free = pl.BlockSpec(memory_space=pl.ANY)

    patch_of = patch_of.reshape(n_strips)

    v, d = lax.axis_index("visit"), lax.axis_index("det")
    first, last = template[:, :SIDE], template[:, width - SIDE :]
    ahead = d % 4 < 2
    even = swap(template, "det", 1, 0)
    odd = swap(template, "det", 1, 1)
    for_near, for_away = jnp.where(ahead, last, first), jnp.where(ahead, first, last)
    patch_of, for_near, for_away = lax.optimization_barrier((patch_of, for_near, for_away))
    near = swap(for_near, "det", 2, 0)
    away = swap(for_away, "det", 2, 2)

    sums = jax.ShapeDtypeStruct((3, PHASES, height + ROWS, LANES), F32)
    in_vmem = pltpu.VMEM(sums.shape, F32)
    for_even, mid, for_odd = pl.pallas_call(
        functools.partial(sums_kernel, n_cols),
        out_shape=(in_vmem, sums, in_vmem),
        in_specs=[smem] * 3 + [hbm],
        out_specs=(vmem,) * 3,
        scratch_shapes=[
            pltpu.VMEM(strips.shape, F32),
            pltpu.VMEM((9, PHASES, height + ROWS, LANES), F32),
            pltpu.SemaphoreType.DMA((4,)),
        ],
        compiler_params=pltpu.CompilerParams(vmem_limit_bytes=56 * MIB),
        cost_estimate=pl.CostEstimate(flops=3 << 30, bytes_accessed=5 << 20, transcendentals=0),
        name="strip_sums",
    )(patch_of, box_row, kernel_set, strips)

    far_left, far_right = jnp.where(ahead, away, near), jnp.where(ahead, near, away)
    left, right = jnp.where(d % 2 == 0, odd, even), jnp.where(d % 2 == 0, even, odd)
    blank = jnp.zeros((height, LANES - 2 * SIDE), F32)
    here = jnp.concatenate([far_left, left, template, right, far_right, blank], axis=1)

    for_even, for_odd, here = lax.optimization_barrier((for_even, for_odd, here))
    odd = swap(here, "visit", 1, 1)
    even = swap(here, "visit", 1, 0)
    first, last = here[:EDGE], here[height - EDGE :]
    ahead = v % 4 < 2
    near_rows = swap(jnp.where(ahead, last, first), "visit", 2, 0)
    away_rows = swap(jnp.where(ahead, first, last), "visit", 2, 2)

    for_odd, even, row_taps = lax.optimization_barrier((for_odd, even, row_taps))
    sum_even = swap(for_even, "det", 1, 0)
    sum_odd = swap(for_odd, "det", 1, 1)

    flat, table, table8, top = pl.pallas_call(
        functools.partial(taps_kernel, n_rows, n_cols),
        out_shape=(
            pltpu.VMEM((n_sets * n_terms, DEPTH), F32),
            pltpu.VMEM((n_sets, (n_terms + FINE) * block, DEPTH), BF16),
            pltpu.VMEM((n_sets, FINE * block, DEPTH), F8),
            pltpu.VMEM((ROWS, LANES), F32),
        ),
        in_specs=[vmem] * 3,
        out_specs=(vmem,) * 4,
        scratch_shapes=[pltpu.VMEM((TILES, n_sets * n_terms * ROWS, LANES), F32)],
        compiler_params=pltpu.CompilerParams(vmem_limit_bytes=56 * MIB),
        cost_estimate=pl.CostEstimate(flops=3 << 30, bytes_accessed=5 << 20, transcendentals=0),
        name="tap_tables",
    )(row_taps.T, col_taps.T, jnp.swapaxes(kernel_coef, 0, 1).reshape(n_terms * n_sets, n_basis))

    flat, table, table8, top = [
        pltpu.with_memory_space_constraint(x, pltpu.VMEM) for x in (flat, table, table8, top)
    ]

    even, odd, near_rows, away_rows, here = [
        pltpu.with_memory_space_constraint(x, pltpu.VMEM) for x in (even, odd, near_rows, away_rows, here)
    ]

    flops = n_strips * 2 * n_terms * block * DEPTH * 2 * LANES * 2
    buffers = [pltpu.VMEM((DEPTH, 2 * LANES), kind) for kind in (BF16, F8, BF16, F8)]
    image, models = pl.pallas_call(
        functools.partial(strips_kernel, n_rows, n_cols),
        out_shape=(
            pltpu.VMEM((2, PHASES, 4, 3 * height + 2 * EDGE, LANES), F32),
            pltpu.VMEM(((n_strips - LATER) * strip_rows, width), F32),
        ),
        in_specs=[smem] * 3 + [vmem] * 8,
        out_specs=(vmem, vmem),
        scratch_shapes=buffers,
        compiler_params=pltpu.CompilerParams(vmem_limit_bytes=32 * MIB),
        cost_estimate=pl.CostEstimate(flops=flops, bytes_accessed=14 << 20, transcendentals=0),
        name="strip_models",
    )(patch_of, box_row, kernel_set, top, near_rows, away_rows, here, even, odd, table8, table)

    image, models, sum_even, sum_odd = lax.optimization_barrier((image, models, sum_even, sum_odd))
    mid = mid + sum_even + sum_odd
    image, models = [pltpu.with_memory_space_constraint(x, pltpu.VMEM) for x in (image, models)]
    from_even = swap(jnp.where(v % 2 == 0, mid[2], mid[0]), "visit", 1, 0)
    from_odd = swap(jnp.where(v % 2 == 0, mid[0], mid[2]), "visit", 1, 1)

    patch_of, mid = lax.optimization_barrier((patch_of, mid))
    difference = pl.pallas_call(
        functools.partial(finish_kernel, n_rows, n_cols, height),
        out_shape=jax.ShapeDtypeStruct(strips.shape, F32),
        in_specs=[smem] * 3 + [vmem] * 5 + [hbm],
        out_specs=hbm,
        scratch_shapes=[pltpu.VMEM(strips.shape, F32), pltpu.VMEM((LATER * strip_rows, width), F32)]
        + buffers
        + [pltpu.SemaphoreType.DMA((5,))],
        compiler_params=pltpu.CompilerParams(vmem_limit_bytes=32 * MIB),
        cost_estimate=pl.CostEstimate(flops=flops // 4, bytes_accessed=4 << 20, transcendentals=0),
        name="finish",
    )(patch_of, box_row, kernel_set, top, table8, table, image, models, strips)

    coadd = pl.pallas_call(
        functools.partial(coadd_kernel, n_rows, n_cols),
        out_shape=jax.ShapeDtypeStruct(template.shape, F32),
        in_specs=[vmem, vmem] + [free] * 3,
        out_specs=vmem,
        scratch_shapes=[pltpu.VMEM(x.shape, F32) for x in (from_even, from_even, from_odd)]
        + [
            pltpu.VMEM((TILES, 3 * height, LANES), F32),
            pltpu.VMEM((TILES, 3 * height, LANES), F32),
            pltpu.VMEM((height, PHASES * LANES), F32),
        ]
        + [pltpu.VMEM((DEPTH, LANES), BF16)] * 4
        + [pltpu.SemaphoreType.DMA((3,))],
        compiler_params=pltpu.CompilerParams(vmem_limit_bytes=32 * MIB),
        cost_estimate=pl.CostEstimate(flops=6 << 30, bytes_accessed=3 << 20, transcendentals=0),
        name="coadd_models",
    )(flat, image, mid[1], from_even, from_odd)
    return difference, coadd


def solution(mesh):
    tiles = ("visit", "det")
    in_specs = (P(tiles, None, None), P(tiles, None), P(tiles), P(tiles), P("visit", "det"), P(), P(), P())
    out_specs = (P(tiles, None, None), P("visit", "det"))
    return jax.shard_map(per_device, mesh=mesh, in_specs=in_specs, out_specs=out_specs, check_vma=False)
```

```python
import functools

import jax
import jax.numpy as jnp
from jax import lax
from jax.experimental import pallas as pl
from jax.experimental.pallas import tpu as pltpu
from jax.sharding import PartitionSpec as P

F32 = jnp.float32
BF16 = jnp.bfloat16
F8 = jnp.float8_e4m3fn
HIGHEST = lax.Precision.HIGHEST

HALF = 10
SIDE = 12
EDGE = 16
PHASES = 4
LANES = 128
ROWS = 8
WIN = 32
SHIFTS = 24
DEPTH = SHIFTS * WIN
TILES = DEPTH // LANES
LATER = 8
FINE = 3
SCALE = 2.0**14
TOP = 256.0
MIB = 1024 * 1024


def iota(shape, dim):
    return lax.broadcasted_iota(jnp.int32, shape, dim)


def split(x):
    hi = x.astype(BF16)
    lo = (x - hi.astype(F32)).astype(BF16)
    return hi, lo


def mxu(a, b):
    return jnp.dot(a, b, preferred_element_type=F32)


def exact(a, b):
    return jnp.dot(a, b, precision=HIGHEST, preferred_element_type=F32)


def to_phases(width):
    out = iota((width, PHASES * LANES), 1)
    source = (out % LANES) * PHASES + out // LANES
    return jnp.where(iota((width, PHASES * LANES), 0) == source, 1.0, 0.0).astype(BF16)


def from_phases():
    src = iota((PHASES * LANES, PHASES * LANES), 0)
    target = (src % LANES) * PHASES + src // LANES
    return jnp.where(iota((PHASES * LANES, PHASES * LANES), 1) == target, 1.0, 0.0).astype(BF16)


def place(patch, n_cols):
    step_row = (patch >> (n_cols.bit_length() - 1)) - lax.axis_index("visit") + 1
    step_col = (patch & (n_cols - 1)) - lax.axis_index("det") + 1
    return step_row, step_col


def sums_kernel(n_cols, patch_ref, row_ref, set_ref, strips_hbm, even_ref, mid_ref, odd_ref, strips_ref, acc, sems):
    n_strips, strip_rows, _ = strips_ref.shape
    n_parts = 4
    some = n_strips // n_parts
    copies = []
    for i in range(n_parts):
        part = pl.ds(i * some, some)
        copies.append(pltpu.make_async_copy(strips_hbm.at[part], strips_ref.at[part], sems.at[i]))
        copies[i].start()
    acc[...] = jnp.zeros(acc.shape, F32)
    height = acc.shape[2] - ROWS
    place_lane = iota((ROWS, LANES), 1)
    place_sub = iota((ROWS, LANES), 0)

    def one_strip(t, carry):
        step_row, step_col = place(patch_ref[t], n_cols)
        top = row_ref[t]
        q = step_col * 3 + step_row
        for c in range(PHASES):
            acc[q, c, pl.ds(top, strip_rows), :] += strips_ref[t, :, c * LANES : (c + 1) * LANES]
        hit = (place_sub == set_ref[t]) & (place_lane >= top) & (place_lane < top + strip_rows)
        acc[q, 0, height:, :] += jnp.where(hit, 1.0, 0.0)
        return carry

    for i in range(n_parts):
        copies[i].wait()
        lax.fori_loop(i * some, (i + 1) * some, one_strip, 0, unroll=4)
    parity = lax.axis_index("det") % 2
    for first, out in ((6 - 6 * parity, even_ref), (3, mid_ref), (6 * parity, odd_ref)):
        out[...] = acc[pl.ds(first, 3)]


def taps_kernel(
    n_rows, n_cols, row_taps_ref, col_taps_ref, coef_ref, flat_ref, table_ref, table8_ref, top_ref, wide
):
    taps = row_taps_ref.shape[0]
    lane = iota((taps, DEPTH), 1)
    sub = iota((taps, DEPTH), 0)
    row_part = exact(row_taps_ref[...].T, jnp.where(lane % WIN == sub, 1.0, 0.0))
    col_part = exact(col_taps_ref[...].T, jnp.where(lane // WIN == sub, 1.0, 0.0))
    n_sets = table_ref.shape[0]
    one, u, v, uu, uv, vv = [coef_ref[p * n_sets : (p + 1) * n_sets, :] for p in range(6)]
    u0 = (2 * lax.axis_index("det") + 1).astype(F32) / n_cols - 1.0
    v0 = (2 * lax.axis_index("visit") + 1).astype(F32) / n_rows - 1.0
    one, u, v = (
        one + u0 * (u + u0 * uu) + v0 * (v + u0 * uv + v0 * vv),
        u + 2.0 * u0 * uu + v0 * uv,
        v + u0 * uv + 2.0 * v0 * vv,
    )
    flat = exact(jnp.concatenate([one, v, u, uu, uv, vv], axis=0), row_part * col_part)
    flat_ref[...] = flat
    top = jnp.maximum(jnp.max(jnp.max(jnp.abs(flat), axis=1, keepdims=True), axis=0, keepdims=True), 1e-30)
    top_ref[...] = jnp.broadcast_to(top, top_ref.shape)
    scale = TOP / top
    n = flat.shape[0]
    block = PHASES * ROWS
    for dy in range(ROWS):
        moved = flat if dy == 0 else pltpu.roll(flat, dy, 1)
        for c in range(TILES):
            wide[c, pl.ds(dy, n, stride=ROWS), :] = moved[:, c * LANES : (c + 1) * LANES]
    for s in range(n_sets):
        for p in range(6):
            rows = on_phases(wide, (p * n_sets + s) * ROWS)
            hi = rows.astype(BF16)
            table_ref[s, p * block : (p + 1) * block, :] = hi
            if p < FINE:
                table_ref[s, (6 + p) * block : (7 + p) * block, :] = (rows - hi.astype(F32)).astype(BF16)
                table8_ref[s, p * block : (p + 1) * block, :] = (rows * scale).astype(F8)


def on_phases(wide, first):
    rows = jnp.concatenate([wide[c, pl.ds(first, ROWS), :] for c in range(TILES)], axis=1)
    return jnp.concatenate([rows] + [pltpu.roll(rows, dx * WIN, 1) for dx in range(1, PHASES)], axis=0)


def columns_of(step_col, n_cols, width):
    shape = (PHASES * ROWS, LANES)
    col = (step_col - 1) * width - width // 2 + iota(shape, 1) * PHASES + iota(shape, 0) // ROWS
    return 2.0 * (col.astype(F32) + 0.5) / (n_cols * width)


def fill(image_ref, part, row, col, halves, kind, data):
    lane = iota((WIN, LANES), 1)
    for phase in range(PHASES):
        near, far = [image_ref[part, phase, col + i, pl.ds(row, WIN + (halves - 1) * ROWS), :] for i in range(2)]
        for half in range(halves):
            rows = slice(half * ROWS, half * ROWS + WIN)
            a, b = near[rows].astype(kind), far[rows].astype(kind)
            for shift in range((SIDE - HALF + SHIFTS - 1) // PHASES + 1):
                k = shift * PHASES + phase - (SIDE - HALF)
                if 0 <= k < SHIFTS:
                    moved = a if shift == 0 else pltpu.roll(jnp.where(lane < shift, b, a), LANES - shift, 1)
                    data[k * WIN : (k + 1) * WIN, half * LANES : (half + 1) * LANES] = moved


def model_loop(
    n_rows, n_cols, height, patch_ref, row_ref, set_ref, top_ref, table8_ref, table_ref, image, buffers, first, last, store
):
    width = PHASES * LANES
    block = PHASES * ROWS
    fine = FINE * block
    shape = (block, 2 * LANES)
    row_in = iota(shape, 0) % ROWS + iota(shape, 1) // LANES * ROWS
    undo = top_ref[0:1, 0:1] * (1.0 / (TOP * SCALE))

    def build(t, data_hi, data_lo):
        step_row, step_col = place(patch_ref[t], n_cols)
        row = step_row * height + row_ref[t] + EDGE - HALF
        fill(image, 0, row, step_col, 2, BF16, data_hi)
        fill(image, 1, row, step_col, 2, F8, data_lo)

    def multiply(t, data_hi, data_lo):
        step_row, step_col = place(patch_ref[t], n_cols)
        which = set_ref[t]
        big = mxu(table_ref[which], data_hi[...])
        small = mxu(table8_ref[which], data_lo[...])
        exact_terms = big[:fine] + big[6 * block :] + small * undo
        term_1, term_v, term_u = [exact_terms[p * block : (p + 1) * block] for p in range(FINE)]
        term_uu, term_uv, term_vv = [big[p * block : (p + 1) * block] for p in range(FINE, 6)]
        one_u = columns_of(step_col, n_cols, width)
        u = jnp.concatenate([one_u, one_u], axis=1)
        y = (step_row - 1) * height - height // 2 + row_ref[t] + row_in
        v = 2.0 * (y.astype(F32) + 0.5) / (n_rows * height)
        store(t, term_1 + u * (term_u + u * term_uu + v * term_uv) + v * (term_v + v * term_vv))

    build(first, *buffers[0])
    n = last - first
    some = next(k for k in (14, 8, 4) if n % k == 0)

    def some_strips(i, carry):
        for j in range(some):
            t = first + some * i + j
            build(jnp.minimum(t + 1, last - 1), *buffers[(j + 1) % 2])
            multiply(t, *buffers[j % 2])
        return carry

    lax.fori_loop(0, n // some, some_strips, 0)


def store_model(models, first, strip_rows, t, model):
    for half in range(2):
        rows_of = pl.ds(pl.multiple_of((t - first) * strip_rows + half * ROWS, ROWS), ROWS)
        for dx in range(PHASES):
            models[rows_of, dx * LANES : (dx + 1) * LANES] = model[
                dx * ROWS : (dx + 1) * ROWS, half * LANES : (half + 1) * LANES
            ]


def strips_kernel(
    n_rows, n_cols, patch_ref, row_ref, set_ref, top_ref, near_rows, away_rows, here_ref, even_ref, odd_ref,
    table8_ref, table_ref, image, models, hi_a, lo_a, hi_b, lo_b,
):
    height = here_ref.shape[0]
    width = PHASES * LANES
    scatter = to_phases(width)
    rows = image.shape[3]
    upper = lax.axis_index("visit") % 2 == 0
    ahead = lax.axis_index("visit") % 4 < 2
    for b in range(4):
        cols = slice(b * width, min((b + 1) * width, here_ref.shape[1]))
        near, away, even, odd = [r[:, cols] for r in (near_rows, away_rows, even_ref, odd_ref)]
        pieces = (
            jnp.where(ahead, away, near),
            jnp.where(upper, odd, even),
            here_ref[:, cols],
            jnp.where(upper, even, odd),
            jnp.where(ahead, near, away),
        )
        parts = [split(piece) for piece in pieces]
        both = jnp.concatenate([hi for hi, _ in parts] + [lo for _, lo in parts], axis=0)
        moved = mxu(both, scatter[: cols.stop - cols.start])
        for f in range(PHASES):
            for part in range(2):
                some = moved[part * rows : (part + 1) * rows, f * LANES : (f + 1) * LANES]
                image[part, f, b] = some * SCALE if part else some

    strip_rows = models.shape[0] // (patch_ref.shape[0] - LATER)
    model_loop(
        n_rows, n_cols, height, patch_ref, row_ref, set_ref, top_ref, table8_ref, table_ref, image,
        ((hi_a, lo_a), (hi_b, lo_b)), 0, patch_ref.shape[0] - LATER,
        functools.partial(store_model, models, 0, strip_rows),
    )


def finish_kernel(
    n_rows, n_cols, height, patch_ref, row_ref, set_ref, top_ref, table8_ref, table_ref, image, models, strips_hbm, diff_hbm,
    strips_ref, rest, hi_a, lo_a, hi_b, lo_b, sems,
):
    n_strips, strip_rows, width = strips_ref.shape
    copy_strips = pltpu.make_async_copy(strips_hbm, strips_ref, sems.at[4])
    copy_strips.start()
    model_loop(
        n_rows, n_cols, height, patch_ref, row_ref, set_ref, top_ref, table8_ref, table_ref, image,
        ((hi_a, lo_a), (hi_b, lo_b)), n_strips - LATER, n_strips,
        functools.partial(store_model, rest, n_strips - LATER, strip_rows),
    )
    gather = from_phases()
    gather = jnp.concatenate([gather, gather], axis=0)
    copy_strips.wait()
    some = 16
    ready = models.shape[0]
    for c in range(n_strips // some):
        rows = slice(c * some * strip_rows, (c + 1) * some * strip_rows)
        found = models[rows] if rows.stop <= ready else jnp.concatenate([models[rows.start : ready], rest[...]], axis=0)
        natural = mxu(jnp.concatenate(split(found), axis=1), gather)
        part = pl.ds(c * some, some)
        strips_ref[part] = strips_ref[part] - natural.reshape(some, strip_rows, width)
        pltpu.make_async_copy(strips_ref.at[part], diff_hbm.at[part], sems.at[c]).start()
    for c in range(n_strips // some):
        part = pl.ds(c * some, some)
        pltpu.make_async_copy(strips_ref.at[part], diff_hbm.at[part], sems.at[c]).wait()


def coadd_kernel(
    n_rows, n_cols, flat_ref, image, mid_any, even_any, odd_any, coadd_ref,
    mid_ref, even_ref, odd_ref, taps, wide, models, hi_a, lo_a, hi_b, lo_b, sems,
):
    height, width = coadd_ref.shape
    sources = (mid_any, even_any, odd_any)
    targets = (mid_ref, even_ref, odd_ref)
    copies = [pltpu.make_async_copy(source, target, sems.at[i]) for i, (source, target) in enumerate(zip(sources, targets))]
    for copy in copies:
        copy.start()
    for copy in copies:
        copy.wait()
    count = mid_ref[0, height:, :] + even_ref[0, height:, :] + odd_ref[0, height:, :]
    n_sets = count.shape[0]
    v = 2.0 * ((iota(count.shape, 1) - height // 2).astype(F32) + 0.5) / (n_rows * height)

    def three(x, p):
        taps_of = flat_ref[p * n_sets : (p + 1) * n_sets, :]
        x_hi, t_hi = x.astype(BF16).astype(F32), taps_of.astype(BF16).astype(F32)
        return [(x_hi, t_hi), (x - x_hi, t_hi), (x_hi, taps_of - t_hi)]

    by_power = []
    for terms in ((0, 1, 5), (2, 4), (3,)):
        rows, x = [], count
        for p in terms:
            rows, x = rows + three(x, p), x * v
        sides = [jnp.concatenate(side, axis=0) for side in zip(*rows)]
        by_power.append(mxu(sides[0].T.astype(BF16), sides[1].astype(BF16)))
    for a in range(3):
        for c in range(TILES):
            taps[c, a * height : (a + 1) * height, :] = by_power[a][:, c * LANES : (c + 1) * LANES]
    n = 3 * height // ROWS
    for dy in range(ROWS):
        some = jnp.concatenate([taps[c, pl.ds(dy, n, stride=ROWS), :] for c in range(TILES)], axis=1)
        moved = some if dy == 0 else pltpu.roll(some, dy, 1)
        for c in range(TILES):
            wide[c, pl.ds(dy, n, stride=ROWS), :] = moved[:, c * LANES : (c + 1) * LANES]
    one_u = columns_of(1, n_cols, width)

    def build(b, data_hi, data_lo):
        fill(image, 0, height + b * ROWS + EDGE - HALF, 1, 1, BF16, data_hi)
        fill(image, 1, height + b * ROWS + EDGE - HALF, 1, 1, BF16, data_lo)

    def multiply(b, data_hi, data_lo):
        row = pl.multiple_of(b * ROWS, ROWS)
        fine_hi, fine_lo = split(on_phases(wide, row))
        rest = [on_phases(wide, a * height + row).astype(BF16) for a in (1, 2)]
        big = mxu(jnp.concatenate([fine_hi] + rest + [fine_lo], axis=0), data_hi[...])
        terms = big.reshape(4, PHASES * ROWS, LANES)
        small = mxu(fine_hi, data_lo[...]) * (1.0 / SCALE)
        model = terms[0] + terms[3] + small + one_u * (terms[1] + one_u * terms[2])
        for dx in range(PHASES):
            models[pl.ds(row, ROWS), dx * LANES : (dx + 1) * LANES] = model[dx * ROWS : (dx + 1) * ROWS]

    n_blocks = height // ROWS
    build(0, hi_a, lo_a)
    some = n_blocks
    buffers = ((hi_a, lo_a), (hi_b, lo_b))

    def some_blocks(i, carry):
        for j in range(some):
            b = some * i + j
            build(jnp.minimum(b + 1, n_blocks - 1), *buffers[(j + 1) % 2])
            multiply(b, *buffers[j % 2])
        return carry

    lax.fori_loop(0, n_blocks // some, some_blocks, 0)
    gather = from_phases()
    gather = jnp.concatenate([gather, gather], axis=0)
    natural = mxu(jnp.concatenate(split(models[...]), axis=1), gather)
    for c in range(PHASES):
        total = mid_ref[c, 0:height, :] + even_ref[c, 0:height, :] + odd_ref[c, 0:height, :]
        coadd_ref[:, c * LANES : (c + 1) * LANES] = total - natural[:, c * LANES : (c + 1) * LANES]


def swap(x, axis, apart, first):
    size = lax.axis_size(axis)
    lower = [i for i in range(size - apart) if (i - first) % (2 * apart) < apart]
    pairs = [(i, i + apart) for i in lower] + [(i + apart, i) for i in lower]
    return lax.ppermute(x, axis, pairs)


def per_device(strips, patch_of, box_row, kernel_set, template, row_taps, col_taps, kernel_coef):
    n_rows, n_cols = lax.axis_size("visit"), lax.axis_size("det")
    n_strips, strip_rows, width = strips.shape
    height = template.shape[0]
    n_sets, n_terms, n_basis = kernel_coef.shape
    block = PHASES * ROWS
    smem = pl.BlockSpec(memory_space=pltpu.SMEM)
    vmem = pl.BlockSpec(memory_space=pltpu.VMEM)
    hbm = pl.BlockSpec(memory_space=pltpu.HBM)
    free = pl.BlockSpec(memory_space=pl.ANY)

    patch_of = patch_of.reshape(n_strips)

    v, d = lax.axis_index("visit"), lax.axis_index("det")
    first, last = template[:, :SIDE], template[:, width - SIDE :]
    ahead = d % 4 < 2
    even = swap(template, "det", 1, 0)
    odd = swap(template, "det", 1, 1)
    for_near, for_away = jnp.where(ahead, last, first), jnp.where(ahead, first, last)
    patch_of, for_near, for_away = lax.optimization_barrier((patch_of, for_near, for_away))
    near = swap(for_near, "det", 2, 0)
    away = swap(for_away, "det", 2, 2)

    sums = jax.ShapeDtypeStruct((3, PHASES, height + ROWS, LANES), F32)
    for_even, mid, for_odd = pl.pallas_call(
        functools.partial(sums_kernel, n_cols),
        out_shape=(sums, sums, sums),
        in_specs=[smem] * 3 + [hbm],
        out_specs=(vmem,) * 3,
        scratch_shapes=[
            pltpu.VMEM(strips.shape, F32),
            pltpu.VMEM((9, PHASES, height + ROWS, LANES), F32),
            pltpu.SemaphoreType.DMA((4,)),
        ],
        compiler_params=pltpu.CompilerParams(vmem_limit_bytes=56 * MIB),
        cost_estimate=pl.CostEstimate(flops=3 << 30, bytes_accessed=5 << 20, transcendentals=0),
        name="strip_sums",
    )(patch_of, box_row, kernel_set, strips)

    far_left, far_right = jnp.where(ahead, away, near), jnp.where(ahead, near, away)
    left, right = jnp.where(d % 2 == 0, odd, even), jnp.where(d % 2 == 0, even, odd)
    blank = jnp.zeros((height, LANES - 2 * SIDE), F32)
    here = jnp.concatenate([far_left, left, template, right, far_right, blank], axis=1)

    for_even, for_odd, here = lax.optimization_barrier((for_even, for_odd, here))
    odd = swap(here, "visit", 1, 1)
    even = swap(here, "visit", 1, 0)
    first, last = here[:EDGE], here[height - EDGE :]
    ahead = v % 4 < 2
    for_near, for_away = jnp.where(ahead, last, first), jnp.where(ahead, first, last)
    for_near, for_away, even, row_taps = lax.optimization_barrier((for_near, for_away, even, row_taps))
    near_rows = swap(for_near, "visit", 2, 0)
    away_rows = swap(for_away, "visit", 2, 2)

    sum_even = swap(for_even, "det", 1, 0)
    sum_odd = swap(for_odd, "det", 1, 1)

    flat, table, table8, top = pl.pallas_call(
        functools.partial(taps_kernel, n_rows, n_cols),
        out_shape=(
            pltpu.VMEM((n_sets * n_terms, DEPTH), F32),
            pltpu.VMEM((n_sets, (n_terms + FINE) * block, DEPTH), BF16),
            pltpu.VMEM((n_sets, FINE * block, DEPTH), F8),
            pltpu.VMEM((ROWS, LANES), F32),
        ),
        in_specs=[vmem] * 3,
        out_specs=(vmem,) * 4,
        scratch_shapes=[pltpu.VMEM((TILES, n_sets * n_terms * ROWS, LANES), F32)],
        compiler_params=pltpu.CompilerParams(vmem_limit_bytes=56 * MIB),
        cost_estimate=pl.CostEstimate(flops=3 << 30, bytes_accessed=5 << 20, transcendentals=0),
        name="tap_tables",
    )(row_taps.T, col_taps.T, jnp.swapaxes(kernel_coef, 0, 1).reshape(n_terms * n_sets, n_basis))

    flat, table, table8, top = [
        pltpu.with_memory_space_constraint(x, pltpu.VMEM) for x in (flat, table, table8, top)
    ]

    even, odd, near_rows, away_rows, here = [
        pltpu.with_memory_space_constraint(x, pltpu.VMEM) for x in (even, odd, near_rows, away_rows, here)
    ]

    flops = n_strips * 2 * n_terms * block * DEPTH * 2 * LANES * 2
    buffers = [pltpu.VMEM((DEPTH, 2 * LANES), kind) for kind in (BF16, F8, BF16, F8)]
    image, models = pl.pallas_call(
        functools.partial(strips_kernel, n_rows, n_cols),
        out_shape=(
            pltpu.VMEM((2, PHASES, 4, 3 * height + 2 * EDGE, LANES), F32),
            pltpu.VMEM(((n_strips - LATER) * strip_rows, width), F32),
        ),
        in_specs=[smem] * 3 + [vmem] * 8,
        out_specs=(vmem, vmem),
        scratch_shapes=buffers,
        compiler_params=pltpu.CompilerParams(vmem_limit_bytes=32 * MIB),
        cost_estimate=pl.CostEstimate(flops=flops, bytes_accessed=14 << 20, transcendentals=0),
        name="strip_models",
    )(patch_of, box_row, kernel_set, top, near_rows, away_rows, here, even, odd, table8, table)

    image, models, sum_even, sum_odd = lax.optimization_barrier((image, models, sum_even, sum_odd))
    mid = mid + sum_even + sum_odd
    image, models = [pltpu.with_memory_space_constraint(x, pltpu.VMEM) for x in (image, models)]
    from_even = swap(jnp.where(v % 2 == 0, mid[2], mid[0]), "visit", 1, 0)
    from_odd = swap(jnp.where(v % 2 == 0, mid[0], mid[2]), "visit", 1, 1)

    patch_of, mid = lax.optimization_barrier((patch_of, mid))
    difference = pl.pallas_call(
        functools.partial(finish_kernel, n_rows, n_cols, height),
        out_shape=jax.ShapeDtypeStruct(strips.shape, F32),
        in_specs=[smem] * 3 + [vmem] * 5 + [hbm],
        out_specs=hbm,
        scratch_shapes=[pltpu.VMEM(strips.shape, F32), pltpu.VMEM((LATER * strip_rows, width), F32)]
        + buffers
        + [pltpu.SemaphoreType.DMA((5,))],
        compiler_params=pltpu.CompilerParams(vmem_limit_bytes=32 * MIB),
        cost_estimate=pl.CostEstimate(flops=flops // 4, bytes_accessed=4 << 20, transcendentals=0),
        name="finish",
    )(patch_of, box_row, kernel_set, top, table8, table, image, models, strips)

    coadd = pl.pallas_call(
        functools.partial(coadd_kernel, n_rows, n_cols),
        out_shape=jax.ShapeDtypeStruct(template.shape, F32),
        in_specs=[vmem, vmem] + [free] * 3,
        out_specs=vmem,
        scratch_shapes=[pltpu.VMEM(x.shape, F32) for x in (from_even, from_even, from_odd)]
        + [
            pltpu.VMEM((TILES, 3 * height, LANES), F32),
            pltpu.VMEM((TILES, 3 * height, LANES), F32),
            pltpu.VMEM((height, PHASES * LANES), F32),
        ]
        + [pltpu.VMEM((DEPTH, LANES), BF16)] * 4
        + [pltpu.SemaphoreType.DMA((3,))],
        compiler_params=pltpu.CompilerParams(vmem_limit_bytes=32 * MIB),
        cost_estimate=pl.CostEstimate(flops=6 << 30, bytes_accessed=3 << 20, transcendentals=0),
        name="coadd_models",
    )(flat, image, mid[1], from_even, from_odd)
    return difference, coadd


def solution(mesh):
    tiles = ("visit", "det")
    in_specs = (P(tiles, None, None), P(tiles, None), P(tiles), P(tiles), P("visit", "det"), P(), P(), P())
    out_specs = (P(tiles, None, None), P("visit", "det"))
    return jax.shard_map(per_device, mesh=mesh, in_specs=in_specs, out_specs=out_specs, check_vma=False)
```

```python
import functools

import jax
import jax.numpy as jnp
from jax import lax
from jax.experimental import pallas as pl
from jax.experimental.pallas import tpu as pltpu
from jax.sharding import PartitionSpec as P

F32 = jnp.float32
BF16 = jnp.bfloat16
F8 = jnp.float8_e4m3fn
HIGHEST = lax.Precision.HIGHEST

HALF = 10
SIDE = 12
EDGE = 16
PHASES = 4
LANES = 128
ROWS = 8
WIN = 32
SHIFTS = 24
DEPTH = SHIFTS * WIN
TILES = DEPTH // LANES
LATER = 8
FINE = 3
SCALE = 2.0**14
TOP = 256.0
MIB = 1024 * 1024


def iota(shape, dim):
    return lax.broadcasted_iota(jnp.int32, shape, dim)


def split(x):
    hi = x.astype(BF16)
    lo = (x - hi.astype(F32)).astype(BF16)
    return hi, lo


def mxu(a, b):
    return jnp.dot(a, b, preferred_element_type=F32)


def exact(a, b):
    return jnp.dot(a, b, precision=HIGHEST, preferred_element_type=F32)


def to_phases(width):
    out = iota((width, PHASES * LANES), 1)
    source = (out % LANES) * PHASES + out // LANES
    return jnp.where(iota((width, PHASES * LANES), 0) == source, 1.0, 0.0).astype(BF16)


def from_phases():
    src = iota((PHASES * LANES, PHASES * LANES), 0)
    target = (src % LANES) * PHASES + src // LANES
    return jnp.where(iota((PHASES * LANES, PHASES * LANES), 1) == target, 1.0, 0.0).astype(BF16)


def place(patch, n_cols):
    step_row = (patch >> (n_cols.bit_length() - 1)) - lax.axis_index("visit") + 1
    step_col = (patch & (n_cols - 1)) - lax.axis_index("det") + 1
    return step_row, step_col


def sums_kernel(n_cols, patch_ref, row_ref, set_ref, strips_hbm, even_hbm, mid_ref, odd_hbm, strips_ref, acc, sems):
    n_strips, strip_rows, _ = strips_ref.shape
    n_parts = 4
    some = n_strips // n_parts
    inputs = []
    for i in range(n_parts):
        part = pl.ds(i * some, some)
        inputs.append(pltpu.make_async_copy(strips_hbm.at[part], strips_ref.at[part], sems.at[2 + i]))
        inputs[i].start()
    acc[...] = jnp.zeros(acc.shape, F32)
    height = acc.shape[2] - ROWS
    place_lane = iota((ROWS, LANES), 1)
    place_sub = iota((ROWS, LANES), 0)

    def one_strip(t, carry):
        step_row, step_col = place(patch_ref[t], n_cols)
        top = row_ref[t]
        q = step_col * 3 + step_row
        for c in range(PHASES):
            acc[q, c, pl.ds(top, strip_rows), :] += strips_ref[t, :, c * LANES : (c + 1) * LANES]
        hit = (place_sub == set_ref[t]) & (place_lane >= top) & (place_lane < top + strip_rows)
        acc[q, 0, height:, :] += jnp.where(hit, 1.0, 0.0)
        return carry

    for i in range(n_parts):
        inputs[i].wait()
        lax.fori_loop(i * some, (i + 1) * some, one_strip, 0, unroll=8)
    parity = lax.axis_index("det") % 2
    copies = [
        pltpu.make_async_copy(acc.at[pl.ds(first, 3)], out, sems.at[i])
        for i, (first, out) in enumerate(((6 - 6 * parity, even_hbm), (6 * parity, odd_hbm)))
    ]
    for copy in copies:
        copy.start()
    mid_ref[...] = acc[3:6]
    for copy in copies:
        copy.wait()


def taps_kernel(
    n_rows, n_cols, row_taps_ref, col_taps_ref, coef_ref, flat_ref, table_ref, table8_ref, top_ref, wide
):
    taps = row_taps_ref.shape[0]
    lane = iota((taps, DEPTH), 1)
    sub = iota((taps, DEPTH), 0)
    row_part = exact(row_taps_ref[...].T, jnp.where(lane % WIN == sub, 1.0, 0.0))
    col_part = exact(col_taps_ref[...].T, jnp.where(lane // WIN == sub, 1.0, 0.0))
    n_sets = table_ref.shape[0]
    one, u, v, uu, uv, vv = [coef_ref[p * n_sets : (p + 1) * n_sets, :] for p in range(6)]
    u0 = (2 * lax.axis_index("det") + 1).astype(F32) / n_cols - 1.0
    v0 = (2 * lax.axis_index("visit") + 1).astype(F32) / n_rows - 1.0
    one, u, v = (
        one + u0 * (u + u0 * uu) + v0 * (v + u0 * uv + v0 * vv),
        u + 2.0 * u0 * uu + v0 * uv,
        v + u0 * uv + 2.0 * v0 * vv,
    )
    flat = exact(jnp.concatenate([one, v, u, uu, uv, vv], axis=0), row_part * col_part)
    flat_ref[...] = flat
    top = jnp.maximum(jnp.max(jnp.max(jnp.abs(flat), axis=1, keepdims=True), axis=0, keepdims=True), 1e-30)
    top_ref[...] = jnp.broadcast_to(top, top_ref.shape)
    scale = TOP / top
    n = flat.shape[0]
    block = PHASES * ROWS
    for dy in range(ROWS):
        moved = flat if dy == 0 else pltpu.roll(flat, dy, 1)
        for c in range(TILES):
            wide[c, pl.ds(dy, n, stride=ROWS), :] = moved[:, c * LANES : (c + 1) * LANES]
    for s in range(n_sets):
        for p in range(6):
            rows = on_phases(wide, (p * n_sets + s) * ROWS)
            hi = rows.astype(BF16)
            table_ref[s, p * block : (p + 1) * block, :] = hi
            if p < FINE:
                table_ref[s, (6 + p) * block : (7 + p) * block, :] = (rows - hi.astype(F32)).astype(BF16)
                table8_ref[s, p * block : (p + 1) * block, :] = (rows * scale).astype(F8)


def on_phases(wide, first):
    rows = jnp.concatenate([wide[c, pl.ds(first, ROWS), :] for c in range(TILES)], axis=1)
    return jnp.concatenate([rows] + [pltpu.roll(rows, dx * WIN, 1) for dx in range(1, PHASES)], axis=0)


def columns_of(step_col, n_cols, width):
    shape = (PHASES * ROWS, LANES)
    col = (step_col - 1) * width - width // 2 + iota(shape, 1) * PHASES + iota(shape, 0) // ROWS
    return 2.0 * (col.astype(F32) + 0.5) / (n_cols * width)


def fill(image_ref, part, row, col, halves, kind, data):
    lane = iota((WIN, LANES), 1)
    for phase in range(PHASES):
        near, far = [image_ref[part, phase, col + i, pl.ds(row, WIN + (halves - 1) * ROWS), :] for i in range(2)]
        for half in range(halves):
            rows = slice(half * ROWS, half * ROWS + WIN)
            a, b = near[rows].astype(kind), far[rows].astype(kind)
            for shift in range((SIDE - HALF + SHIFTS - 1) // PHASES + 1):
                k = shift * PHASES + phase - (SIDE - HALF)
                if 0 <= k < SHIFTS:
                    moved = a if shift == 0 else pltpu.roll(jnp.where(lane < shift, b, a), LANES - shift, 1)
                    data[k * WIN : (k + 1) * WIN, half * LANES : (half + 1) * LANES] = moved


def model_loop(
    n_rows, n_cols, height, patch_ref, row_ref, set_ref, top_ref, table8_ref, table_ref, image, buffers, first, last, store
):
    width = PHASES * LANES
    block = PHASES * ROWS
    fine = FINE * block
    shape = (block, 2 * LANES)
    row_in = iota(shape, 0) % ROWS + iota(shape, 1) // LANES * ROWS
    undo = top_ref[0:1, 0:1] * (1.0 / (TOP * SCALE))

    def build(t, data_hi, data_lo):
        step_row, step_col = place(patch_ref[t], n_cols)
        row = step_row * height + row_ref[t] + EDGE - HALF
        fill(image, 0, row, step_col, 2, BF16, data_hi)
        fill(image, 1, row, step_col, 2, F8, data_lo)

    def multiply(t, data_hi, data_lo):
        step_row, step_col = place(patch_ref[t], n_cols)
        which = set_ref[t]
        big = mxu(table_ref[which], data_hi[...])
        small = mxu(table8_ref[which], data_lo[...])
        exact_terms = big[:fine] + big[6 * block :] + small * undo
        term_1, term_v, term_u = [exact_terms[p * block : (p + 1) * block] for p in range(FINE)]
        term_uu, term_uv, term_vv = [big[p * block : (p + 1) * block] for p in range(FINE, 6)]
        one_u = columns_of(step_col, n_cols, width)
        u = jnp.concatenate([one_u, one_u], axis=1)
        y = (step_row - 1) * height - height // 2 + row_ref[t] + row_in
        v = 2.0 * (y.astype(F32) + 0.5) / (n_rows * height)
        store(t, term_1 + u * (term_u + u * term_uu + v * term_uv) + v * (term_v + v * term_vv))

    build(first, *buffers[0])
    n = last - first
    some = next(k for k in (14, 8, 4) if n % k == 0)

    def some_strips(i, carry):
        for j in range(some):
            t = first + some * i + j
            build(jnp.minimum(t + 1, last - 1), *buffers[(j + 1) % 2])
            multiply(t, *buffers[j % 2])
        return carry

    lax.fori_loop(0, n // some, some_strips, 0)


def store_model(models, first, strip_rows, t, model):
    for half in range(2):
        rows_of = pl.ds(pl.multiple_of((t - first) * strip_rows + half * ROWS, ROWS), ROWS)
        for dx in range(PHASES):
            models[rows_of, dx * LANES : (dx + 1) * LANES] = model[
                dx * ROWS : (dx + 1) * ROWS, half * LANES : (half + 1) * LANES
            ]


def strips_kernel(
    n_rows, n_cols, patch_ref, row_ref, set_ref, top_ref, near_rows, away_rows, here_ref, even_ref, odd_ref,
    table8_ref, table_ref, image, models, hi_a, lo_a, hi_b, lo_b,
):
    height = here_ref.shape[0]
    width = PHASES * LANES
    scatter = to_phases(width)
    rows = image.shape[3]
    upper = lax.axis_index("visit") % 2 == 0
    ahead = lax.axis_index("visit") % 4 < 2
    for b in range(4):
        cols = slice(b * width, min((b + 1) * width, here_ref.shape[1]))
        near, away, even, odd = [r[:, cols] for r in (near_rows, away_rows, even_ref, odd_ref)]
        pieces = (
            jnp.where(ahead, away, near),
            jnp.where(upper, odd, even),
            here_ref[:, cols],
            jnp.where(upper, even, odd),
            jnp.where(ahead, near, away),
        )
        parts = [split(piece) for piece in pieces]
        both = jnp.concatenate([hi for hi, _ in parts] + [lo for _, lo in parts], axis=0)
        moved = mxu(both, scatter[: cols.stop - cols.start])
        for f in range(PHASES):
            for part in range(2):
                some = moved[part * rows : (part + 1) * rows, f * LANES : (f + 1) * LANES]
                image[part, f, b] = some * SCALE if part else some

    strip_rows = models.shape[0] // (patch_ref.shape[0] - LATER)
    model_loop(
        n_rows, n_cols, height, patch_ref, row_ref, set_ref, top_ref, table8_ref, table_ref, image,
        ((hi_a, lo_a), (hi_b, lo_b)), 0, patch_ref.shape[0] - LATER,
        functools.partial(store_model, models, 0, strip_rows),
    )


def finish_kernel(
    n_rows, n_cols, height, patch_ref, row_ref, set_ref, top_ref, table8_ref, table_ref, image, models, strips_hbm, diff_hbm,
    strips_ref, rest, hi_a, lo_a, hi_b, lo_b, sems,
):
    n_strips, strip_rows, width = strips_ref.shape
    copy_strips = pltpu.make_async_copy(strips_hbm, strips_ref, sems.at[4])
    copy_strips.start()
    model_loop(
        n_rows, n_cols, height, patch_ref, row_ref, set_ref, top_ref, table8_ref, table_ref, image,
        ((hi_a, lo_a), (hi_b, lo_b)), n_strips - LATER, n_strips,
        functools.partial(store_model, rest, n_strips - LATER, strip_rows),
    )
    gather = from_phases()
    gather = jnp.concatenate([gather, gather], axis=0)
    copy_strips.wait()
    some = 16
    ready = models.shape[0]
    for c in range(n_strips // some):
        rows = slice(c * some * strip_rows, (c + 1) * some * strip_rows)
        found = models[rows] if rows.stop <= ready else jnp.concatenate([models[rows.start : ready], rest[...]], axis=0)
        natural = mxu(jnp.concatenate(split(found), axis=1), gather)
        part = pl.ds(c * some, some)
        strips_ref[part] = strips_ref[part] - natural.reshape(some, strip_rows, width)
        pltpu.make_async_copy(strips_ref.at[part], diff_hbm.at[part], sems.at[c]).start()
    for c in range(n_strips // some):
        part = pl.ds(c * some, some)
        pltpu.make_async_copy(strips_ref.at[part], diff_hbm.at[part], sems.at[c]).wait()


def coadd_kernel(
    n_rows, n_cols, flat_ref, image, mid_any, even_any, odd_any, coadd_ref,
    mid_ref, even_ref, odd_ref, taps, wide, models, hi_a, lo_a, hi_b, lo_b, sems,
):
    height, width = coadd_ref.shape
    sources = (mid_any, even_any, odd_any)
    targets = (mid_ref, even_ref, odd_ref)
    copies = [pltpu.make_async_copy(source, target, sems.at[i]) for i, (source, target) in enumerate(zip(sources, targets))]
    for copy in copies:
        copy.start()
    for copy in copies:
        copy.wait()
    count = mid_ref[0, height:, :] + even_ref[0, height:, :] + odd_ref[0, height:, :]
    n_sets = count.shape[0]
    v = 2.0 * ((iota(count.shape, 1) - height // 2).astype(F32) + 0.5) / (n_rows * height)

    def three(x, p):
        taps_of = flat_ref[p * n_sets : (p + 1) * n_sets, :]
        x_hi, t_hi = x.astype(BF16).astype(F32), taps_of.astype(BF16).astype(F32)
        return [(x_hi, t_hi), (x - x_hi, t_hi), (x_hi, taps_of - t_hi)]

    by_power = []
    for terms in ((0, 1, 5), (2, 4), (3,)):
        rows, x = [], count
        for p in terms:
            rows, x = rows + three(x, p), x * v
        sides = [jnp.concatenate(side, axis=0) for side in zip(*rows)]
        by_power.append(mxu(sides[0].T.astype(BF16), sides[1].astype(BF16)))
    for a in range(3):
        for c in range(TILES):
            taps[c, a * height : (a + 1) * height, :] = by_power[a][:, c * LANES : (c + 1) * LANES]
    n = 3 * height // ROWS
    for dy in range(ROWS):
        some = jnp.concatenate([taps[c, pl.ds(dy, n, stride=ROWS), :] for c in range(TILES)], axis=1)
        moved = some if dy == 0 else pltpu.roll(some, dy, 1)
        for c in range(TILES):
            wide[c, pl.ds(dy, n, stride=ROWS), :] = moved[:, c * LANES : (c + 1) * LANES]
    one_u = columns_of(1, n_cols, width)

    def build(b, data_hi, data_lo):
        fill(image, 0, height + b * ROWS + EDGE - HALF, 1, 1, BF16, data_hi)
        fill(image, 1, height + b * ROWS + EDGE - HALF, 1, 1, BF16, data_lo)

    def multiply(b, data_hi, data_lo):
        row = pl.multiple_of(b * ROWS, ROWS)
        fine_hi, fine_lo = split(on_phases(wide, row))
        rest = [on_phases(wide, a * height + row).astype(BF16) for a in (1, 2)]
        big = mxu(jnp.concatenate([fine_hi] + rest + [fine_lo], axis=0), data_hi[...])
        terms = big.reshape(4, PHASES * ROWS, LANES)
        small = mxu(fine_hi, data_lo[...]) * (1.0 / SCALE)
        model = terms[0] + terms[3] + small + one_u * (terms[1] + one_u * terms[2])
        for dx in range(PHASES):
            models[pl.ds(row, ROWS), dx * LANES : (dx + 1) * LANES] = model[dx * ROWS : (dx + 1) * ROWS]

    n_blocks = height // ROWS
    build(0, hi_a, lo_a)
    some = n_blocks
    buffers = ((hi_a, lo_a), (hi_b, lo_b))

    def some_blocks(i, carry):
        for j in range(some):
            b = some * i + j
            build(jnp.minimum(b + 1, n_blocks - 1), *buffers[(j + 1) % 2])
            multiply(b, *buffers[j % 2])
        return carry

    lax.fori_loop(0, n_blocks // some, some_blocks, 0)
    gather = from_phases()
    gather = jnp.concatenate([gather, gather], axis=0)
    natural = mxu(jnp.concatenate(split(models[...]), axis=1), gather)
    for c in range(PHASES):
        total = mid_ref[c, 0:height, :] + even_ref[c, 0:height, :] + odd_ref[c, 0:height, :]
        coadd_ref[:, c * LANES : (c + 1) * LANES] = total - natural[:, c * LANES : (c + 1) * LANES]


def swap(x, axis, apart, first):
    size = lax.axis_size(axis)
    lower = [i for i in range(size - apart) if (i - first) % (2 * apart) < apart]
    pairs = [(i, i + apart) for i in lower] + [(i + apart, i) for i in lower]
    return lax.ppermute(x, axis, pairs)


def per_device(strips, patch_of, box_row, kernel_set, template, row_taps, col_taps, kernel_coef):
    n_rows, n_cols = lax.axis_size("visit"), lax.axis_size("det")
    n_strips, strip_rows, width = strips.shape
    height = template.shape[0]
    n_sets, n_terms, n_basis = kernel_coef.shape
    block = PHASES * ROWS
    smem = pl.BlockSpec(memory_space=pltpu.SMEM)
    vmem = pl.BlockSpec(memory_space=pltpu.VMEM)
    hbm = pl.BlockSpec(memory_space=pltpu.HBM)
    free = pl.BlockSpec(memory_space=pl.ANY)

    patch_of = patch_of.reshape(n_strips)

    v, d = lax.axis_index("visit"), lax.axis_index("det")
    first, last = template[:, :SIDE], template[:, width - SIDE :]
    ahead = d % 4 < 2
    even = swap(template, "det", 1, 0)
    odd = swap(template, "det", 1, 1)
    for_near, for_away = jnp.where(ahead, last, first), jnp.where(ahead, first, last)
    patch_of, for_near, for_away = lax.optimization_barrier((patch_of, for_near, for_away))
    near = swap(for_near, "det", 2, 0)
    away = swap(for_away, "det", 2, 2)

    sums = jax.ShapeDtypeStruct((3, PHASES, height + ROWS, LANES), F32)
    for_even, mid, for_odd = pl.pallas_call(
        functools.partial(sums_kernel, n_cols),
        out_shape=(sums, pltpu.VMEM(sums.shape, F32), sums),
        in_specs=[smem] * 3 + [hbm],
        out_specs=(hbm, vmem, hbm),
        scratch_shapes=[
            pltpu.VMEM(strips.shape, F32),
            pltpu.VMEM((9, PHASES, height + ROWS, LANES), F32),
            pltpu.SemaphoreType.DMA((6,)),
        ],
        compiler_params=pltpu.CompilerParams(vmem_limit_bytes=56 * MIB),
        cost_estimate=pl.CostEstimate(flops=3 << 30, bytes_accessed=5 << 20, transcendentals=0),
        name="strip_sums",
    )(patch_of, box_row, kernel_set, strips)

    far_left, far_right = jnp.where(ahead, away, near), jnp.where(ahead, near, away)
    left, right = jnp.where(d % 2 == 0, odd, even), jnp.where(d % 2 == 0, even, odd)
    blank = jnp.zeros((height, LANES - 2 * SIDE), F32)
    here = jnp.concatenate([far_left, left, template, right, far_right, blank], axis=1)

    for_even, for_odd, here = lax.optimization_barrier((for_even, for_odd, here))
    odd = swap(here, "visit", 1, 1)
    even = swap(here, "visit", 1, 0)
    first, last = here[:EDGE], here[height - EDGE :]
    ahead = v % 4 < 2
    for_near, for_away = jnp.where(ahead, last, first), jnp.where(ahead, first, last)
    for_near, for_away, even, row_taps = lax.optimization_barrier((for_near, for_away, even, row_taps))
    near_rows = swap(for_near, "visit", 2, 0)
    away_rows = swap(for_away, "visit", 2, 2)

    sum_even = swap(for_even, "det", 1, 0)
    sum_odd = swap(for_odd, "det", 1, 1)

    flat, table, table8, top = pl.pallas_call(
        functools.partial(taps_kernel, n_rows, n_cols),
        out_shape=(
            pltpu.VMEM((n_sets * n_terms, DEPTH), F32),
            pltpu.VMEM((n_sets, (n_terms + FINE) * block, DEPTH), BF16),
            pltpu.VMEM((n_sets, FINE * block, DEPTH), F8),
            pltpu.VMEM((ROWS, LANES), F32),
        ),
        in_specs=[vmem] * 3,
        out_specs=(vmem,) * 4,
        scratch_shapes=[pltpu.VMEM((TILES, n_sets * n_terms * ROWS, LANES), F32)],
        compiler_params=pltpu.CompilerParams(vmem_limit_bytes=56 * MIB),
        cost_estimate=pl.CostEstimate(flops=3 << 30, bytes_accessed=5 << 20, transcendentals=0),
        name="tap_tables",
    )(row_taps.T, col_taps.T, jnp.swapaxes(kernel_coef, 0, 1).reshape(n_terms * n_sets, n_basis))

    flat, table, table8, top = [
        pltpu.with_memory_space_constraint(x, pltpu.VMEM) for x in (flat, table, table8, top)
    ]

    even, odd, near_rows, away_rows, here = [
        pltpu.with_memory_space_constraint(x, pltpu.VMEM) for x in (even, odd, near_rows, away_rows, here)
    ]

    flops = n_strips * 2 * n_terms * block * DEPTH * 2 * LANES * 2
    buffers = [pltpu.VMEM((DEPTH, 2 * LANES), kind) for kind in (BF16, F8, BF16, F8)]
    image, models = pl.pallas_call(
        functools.partial(strips_kernel, n_rows, n_cols),
        out_shape=(
            pltpu.VMEM((2, PHASES, 4, 3 * height + 2 * EDGE, LANES), F32),
            pltpu.VMEM(((n_strips - LATER) * strip_rows, width), F32),
        ),
        in_specs=[smem] * 3 + [vmem] * 8,
        out_specs=(vmem, vmem),
        scratch_shapes=buffers,
        compiler_params=pltpu.CompilerParams(vmem_limit_bytes=32 * MIB),
        cost_estimate=pl.CostEstimate(flops=flops, bytes_accessed=14 << 20, transcendentals=0),
        name="strip_models",
    )(patch_of, box_row, kernel_set, top, near_rows, away_rows, here, even, odd, table8, table)

    image, models, sum_even, sum_odd = lax.optimization_barrier((image, models, sum_even, sum_odd))
    mid = mid + sum_even + sum_odd
    image, models = [pltpu.with_memory_space_constraint(x, pltpu.VMEM) for x in (image, models)]
    from_even = swap(jnp.where(v % 2 == 0, mid[2], mid[0]), "visit", 1, 0)
    from_odd = swap(jnp.where(v % 2 == 0, mid[0], mid[2]), "visit", 1, 1)

    patch_of, mid = lax.optimization_barrier((patch_of, mid))
    difference = pl.pallas_call(
        functools.partial(finish_kernel, n_rows, n_cols, height),
        out_shape=jax.ShapeDtypeStruct(strips.shape, F32),
        in_specs=[smem] * 3 + [vmem] * 5 + [hbm],
        out_specs=hbm,
        scratch_shapes=[pltpu.VMEM(strips.shape, F32), pltpu.VMEM((LATER * strip_rows, width), F32)]
        + buffers
        + [pltpu.SemaphoreType.DMA((5,))],
        compiler_params=pltpu.CompilerParams(vmem_limit_bytes=32 * MIB),
        cost_estimate=pl.CostEstimate(flops=flops // 4, bytes_accessed=4 << 20, transcendentals=0),
        name="finish",
    )(patch_of, box_row, kernel_set, top, table8, table, image, models, strips)

    coadd = pl.pallas_call(
        functools.partial(coadd_kernel, n_rows, n_cols),
        out_shape=jax.ShapeDtypeStruct(template.shape, F32),
        in_specs=[vmem, vmem] + [free] * 3,
        out_specs=vmem,
        scratch_shapes=[pltpu.VMEM(x.shape, F32) for x in (from_even, from_even, from_odd)]
        + [
            pltpu.VMEM((TILES, 3 * height, LANES), F32),
            pltpu.VMEM((TILES, 3 * height, LANES), F32),
            pltpu.VMEM((height, PHASES * LANES), F32),
        ]
        + [pltpu.VMEM((DEPTH, LANES), BF16)] * 4
        + [pltpu.SemaphoreType.DMA((3,))],
        compiler_params=pltpu.CompilerParams(vmem_limit_bytes=32 * MIB),
        cost_estimate=pl.CostEstimate(flops=6 << 30, bytes_accessed=3 << 20, transcendentals=0),
        name="coadd_models",
    )(flat, image, mid[1], from_even, from_odd)
    return difference, coadd


def solution(mesh):
    tiles = ("visit", "det")
    in_specs = (P(tiles, None, None), P(tiles, None), P(tiles), P(tiles), P("visit", "det"), P(), P(), P())
    out_specs = (P(tiles, None, None), P("visit", "det"))
    return jax.shard_map(per_device, mesh=mesh, in_specs=in_specs, out_specs=out_specs, check_vma=False)
```

```python
import functools

import jax
import jax.numpy as jnp
from jax import lax
from jax.experimental import pallas as pl
from jax.experimental.pallas import tpu as pltpu
from jax.sharding import PartitionSpec as P

F32 = jnp.float32
BF16 = jnp.bfloat16
F8 = jnp.float8_e4m3fn
HIGHEST = lax.Precision.HIGHEST

HALF = 10
SIDE = 12
EDGE = 16
PHASES = 4
LANES = 128
ROWS = 8
WIN = 32
SHIFTS = 24
DEPTH = SHIFTS * WIN
TILES = DEPTH // LANES
LATER = 8
FINE = 3
SCALE = 2.0**14
TOP = 256.0
MIB = 1024 * 1024


def iota(shape, dim):
    return lax.broadcasted_iota(jnp.int32, shape, dim)


def split(x):
    hi = x.astype(BF16)
    lo = (x - hi.astype(F32)).astype(BF16)
    return hi, lo


def mxu(a, b):
    return jnp.dot(a, b, preferred_element_type=F32)


def exact(a, b):
    return jnp.dot(a, b, precision=HIGHEST, preferred_element_type=F32)


def to_phases(width):
    out = iota((width, PHASES * LANES), 1)
    source = (out % LANES) * PHASES + out // LANES
    return jnp.where(iota((width, PHASES * LANES), 0) == source, 1.0, 0.0).astype(BF16)


def from_phases():
    src = iota((PHASES * LANES, PHASES * LANES), 0)
    target = (src % LANES) * PHASES + src // LANES
    return jnp.where(iota((PHASES * LANES, PHASES * LANES), 1) == target, 1.0, 0.0).astype(BF16)


def place(patch, n_cols):
    step_row = (patch >> (n_cols.bit_length() - 1)) - lax.axis_index("visit") + 1
    step_col = (patch & (n_cols - 1)) - lax.axis_index("det") + 1
    return step_row, step_col


def sums_kernel(n_cols, patch_ref, row_ref, set_ref, strips_hbm, even_hbm, mid_ref, odd_hbm, strips_ref, acc, sems):
    n_strips, strip_rows, _ = strips_ref.shape
    n_parts = 4
    some = n_strips // n_parts
    inputs = []
    for i in range(n_parts):
        part = pl.ds(i * some, some)
        inputs.append(pltpu.make_async_copy(strips_hbm.at[part], strips_ref.at[part], sems.at[2 + i]))
        inputs[i].start()
    acc[...] = jnp.zeros(acc.shape, F32)
    height = acc.shape[2] - ROWS
    place_lane = iota((ROWS, LANES), 1)
    place_sub = iota((ROWS, LANES), 0)

    def one_strip(t, carry):
        step_row, step_col = place(patch_ref[t], n_cols)
        top = row_ref[t]
        q = step_col * 3 + step_row
        for c in range(PHASES):
            acc[q, c, pl.ds(top, strip_rows), :] += strips_ref[t, :, c * LANES : (c + 1) * LANES]
        hit = (place_sub == set_ref[t]) & (place_lane >= top) & (place_lane < top + strip_rows)
        acc[q, 0, height:, :] += jnp.where(hit, 1.0, 0.0)
        return carry

    for i in range(n_parts):
        inputs[i].wait()
        lax.fori_loop(i * some, (i + 1) * some, one_strip, 0, unroll=8)
    parity = lax.axis_index("det") % 2
    copies = [
        pltpu.make_async_copy(acc.at[pl.ds(first, 3)], out, sems.at[i])
        for i, (first, out) in enumerate(((6 - 6 * parity, even_hbm), (6 * parity, odd_hbm)))
    ]
    for copy in copies:
        copy.start()
    mid_ref[...] = acc[3:6]
    for copy in copies:
        copy.wait()


def taps_kernel(
    n_rows, n_cols, row_taps_ref, col_taps_ref, coef_ref, flat_ref, table_ref, table8_ref, top_ref, wide
):
    taps = row_taps_ref.shape[0]
    lane = iota((taps, DEPTH), 1)
    sub = iota((taps, DEPTH), 0)
    row_part = exact(row_taps_ref[...].T, jnp.where(lane % WIN == sub, 1.0, 0.0))
    col_part = exact(col_taps_ref[...].T, jnp.where(lane // WIN == sub, 1.0, 0.0))
    n_sets = table_ref.shape[0]
    one, u, v, uu, uv, vv = [coef_ref[p * n_sets : (p + 1) * n_sets, :] for p in range(6)]
    u0 = (2 * lax.axis_index("det") + 1).astype(F32) / n_cols - 1.0
    v0 = (2 * lax.axis_index("visit") + 1).astype(F32) / n_rows - 1.0
    one, u, v = (
        one + u0 * (u + u0 * uu) + v0 * (v + u0 * uv + v0 * vv),
        u + 2.0 * u0 * uu + v0 * uv,
        v + u0 * uv + 2.0 * v0 * vv,
    )
    flat = exact(jnp.concatenate([one, v, u, uu, uv, vv], axis=0), row_part * col_part)
    flat_ref[...] = flat
    top = jnp.maximum(jnp.max(jnp.max(jnp.abs(flat), axis=1, keepdims=True), axis=0, keepdims=True), 1e-30)
    top_ref[...] = jnp.broadcast_to(top, top_ref.shape)
    scale = TOP / top
    n = flat.shape[0]
    block = PHASES * ROWS
    for dy in range(ROWS):
        moved = flat if dy == 0 else pltpu.roll(flat, dy, 1)
        for c in range(TILES):
            wide[c, pl.ds(dy, n, stride=ROWS), :] = moved[:, c * LANES : (c + 1) * LANES]
    for s in range(n_sets):
        for p in range(6):
            rows = on_phases(wide, (p * n_sets + s) * ROWS)
            hi = rows.astype(BF16)
            table_ref[s, p * block : (p + 1) * block, :] = hi
            if p < FINE:
                table_ref[s, (6 + p) * block : (7 + p) * block, :] = (rows - hi.astype(F32)).astype(BF16)
                table8_ref[s, p * block : (p + 1) * block, :] = (rows * scale).astype(F8)


def on_phases(wide, first):
    rows = jnp.concatenate([wide[c, pl.ds(first, ROWS), :] for c in range(TILES)], axis=1)
    return jnp.concatenate([rows] + [pltpu.roll(rows, dx * WIN, 1) for dx in range(1, PHASES)], axis=0)


def columns_of(step_col, n_cols, width):
    shape = (PHASES * ROWS, LANES)
    col = (step_col - 1) * width - width // 2 + iota(shape, 1) * PHASES + iota(shape, 0) // ROWS
    return 2.0 * (col.astype(F32) + 0.5) / (n_cols * width)


def fill(image_ref, part, row, col, halves, kind, data):
    lane = iota((WIN, LANES), 1)
    for phase in range(PHASES):
        near, far = [image_ref[part, phase, col + i, pl.ds(row, WIN + (halves - 1) * ROWS), :] for i in range(2)]
        for half in range(halves):
            rows = slice(half * ROWS, half * ROWS + WIN)
            a, b = near[rows].astype(kind), far[rows].astype(kind)
            for shift in range((SIDE - HALF + SHIFTS - 1) // PHASES + 1):
                k = shift * PHASES + phase - (SIDE - HALF)
                if 0 <= k < SHIFTS:
                    moved = a if shift == 0 else pltpu.roll(jnp.where(lane < shift, b, a), LANES - shift, 1)
                    data[k * WIN : (k + 1) * WIN, half * LANES : (half + 1) * LANES] = moved


def model_loop(
    n_rows, n_cols, height, patch_ref, row_ref, set_ref, top_ref, table8_ref, table_ref, image, buffers, first, last, store
):
    width = PHASES * LANES
    block = PHASES * ROWS
    fine = FINE * block
    shape = (block, 2 * LANES)
    row_in = iota(shape, 0) % ROWS + iota(shape, 1) // LANES * ROWS
    undo = top_ref[0:1, 0:1] * (1.0 / (TOP * SCALE))

    def build(t, data_hi, data_lo):
        step_row, step_col = place(patch_ref[t], n_cols)
        row = step_row * height + row_ref[t] + EDGE - HALF
        fill(image, 0, row, step_col, 2, BF16, data_hi)
        fill(image, 1, row, step_col, 2, F8, data_lo)

    def multiply(t, data_hi, data_lo):
        step_row, step_col = place(patch_ref[t], n_cols)
        which = set_ref[t]
        big = mxu(table_ref[which], data_hi[...])
        small = mxu(table8_ref[which], data_lo[...])
        exact_terms = big[:fine] + big[6 * block :] + small * undo
        term_1, term_v, term_u = [exact_terms[p * block : (p + 1) * block] for p in range(FINE)]
        term_uu, term_uv, term_vv = [big[p * block : (p + 1) * block] for p in range(FINE, 6)]
        one_u = columns_of(step_col, n_cols, width)
        u = jnp.concatenate([one_u, one_u], axis=1)
        y = (step_row - 1) * height - height // 2 + row_ref[t] + row_in
        v = 2.0 * (y.astype(F32) + 0.5) / (n_rows * height)
        store(t, term_1 + u * (term_u + u * term_uu + v * term_uv) + v * (term_v + v * term_vv))

    build(first, *buffers[0])
    n = last - first
    some = next(k for k in (14, 8, 4) if n % k == 0)

    def some_strips(i, carry):
        for j in range(some):
            t = first + some * i + j
            build(jnp.minimum(t + 1, last - 1), *buffers[(j + 1) % 2])
            multiply(t, *buffers[j % 2])
        return carry

    lax.fori_loop(0, n // some, some_strips, 0)


def store_model(models, first, strip_rows, t, model):
    for half in range(2):
        rows_of = pl.ds(pl.multiple_of((t - first) * strip_rows + half * ROWS, ROWS), ROWS)
        for dx in range(PHASES):
            models[rows_of, dx * LANES : (dx + 1) * LANES] = model[
                dx * ROWS : (dx + 1) * ROWS, half * LANES : (half + 1) * LANES
            ]


def strips_kernel(
    n_rows, n_cols, patch_ref, row_ref, set_ref, top_ref, near_rows, away_rows, here_ref, even_ref, beside_ref, own_ref,
    table8_ref, table_ref, image, models, hi_a, lo_a, hi_b, lo_b,
):
    height = here_ref.shape[0]
    width = PHASES * LANES
    scatter = to_phases(width)
    rows = image.shape[3]
    upper = lax.axis_index("visit") % 2 == 0
    ahead = lax.axis_index("visit") % 4 < 2
    cut = SIDE + width
    odd_band = jnp.concatenate([beside_ref[:, :cut], own_ref[...], beside_ref[:, cut:]], axis=1)
    for b in range(4):
        cols = slice(b * width, min((b + 1) * width, here_ref.shape[1]))
        near, away, even = [r[:, cols] for r in (near_rows, away_rows, even_ref)]
        odd = odd_band[:, cols]
        pieces = (
            jnp.where(ahead, away, near),
            jnp.where(upper, odd, even),
            here_ref[:, cols],
            jnp.where(upper, even, odd),
            jnp.where(ahead, near, away),
        )
        parts = [split(piece) for piece in pieces]
        both = jnp.concatenate([hi for hi, _ in parts] + [lo for _, lo in parts], axis=0)
        moved = mxu(both, scatter[: cols.stop - cols.start])
        for f in range(PHASES):
            for part in range(2):
                some = moved[part * rows : (part + 1) * rows, f * LANES : (f + 1) * LANES]
                image[part, f, b] = some * SCALE if part else some

    strip_rows = models.shape[0] // (patch_ref.shape[0] - LATER)
    model_loop(
        n_rows, n_cols, height, patch_ref, row_ref, set_ref, top_ref, table8_ref, table_ref, image,
        ((hi_a, lo_a), (hi_b, lo_b)), 0, patch_ref.shape[0] - LATER,
        functools.partial(store_model, models, 0, strip_rows),
    )


def finish_kernel(
    n_rows, n_cols, height, patch_ref, row_ref, set_ref, top_ref, table8_ref, table_ref, image, models, strips_hbm, diff_hbm,
    strips_ref, rest, hi_a, lo_a, hi_b, lo_b, sems,
):
    n_strips, strip_rows, width = strips_ref.shape
    copy_strips = pltpu.make_async_copy(strips_hbm, strips_ref, sems.at[4])
    copy_strips.start()
    model_loop(
        n_rows, n_cols, height, patch_ref, row_ref, set_ref, top_ref, table8_ref, table_ref, image,
        ((hi_a, lo_a), (hi_b, lo_b)), n_strips - LATER, n_strips,
        functools.partial(store_model, rest, n_strips - LATER, strip_rows),
    )
    gather = from_phases()
    gather = jnp.concatenate([gather, gather], axis=0)
    copy_strips.wait()
    some = 16
    ready = models.shape[0]
    for c in range(n_strips // some):
        rows = slice(c * some * strip_rows, (c + 1) * some * strip_rows)
        found = models[rows] if rows.stop <= ready else jnp.concatenate([models[rows.start : ready], rest[...]], axis=0)
        natural = mxu(jnp.concatenate(split(found), axis=1), gather)
        part = pl.ds(c * some, some)
        strips_ref[part] = strips_ref[part] - natural.reshape(some, strip_rows, width)
        pltpu.make_async_copy(strips_ref.at[part], diff_hbm.at[part], sems.at[c]).start()
    for c in range(n_strips // some):
        part = pl.ds(c * some, some)
        pltpu.make_async_copy(strips_ref.at[part], diff_hbm.at[part], sems.at[c]).wait()


def coadd_kernel(
    n_rows, n_cols, flat_ref, image, mid_any, even_any, odd_any, coadd_ref,
    mid_ref, even_ref, odd_ref, taps, wide, models, hi_a, lo_a, hi_b, lo_b, sems,
):
    height, width = coadd_ref.shape
    sources = (mid_any, even_any, odd_any)
    targets = (mid_ref, even_ref, odd_ref)
    copies = [pltpu.make_async_copy(source, target, sems.at[i]) for i, (source, target) in enumerate(zip(sources, targets))]
    for copy in copies:
        copy.start()
    for copy in copies:
        copy.wait()
    count = mid_ref[0, height:, :] + even_ref[0, height:, :] + odd_ref[0, height:, :]
    n_sets = count.shape[0]
    v = 2.0 * ((iota(count.shape, 1) - height // 2).astype(F32) + 0.5) / (n_rows * height)

    def three(x, p):
        taps_of = flat_ref[p * n_sets : (p + 1) * n_sets, :]
        x_hi, t_hi = x.astype(BF16).astype(F32), taps_of.astype(BF16).astype(F32)
        return [(x_hi, t_hi), (x - x_hi, t_hi), (x_hi, taps_of - t_hi)]

    by_power = []
    for terms in ((0, 1, 5), (2, 4), (3,)):
        rows, x = [], count
        for p in terms:
            rows, x = rows + three(x, p), x * v
        sides = [jnp.concatenate(side, axis=0) for side in zip(*rows)]
        by_power.append(mxu(sides[0].T.astype(BF16), sides[1].astype(BF16)))
    for a in range(3):
        for c in range(TILES):
            taps[c, a * height : (a + 1) * height, :] = by_power[a][:, c * LANES : (c + 1) * LANES]
    n = 3 * height // ROWS
    for dy in range(ROWS):
        some = jnp.concatenate([taps[c, pl.ds(dy, n, stride=ROWS), :] for c in range(TILES)], axis=1)
        moved = some if dy == 0 else pltpu.roll(some, dy, 1)
        for c in range(TILES):
            wide[c, pl.ds(dy, n, stride=ROWS), :] = moved[:, c * LANES : (c + 1) * LANES]
    one_u = columns_of(1, n_cols, width)

    def build(b, data_hi, data_lo):
        fill(image, 0, height + b * ROWS + EDGE - HALF, 1, 1, BF16, data_hi)
        fill(image, 1, height + b * ROWS + EDGE - HALF, 1, 1, BF16, data_lo)

    def multiply(b, data_hi, data_lo):
        row = pl.multiple_of(b * ROWS, ROWS)
        fine_hi, fine_lo = split(on_phases(wide, row))
        rest = [on_phases(wide, a * height + row).astype(BF16) for a in (1, 2)]
        big = mxu(jnp.concatenate([fine_hi] + rest + [fine_lo], axis=0), data_hi[...])
        terms = big.reshape(4, PHASES * ROWS, LANES)
        small = mxu(fine_hi, data_lo[...]) * (1.0 / SCALE)
        model = terms[0] + terms[3] + small + one_u * (terms[1] + one_u * terms[2])
        for dx in range(PHASES):
            models[pl.ds(row, ROWS), dx * LANES : (dx + 1) * LANES] = model[dx * ROWS : (dx + 1) * ROWS]

    n_blocks = height // ROWS
    build(0, hi_a, lo_a)
    some = n_blocks
    buffers = ((hi_a, lo_a), (hi_b, lo_b))

    def some_blocks(i, carry):
        for j in range(some):
            b = some * i + j
            build(jnp.minimum(b + 1, n_blocks - 1), *buffers[(j + 1) % 2])
            multiply(b, *buffers[j % 2])
        return carry

    lax.fori_loop(0, n_blocks // some, some_blocks, 0)
    gather = from_phases()
    gather = jnp.concatenate([gather, gather], axis=0)
    natural = mxu(jnp.concatenate(split(models[...]), axis=1), gather)
    for c in range(PHASES):
        total = mid_ref[c, 0:height, :] + even_ref[c, 0:height, :] + odd_ref[c, 0:height, :]
        coadd_ref[:, c * LANES : (c + 1) * LANES] = total - natural[:, c * LANES : (c + 1) * LANES]


def swap(x, axis, apart, first):
    size = lax.axis_size(axis)
    lower = [i for i in range(size - apart) if (i - first) % (2 * apart) < apart]
    pairs = [(i, i + apart) for i in lower] + [(i + apart, i) for i in lower]
    return lax.ppermute(x, axis, pairs)


def per_device(strips, patch_of, box_row, kernel_set, template, row_taps, col_taps, kernel_coef):
    n_rows, n_cols = lax.axis_size("visit"), lax.axis_size("det")
    n_strips, strip_rows, width = strips.shape
    height = template.shape[0]
    n_sets, n_terms, n_basis = kernel_coef.shape
    block = PHASES * ROWS
    smem = pl.BlockSpec(memory_space=pltpu.SMEM)
    vmem = pl.BlockSpec(memory_space=pltpu.VMEM)
    hbm = pl.BlockSpec(memory_space=pltpu.HBM)
    free = pl.BlockSpec(memory_space=pl.ANY)

    patch_of = patch_of.reshape(n_strips)

    v, d = lax.axis_index("visit"), lax.axis_index("det")
    first, last = template[:, :SIDE], template[:, width - SIDE :]
    ahead = d % 4 < 2
    even = swap(template, "det", 1, 0)
    odd = swap(template, "det", 1, 1)
    odd_own = swap(template, "visit", 1, 1)
    for_near, for_away = jnp.where(ahead, last, first), jnp.where(ahead, first, last)
    patch_of, for_near, for_away = lax.optimization_barrier((patch_of, for_near, for_away))
    near = swap(for_near, "det", 2, 0)
    away = swap(for_away, "det", 2, 2)

    sums = jax.ShapeDtypeStruct((3, PHASES, height + ROWS, LANES), F32)
    for_even, mid, for_odd = pl.pallas_call(
        functools.partial(sums_kernel, n_cols),
        out_shape=(sums, pltpu.VMEM(sums.shape, F32), sums),
        in_specs=[smem] * 3 + [hbm],
        out_specs=(hbm, vmem, hbm),
        scratch_shapes=[
            pltpu.VMEM(strips.shape, F32),
            pltpu.VMEM((9, PHASES, height + ROWS, LANES), F32),
            pltpu.SemaphoreType.DMA((6,)),
        ],
        compiler_params=pltpu.CompilerParams(vmem_limit_bytes=56 * MIB),
        cost_estimate=pl.CostEstimate(flops=3 << 30, bytes_accessed=5 << 20, transcendentals=0),
        name="strip_sums",
    )(patch_of, box_row, kernel_set, strips)

    near, away, odd_own = lax.optimization_barrier((near, away, odd_own))
    far_left, far_right = jnp.where(ahead, away, near), jnp.where(ahead, near, away)
    left, right = jnp.where(d % 2 == 0, odd, even), jnp.where(d % 2 == 0, even, odd)
    blank = jnp.zeros((height, LANES - 2 * SIDE), F32)
    here = jnp.concatenate([far_left, left, template, right, far_right, blank], axis=1)

    beside = jnp.concatenate([far_left, left, right, far_right, blank], axis=1)
    for_even, for_odd, here, beside = lax.optimization_barrier((for_even, for_odd, here, beside))
    odd = swap(beside, "visit", 1, 1)
    even = swap(here, "visit", 1, 0)
    first, last = here[:EDGE], here[height - EDGE :]
    ahead = v % 4 < 2
    for_near, for_away = jnp.where(ahead, last, first), jnp.where(ahead, first, last)
    for_near, for_away, even, row_taps = lax.optimization_barrier((for_near, for_away, even, row_taps))
    near_rows = swap(for_near, "visit", 2, 0)
    away_rows = swap(for_away, "visit", 2, 2)

    sum_even = swap(for_even, "det", 1, 0)
    sum_odd = swap(for_odd, "det", 1, 1)

    flat, table, table8, top = pl.pallas_call(
        functools.partial(taps_kernel, n_rows, n_cols),
        out_shape=(
            pltpu.VMEM((n_sets * n_terms, DEPTH), F32),
            pltpu.VMEM((n_sets, (n_terms + FINE) * block, DEPTH), BF16),
            pltpu.VMEM((n_sets, FINE * block, DEPTH), F8),
            pltpu.VMEM((ROWS, LANES), F32),
        ),
        in_specs=[vmem] * 3,
        out_specs=(vmem,) * 4,
        scratch_shapes=[pltpu.VMEM((TILES, n_sets * n_terms * ROWS, LANES), F32)],
        compiler_params=pltpu.CompilerParams(vmem_limit_bytes=56 * MIB),
        cost_estimate=pl.CostEstimate(flops=3 << 30, bytes_accessed=5 << 20, transcendentals=0),
        name="tap_tables",
    )(row_taps.T, col_taps.T, jnp.swapaxes(kernel_coef, 0, 1).reshape(n_terms * n_sets, n_basis))

    flat, table, table8, top = [
        pltpu.with_memory_space_constraint(x, pltpu.VMEM) for x in (flat, table, table8, top)
    ]

    even, odd, odd_own, near_rows, away_rows, here = [
        pltpu.with_memory_space_constraint(x, pltpu.VMEM) for x in (even, odd, odd_own, near_rows, away_rows, here)
    ]

    flops = n_strips * 2 * n_terms * block * DEPTH * 2 * LANES * 2
    buffers = [pltpu.VMEM((DEPTH, 2 * LANES), kind) for kind in (BF16, F8, BF16, F8)]
    image, models = pl.pallas_call(
        functools.partial(strips_kernel, n_rows, n_cols),
        out_shape=(
            pltpu.VMEM((2, PHASES, 4, 3 * height + 2 * EDGE, LANES), F32),
            pltpu.VMEM(((n_strips - LATER) * strip_rows, width), F32),
        ),
        in_specs=[smem] * 3 + [vmem] * 9,
        out_specs=(vmem, vmem),
        scratch_shapes=buffers,
        compiler_params=pltpu.CompilerParams(vmem_limit_bytes=32 * MIB),
        cost_estimate=pl.CostEstimate(flops=flops, bytes_accessed=14 << 20, transcendentals=0),
        name="strip_models",
    )(patch_of, box_row, kernel_set, top, near_rows, away_rows, here, even, odd, odd_own, table8, table)

    image, models, sum_even, sum_odd = lax.optimization_barrier((image, models, sum_even, sum_odd))
    mid = mid + sum_even + sum_odd
    image, models = [pltpu.with_memory_space_constraint(x, pltpu.VMEM) for x in (image, models)]
    from_even = swap(jnp.where(v % 2 == 0, mid[2], mid[0]), "visit", 1, 0)
    from_odd = swap(jnp.where(v % 2 == 0, mid[0], mid[2]), "visit", 1, 1)

    patch_of, mid = lax.optimization_barrier((patch_of, mid))
    difference = pl.pallas_call(
        functools.partial(finish_kernel, n_rows, n_cols, height),
        out_shape=jax.ShapeDtypeStruct(strips.shape, F32),
        in_specs=[smem] * 3 + [vmem] * 5 + [hbm],
        out_specs=hbm,
        scratch_shapes=[pltpu.VMEM(strips.shape, F32), pltpu.VMEM((LATER * strip_rows, width), F32)]
        + buffers
        + [pltpu.SemaphoreType.DMA((5,))],
        compiler_params=pltpu.CompilerParams(vmem_limit_bytes=32 * MIB),
        cost_estimate=pl.CostEstimate(flops=flops // 4, bytes_accessed=4 << 20, transcendentals=0),
        name="finish",
    )(patch_of, box_row, kernel_set, top, table8, table, image, models, strips)

    coadd = pl.pallas_call(
        functools.partial(coadd_kernel, n_rows, n_cols),
        out_shape=jax.ShapeDtypeStruct(template.shape, F32),
        in_specs=[vmem, vmem] + [free] * 3,
        out_specs=vmem,
        scratch_shapes=[pltpu.VMEM(x.shape, F32) for x in (from_even, from_even, from_odd)]
        + [
            pltpu.VMEM((TILES, 3 * height, LANES), F32),
            pltpu.VMEM((TILES, 3 * height, LANES), F32),
            pltpu.VMEM((height, PHASES * LANES), F32),
        ]
        + [pltpu.VMEM((DEPTH, LANES), BF16)] * 4
        + [pltpu.SemaphoreType.DMA((3,))],
        compiler_params=pltpu.CompilerParams(vmem_limit_bytes=32 * MIB),
        cost_estimate=pl.CostEstimate(flops=6 << 30, bytes_accessed=3 << 20, transcendentals=0),
        name="coadd_models",
    )(flat, image, mid[1], from_even, from_odd)
    return difference, coadd


def solution(mesh):
    tiles = ("visit", "det")
    in_specs = (P(tiles, None, None), P(tiles, None), P(tiles), P(tiles), P("visit", "det"), P(), P(), P())
    out_specs = (P(tiles, None, None), P("visit", "det"))
    return jax.shard_map(per_device, mesh=mesh, in_specs=in_specs, out_specs=out_specs, check_vma=False)
```

```python
import functools

import jax
import jax.numpy as jnp
from jax import lax
from jax.experimental import pallas as pl
from jax.experimental.pallas import tpu as pltpu
from jax.sharding import PartitionSpec as P

F32 = jnp.float32
BF16 = jnp.bfloat16
F8 = jnp.float8_e4m3fn
HIGHEST = lax.Precision.HIGHEST

HALF = 10
SIDE = 12
EDGE = 16
PHASES = 4
LANES = 128
ROWS = 8
WIN = 32
SHIFTS = 24
DEPTH = SHIFTS * WIN
TILES = DEPTH // LANES
LATER = 8
FINE = 3
SCALE = 2.0**14
TOP = 256.0
MIB = 1024 * 1024


def iota(shape, dim):
    return lax.broadcasted_iota(jnp.int32, shape, dim)


def split(x):
    hi = x.astype(BF16)
    lo = (x - hi.astype(F32)).astype(BF16)
    return hi, lo


def mxu(a, b):
    return jnp.dot(a, b, preferred_element_type=F32)


def exact(a, b):
    return jnp.dot(a, b, precision=HIGHEST, preferred_element_type=F32)


def to_phases(width):
    out = iota((width, PHASES * LANES), 1)
    source = (out % LANES) * PHASES + out // LANES
    return jnp.where(iota((width, PHASES * LANES), 0) == source, 1.0, 0.0).astype(BF16)


def from_phases():
    src = iota((PHASES * LANES, PHASES * LANES), 0)
    target = (src % LANES) * PHASES + src // LANES
    return jnp.where(iota((PHASES * LANES, PHASES * LANES), 1) == target, 1.0, 0.0).astype(BF16)


def place(patch, n_cols):
    step_row = (patch >> (n_cols.bit_length() - 1)) - lax.axis_index("visit") + 1
    step_col = (patch & (n_cols - 1)) - lax.axis_index("det") + 1
    return step_row, step_col


def sums_kernel(n_cols, patch_ref, row_ref, set_ref, strips_hbm, even_hbm, mid_ref, odd_hbm, strips_ref, acc, sems):
    n_strips, strip_rows, _ = strips_ref.shape
    n_parts = 4
    some = n_strips // n_parts
    inputs = []
    for i in range(n_parts):
        part = pl.ds(i * some, some)
        inputs.append(pltpu.make_async_copy(strips_hbm.at[part], strips_ref.at[part], sems.at[2 + i]))
        inputs[i].start()
    acc[...] = jnp.zeros(acc.shape, F32)
    height = acc.shape[2] - ROWS
    place_lane = iota((ROWS, LANES), 1)
    place_sub = iota((ROWS, LANES), 0)

    def one_strip(t, carry):
        step_row, step_col = place(patch_ref[t], n_cols)
        top = row_ref[t]
        q = step_col * 3 + step_row
        for c in range(PHASES):
            acc[q, c, pl.ds(top, strip_rows), :] += strips_ref[t, :, c * LANES : (c + 1) * LANES]
        hit = (place_sub == set_ref[t]) & (place_lane >= top) & (place_lane < top + strip_rows)
        acc[q, 0, height:, :] += jnp.where(hit, 1.0, 0.0)
        return carry

    for i in range(n_parts):
        inputs[i].wait()
        lax.fori_loop(i * some, (i + 1) * some, one_strip, 0, unroll=8)
    parity = lax.axis_index("det") % 2
    copies = [
        pltpu.make_async_copy(acc.at[pl.ds(first, 3)], out, sems.at[i])
        for i, (first, out) in enumerate(((6 - 6 * parity, even_hbm), (6 * parity, odd_hbm)))
    ]
    for copy in copies:
        copy.start()
    mid_ref[...] = acc[3:6]
    for copy in copies:
        copy.wait()


def taps_kernel(
    n_rows, n_cols, row_taps_ref, col_taps_ref, coef_ref, flat_ref, table_ref, table8_ref, top_ref, wide
):
    taps = row_taps_ref.shape[0]
    lane = iota((taps, DEPTH), 1)
    sub = iota((taps, DEPTH), 0)
    row_part = exact(row_taps_ref[...].T, jnp.where(lane % WIN == sub, 1.0, 0.0))
    col_part = exact(col_taps_ref[...].T, jnp.where(lane // WIN == sub, 1.0, 0.0))
    n_sets = table_ref.shape[0]
    one, u, v, uu, uv, vv = [coef_ref[p * n_sets : (p + 1) * n_sets, :] for p in range(6)]
    u0 = (2 * lax.axis_index("det") + 1).astype(F32) / n_cols - 1.0
    v0 = (2 * lax.axis_index("visit") + 1).astype(F32) / n_rows - 1.0
    one, u, v = (
        one + u0 * (u + u0 * uu) + v0 * (v + u0 * uv + v0 * vv),
        u + 2.0 * u0 * uu + v0 * uv,
        v + u0 * uv + 2.0 * v0 * vv,
    )
    flat = exact(jnp.concatenate([one, v, u, uu, uv, vv], axis=0), row_part * col_part)
    flat_ref[...] = flat
    top = jnp.maximum(jnp.max(jnp.max(jnp.abs(flat), axis=1, keepdims=True), axis=0, keepdims=True), 1e-30)
    top_ref[...] = jnp.broadcast_to(top, top_ref.shape)
    scale = TOP / top
    n = flat.shape[0]
    block = PHASES * ROWS
    for dy in range(ROWS):
        moved = flat if dy == 0 else pltpu.roll(flat, dy, 1)
        for c in range(TILES):
            wide[c, pl.ds(dy, n, stride=ROWS), :] = moved[:, c * LANES : (c + 1) * LANES]
    for s in range(n_sets):
        for p in range(6):
            rows = on_phases(wide, (p * n_sets + s) * ROWS)
            hi = rows.astype(BF16)
            table_ref[s, p * block : (p + 1) * block, :] = hi
            if p < FINE:
                table_ref[s, (6 + p) * block : (7 + p) * block, :] = (rows - hi.astype(F32)).astype(BF16)
                table8_ref[s, p * block : (p + 1) * block, :] = (rows * scale).astype(F8)


def on_phases(wide, first):
    rows = jnp.concatenate([wide[c, pl.ds(first, ROWS), :] for c in range(TILES)], axis=1)
    return jnp.concatenate([rows] + [pltpu.roll(rows, dx * WIN, 1) for dx in range(1, PHASES)], axis=0)


def columns_of(step_col, n_cols, width):
    shape = (PHASES * ROWS, LANES)
    col = (step_col - 1) * width - width // 2 + iota(shape, 1) * PHASES + iota(shape, 0) // ROWS
    return 2.0 * (col.astype(F32) + 0.5) / (n_cols * width)


def fill(image_ref, part, row, col, halves, kind, data):
    lane = iota((WIN, LANES), 1)
    for phase in range(PHASES):
        near, far = [image_ref[part, phase, col + i, pl.ds(row, WIN + (halves - 1) * ROWS), :] for i in range(2)]
        for half in range(halves):
            rows = slice(half * ROWS, half * ROWS + WIN)
            a, b = near[rows].astype(kind), far[rows].astype(kind)
            for shift in range((SIDE - HALF + SHIFTS - 1) // PHASES + 1):
                k = shift * PHASES + phase - (SIDE - HALF)
                if 0 <= k < SHIFTS:
                    moved = a if shift == 0 else pltpu.roll(jnp.where(lane < shift, b, a), LANES - shift, 1)
                    data[k * WIN : (k + 1) * WIN, half * LANES : (half + 1) * LANES] = moved


def model_loop(
    n_rows, n_cols, height, patch_ref, row_ref, set_ref, top_ref, table8_ref, table_ref, image, buffers, first, last, store
):
    width = PHASES * LANES
    block = PHASES * ROWS
    fine = FINE * block
    shape = (block, 2 * LANES)
    row_in = iota(shape, 0) % ROWS + iota(shape, 1) // LANES * ROWS
    undo = top_ref[0:1, 0:1] * (1.0 / (TOP * SCALE))

    def build(t, data_hi, data_lo):
        step_row, step_col = place(patch_ref[t], n_cols)
        row = step_row * height + row_ref[t] + EDGE - HALF
        fill(image, 0, row, step_col, 2, BF16, data_hi)
        fill(image, 1, row, step_col, 2, F8, data_lo)

    def multiply(t, data_hi, data_lo):
        step_row, step_col = place(patch_ref[t], n_cols)
        which = set_ref[t]
        big = mxu(table_ref[which], data_hi[...])
        small = mxu(table8_ref[which], data_lo[...])
        exact_terms = big[:fine] + big[6 * block :] + small * undo
        term_1, term_v, term_u = [exact_terms[p * block : (p + 1) * block] for p in range(FINE)]
        term_uu, term_uv, term_vv = [big[p * block : (p + 1) * block] for p in range(FINE, 6)]
        one_u = columns_of(step_col, n_cols, width)
        u = jnp.concatenate([one_u, one_u], axis=1)
        y = (step_row - 1) * height - height // 2 + row_ref[t] + row_in
        v = 2.0 * (y.astype(F32) + 0.5) / (n_rows * height)
        store(t, term_1 + u * (term_u + u * term_uu + v * term_uv) + v * (term_v + v * term_vv))

    build(first, *buffers[0])
    n = last - first
    some = next(k for k in (28, 8, 4) if n % k == 0)

    def some_strips(i, carry):
        for j in range(some):
            t = first + some * i + j
            build(jnp.minimum(t + 1, last - 1), *buffers[(j + 1) % 2])
            multiply(t, *buffers[j % 2])
        return carry

    lax.fori_loop(0, n // some, some_strips, 0)


def store_model(models, first, strip_rows, t, model):
    for half in range(2):
        rows_of = pl.ds(pl.multiple_of((t - first) * strip_rows + half * ROWS, ROWS), ROWS)
        for dx in range(PHASES):
            models[rows_of, dx * LANES : (dx + 1) * LANES] = model[
                dx * ROWS : (dx + 1) * ROWS, half * LANES : (half + 1) * LANES
            ]


def strips_kernel(
    n_rows, n_cols, patch_ref, row_ref, set_ref, top_ref, near_rows, away_rows, here_ref, even_ref, odd_ref,
    table8_ref, table_ref, image, models, hi_a, lo_a, hi_b, lo_b,
):
    height = here_ref.shape[0]
    width = PHASES * LANES
    scatter = to_phases(width)
    rows = image.shape[3]
    upper = lax.axis_index("visit") % 2 == 0
    ahead = lax.axis_index("visit") % 4 < 2
    for b in range(4):
        cols = slice(b * width, min((b + 1) * width, here_ref.shape[1]))
        near, away, even, odd = [r[:, cols] for r in (near_rows, away_rows, even_ref, odd_ref)]
        pieces = (
            jnp.where(ahead, away, near),
            jnp.where(upper, odd, even),
            here_ref[:, cols],
            jnp.where(upper, even, odd),
            jnp.where(ahead, near, away),
        )
        parts = [split(piece) for piece in pieces]
        both = jnp.concatenate([hi for hi, _ in parts] + [lo for _, lo in parts], axis=0)
        moved = mxu(both, scatter[: cols.stop - cols.start])
        for f in range(PHASES):
            for part in range(2):
                some = moved[part * rows : (part + 1) * rows, f * LANES : (f + 1) * LANES]
                image[part, f, b] = some * SCALE if part else some

    strip_rows = models.shape[0] // (patch_ref.shape[0] - LATER)
    model_loop(
        n_rows, n_cols, height, patch_ref, row_ref, set_ref, top_ref, table8_ref, table_ref, image,
        ((hi_a, lo_a), (hi_b, lo_b)), 0, patch_ref.shape[0] - LATER,
        functools.partial(store_model, models, 0, strip_rows),
    )


def finish_kernel(
    n_rows, n_cols, height, patch_ref, row_ref, set_ref, top_ref, table8_ref, table_ref, image, models, strips_hbm, diff_hbm,
    strips_ref, rest, hi_a, lo_a, hi_b, lo_b, sems,
):
    n_strips, strip_rows, width = strips_ref.shape
    copy_strips = pltpu.make_async_copy(strips_hbm, strips_ref, sems.at[4])
    copy_strips.start()
    model_loop(
        n_rows, n_cols, height, patch_ref, row_ref, set_ref, top_ref, table8_ref, table_ref, image,
        ((hi_a, lo_a), (hi_b, lo_b)), n_strips - LATER, n_strips,
        functools.partial(store_model, rest, n_strips - LATER, strip_rows),
    )
    gather = from_phases()
    gather = jnp.concatenate([gather, gather], axis=0)
    copy_strips.wait()
    some = 16
    ready = models.shape[0]
    for c in range(n_strips // some):
        rows = slice(c * some * strip_rows, (c + 1) * some * strip_rows)
        found = models[rows] if rows.stop <= ready else jnp.concatenate([models[rows.start : ready], rest[...]], axis=0)
        natural = mxu(jnp.concatenate(split(found), axis=1), gather)
        part = pl.ds(c * some, some)
        strips_ref[part] = strips_ref[part] - natural.reshape(some, strip_rows, width)
        pltpu.make_async_copy(strips_ref.at[part], diff_hbm.at[part], sems.at[c]).start()
    for c in range(n_strips // some):
        part = pl.ds(c * some, some)
        pltpu.make_async_copy(strips_ref.at[part], diff_hbm.at[part], sems.at[c]).wait()


def coadd_kernel(
    n_rows, n_cols, flat_ref, image, mid_any, left_any, right_any, even_any, odd_any, coadd_ref,
    parts_ref, taps, wide, models, hi_a, lo_a, hi_b, lo_b, sems,
):
    height, width = coadd_ref.shape
    sources = (mid_any, left_any, right_any, even_any, odd_any)
    copies = [pltpu.make_async_copy(source, parts_ref.at[i], sems.at[i]) for i, source in enumerate(sources)]
    for copy in copies:
        copy.start()
    for copy in copies:
        copy.wait()
    count = jnp.sum(parts_ref[:, 0, height:, :], axis=0)
    n_sets = count.shape[0]
    v = 2.0 * ((iota(count.shape, 1) - height // 2).astype(F32) + 0.5) / (n_rows * height)

    def three(x, p):
        taps_of = flat_ref[p * n_sets : (p + 1) * n_sets, :]
        x_hi, t_hi = x.astype(BF16).astype(F32), taps_of.astype(BF16).astype(F32)
        return [(x_hi, t_hi), (x - x_hi, t_hi), (x_hi, taps_of - t_hi)]

    by_power = []
    for terms in ((0, 1, 5), (2, 4), (3,)):
        rows, x = [], count
        for p in terms:
            rows, x = rows + three(x, p), x * v
        sides = [jnp.concatenate(side, axis=0) for side in zip(*rows)]
        by_power.append(mxu(sides[0].T.astype(BF16), sides[1].astype(BF16)))
    for a in range(3):
        for c in range(TILES):
            taps[c, a * height : (a + 1) * height, :] = by_power[a][:, c * LANES : (c + 1) * LANES]
    n = 3 * height // ROWS
    for dy in range(ROWS):
        some = jnp.concatenate([taps[c, pl.ds(dy, n, stride=ROWS), :] for c in range(TILES)], axis=1)
        moved = some if dy == 0 else pltpu.roll(some, dy, 1)
        for c in range(TILES):
            wide[c, pl.ds(dy, n, stride=ROWS), :] = moved[:, c * LANES : (c + 1) * LANES]
    one_u = columns_of(1, n_cols, width)

    def build(b, data_hi, data_lo):
        fill(image, 0, height + b * ROWS + EDGE - HALF, 1, 1, BF16, data_hi)
        fill(image, 1, height + b * ROWS + EDGE - HALF, 1, 1, BF16, data_lo)

    def multiply(b, data_hi, data_lo):
        row = pl.multiple_of(b * ROWS, ROWS)
        fine_hi, fine_lo = split(on_phases(wide, row))
        rest = [on_phases(wide, a * height + row).astype(BF16) for a in (1, 2)]
        big = mxu(jnp.concatenate([fine_hi] + rest + [fine_lo], axis=0), data_hi[...])
        terms = big.reshape(4, PHASES * ROWS, LANES)
        small = mxu(fine_hi, data_lo[...]) * (1.0 / SCALE)
        model = terms[0] + terms[3] + small + one_u * (terms[1] + one_u * terms[2])
        for dx in range(PHASES):
            models[pl.ds(row, ROWS), dx * LANES : (dx + 1) * LANES] = model[dx * ROWS : (dx + 1) * ROWS]

    n_blocks = height // ROWS
    build(0, hi_a, lo_a)
    some = n_blocks
    buffers = ((hi_a, lo_a), (hi_b, lo_b))

    def some_blocks(i, carry):
        for j in range(some):
            b = some * i + j
            build(jnp.minimum(b + 1, n_blocks - 1), *buffers[(j + 1) % 2])
            multiply(b, *buffers[j % 2])
        return carry

    lax.fori_loop(0, n_blocks // some, some_blocks, 0)
    gather = from_phases()
    gather = jnp.concatenate([gather, gather], axis=0)
    natural = mxu(jnp.concatenate(split(models[...]), axis=1), gather)
    for c in range(PHASES):
        total = jnp.sum(parts_ref[:, c, 0:height, :], axis=0)
        coadd_ref[:, c * LANES : (c + 1) * LANES] = total - natural[:, c * LANES : (c + 1) * LANES]


def swap(x, axis, apart, first):
    size = lax.axis_size(axis)
    lower = [i for i in range(size - apart) if (i - first) % (2 * apart) < apart]
    pairs = [(i, i + apart) for i in lower] + [(i + apart, i) for i in lower]
    return lax.ppermute(x, axis, pairs)


def per_device(strips, patch_of, box_row, kernel_set, template, row_taps, col_taps, kernel_coef):
    n_rows, n_cols = lax.axis_size("visit"), lax.axis_size("det")
    n_strips, strip_rows, width = strips.shape
    height = template.shape[0]
    n_sets, n_terms, n_basis = kernel_coef.shape
    block = PHASES * ROWS
    smem = pl.BlockSpec(memory_space=pltpu.SMEM)
    vmem = pl.BlockSpec(memory_space=pltpu.VMEM)
    hbm = pl.BlockSpec(memory_space=pltpu.HBM)
    free = pl.BlockSpec(memory_space=pl.ANY)

    patch_of = patch_of.reshape(n_strips)

    v, d = lax.axis_index("visit"), lax.axis_index("det")
    first, last = template[:, :SIDE], template[:, width - SIDE :]
    ahead = d % 4 < 2
    even = swap(template, "det", 1, 0)
    odd = swap(template, "det", 1, 1)
    for_near, for_away = jnp.where(ahead, last, first), jnp.where(ahead, first, last)
    patch_of, for_near, for_away = lax.optimization_barrier((patch_of, for_near, for_away))
    near = swap(for_near, "det", 2, 0)
    away = swap(for_away, "det", 2, 2)

    sums = jax.ShapeDtypeStruct((3, PHASES, height + ROWS, LANES), F32)
    for_even, mid, for_odd = pl.pallas_call(
        functools.partial(sums_kernel, n_cols),
        out_shape=(sums, pltpu.VMEM(sums.shape, F32), sums),
        in_specs=[smem] * 3 + [hbm],
        out_specs=(hbm, vmem, hbm),
        scratch_shapes=[
            pltpu.VMEM(strips.shape, F32),
            pltpu.VMEM((9, PHASES, height + ROWS, LANES), F32),
            pltpu.SemaphoreType.DMA((6,)),
        ],
        compiler_params=pltpu.CompilerParams(vmem_limit_bytes=56 * MIB),
        cost_estimate=pl.CostEstimate(flops=3 << 30, bytes_accessed=5 << 20, transcendentals=0),
        name="strip_sums",
    )(patch_of, box_row, kernel_set, strips)

    far_left, far_right = jnp.where(ahead, away, near), jnp.where(ahead, near, away)
    left, right = jnp.where(d % 2 == 0, odd, even), jnp.where(d % 2 == 0, even, odd)
    blank = jnp.zeros((height, LANES - 2 * SIDE), F32)
    here = jnp.concatenate([far_left, left, template, right, far_right, blank], axis=1)

    for_even, for_odd, here = lax.optimization_barrier((for_even, for_odd, here))
    odd = swap(here, "visit", 1, 1)
    even = swap(here, "visit", 1, 0)
    first, last = here[:EDGE], here[height - EDGE :]
    ahead = v % 4 < 2
    for_near, for_away = jnp.where(ahead, last, first), jnp.where(ahead, first, last)
    for_near, for_away, even, row_taps = lax.optimization_barrier((for_near, for_away, even, row_taps))
    near_rows = swap(for_near, "visit", 2, 0)
    away_rows = swap(for_away, "visit", 2, 2)

    sum_even = swap(for_even, "det", 1, 0)
    sum_odd = swap(for_odd, "det", 1, 1)

    flat, table, table8, top = pl.pallas_call(
        functools.partial(taps_kernel, n_rows, n_cols),
        out_shape=(
            pltpu.VMEM((n_sets * n_terms, DEPTH), F32),
            pltpu.VMEM((n_sets, (n_terms + FINE) * block, DEPTH), BF16),
            pltpu.VMEM((n_sets, FINE * block, DEPTH), F8),
            pltpu.VMEM((ROWS, LANES), F32),
        ),
        in_specs=[vmem] * 3,
        out_specs=(vmem,) * 4,
        scratch_shapes=[pltpu.VMEM((TILES, n_sets * n_terms * ROWS, LANES), F32)],
        compiler_params=pltpu.CompilerParams(vmem_limit_bytes=56 * MIB),
        cost_estimate=pl.CostEstimate(flops=3 << 30, bytes_accessed=5 << 20, transcendentals=0),
        name="tap_tables",
    )(row_taps.T, col_taps.T, jnp.swapaxes(kernel_coef, 0, 1).reshape(n_terms * n_sets, n_basis))

    flat, table, table8, top = [
        pltpu.with_memory_space_constraint(x, pltpu.VMEM) for x in (flat, table, table8, top)
    ]

    even, odd, near_rows, away_rows, here = [
        pltpu.with_memory_space_constraint(x, pltpu.VMEM) for x in (even, odd, near_rows, away_rows, here)
    ]

    flops = n_strips * 2 * n_terms * block * DEPTH * 2 * LANES * 2
    buffers = [pltpu.VMEM((DEPTH, 2 * LANES), kind) for kind in (BF16, F8, BF16, F8)]
    image, models = pl.pallas_call(
        functools.partial(strips_kernel, n_rows, n_cols),
        out_shape=(
            pltpu.VMEM((2, PHASES, 4, 3 * height + 2 * EDGE, LANES), F32),
            pltpu.VMEM(((n_strips - LATER) * strip_rows, width), F32),
        ),
        in_specs=[smem] * 3 + [vmem] * 8,
        out_specs=(vmem, vmem),
        scratch_shapes=buffers,
        compiler_params=pltpu.CompilerParams(vmem_limit_bytes=32 * MIB),
        cost_estimate=pl.CostEstimate(flops=flops, bytes_accessed=14 << 20, transcendentals=0),
        name="strip_models",
    )(patch_of, box_row, kernel_set, top, near_rows, away_rows, here, even, odd, table8, table)

    image, models, sum_even, sum_odd = lax.optimization_barrier((image, models, sum_even, sum_odd))
    image, models = [pltpu.with_memory_space_constraint(x, pltpu.VMEM) for x in (image, models)]
    above, below = [mid[i] + sum_even[i] + sum_odd[i] for i in (0, 2)]
    for_even, for_odd = jnp.where(v % 2 == 0, below, above), jnp.where(v % 2 == 0, above, below)
    from_even = swap(for_even, "visit", 1, 0)
    from_odd = swap(for_odd, "visit", 1, 1)

    patch_of, for_even = lax.optimization_barrier((patch_of, for_even))
    difference = pl.pallas_call(
        functools.partial(finish_kernel, n_rows, n_cols, height),
        out_shape=jax.ShapeDtypeStruct(strips.shape, F32),
        in_specs=[smem] * 3 + [vmem] * 5 + [hbm],
        out_specs=hbm,
        scratch_shapes=[pltpu.VMEM(strips.shape, F32), pltpu.VMEM((LATER * strip_rows, width), F32)]
        + buffers
        + [pltpu.SemaphoreType.DMA((5,))],
        compiler_params=pltpu.CompilerParams(vmem_limit_bytes=32 * MIB),
        cost_estimate=pl.CostEstimate(flops=flops // 4, bytes_accessed=4 << 20, transcendentals=0),
        name="finish",
    )(patch_of, box_row, kernel_set, top, table8, table, image, models, strips)

    coadd = pl.pallas_call(
        functools.partial(coadd_kernel, n_rows, n_cols),
        out_shape=jax.ShapeDtypeStruct(template.shape, F32),
        in_specs=[vmem, vmem] + [free] * 5,
        out_specs=vmem,
        scratch_shapes=[
            pltpu.VMEM((5,) + from_even.shape, F32),
            pltpu.VMEM((TILES, 3 * height, LANES), F32),
            pltpu.VMEM((TILES, 3 * height, LANES), F32),
            pltpu.VMEM((height, PHASES * LANES), F32),
        ]
        + [pltpu.VMEM((DEPTH, LANES), BF16)] * 4
        + [pltpu.SemaphoreType.DMA((5,))],
        compiler_params=pltpu.CompilerParams(vmem_limit_bytes=32 * MIB),
        cost_estimate=pl.CostEstimate(flops=6 << 30, bytes_accessed=3 << 20, transcendentals=0),
        name="coadd_models",
    )(flat, image, mid[1], sum_even[1], sum_odd[1], from_even, from_odd)
    return difference, coadd


def solution(mesh):
    tiles = ("visit", "det")
    in_specs = (P(tiles, None, None), P(tiles, None), P(tiles), P(tiles), P("visit", "det"), P(), P(), P())
    out_specs = (P(tiles, None, None), P("visit", "det"))
    return jax.shard_map(per_device, mesh=mesh, in_specs=in_specs, out_specs=out_specs, check_vma=False)
```
